256 devices in a mesh: bead: 32 (over z_hi, x, core), dom: 8 (over y, z_lo).
Axes of the slice: x: 4, y: 4, z: 8 (z_hi: 4, z_lo: 2; z = z_hi * 2 + z_lo), core: 2. Of those that a mesh axis runs over, the one named last changes fastest.
Arguments:
- positions: float32 [3, 32, 4096], P(None, 'bead', 'dom'), may hold values from -2.5 to 2.5
- momenta: float32 [3, 32, 4096], P(None, 'bead', 'dom'), may hold values from -6 to 6
- forces: float32 [3, 32, 4096], P(None, 'bead', 'dom'), may hold values from -6 to 6
- masses: float32 [4096], P('dom'), may hold values from 1 to 16
- charges: float32 [4096], P('dom'), may hold values from -1 to 1
- embedding: bfloat16 [4096, 240], P('dom'), may hold values from -6 to 6
- neighbours: int32 [8, 4096], P(None, 'dom'), may hold values from 0 to 895
- send_rows: int32 [3072], P('dom'), may hold values from 0 to 511
- wavevectors: int32 [3, 16384], replicated, may hold values from -12 to 12, as said below
- radial_weight: bfloat16 [2, 16, 240], replicated, may hold values from -1.5 to 1.5
- mix_weight: bfloat16 [2, 240, 240], replicated, may hold values from -0.375 to 0.375
- update_weight: bfloat16 [2, 240, 240], replicated, may hold values from -0.375 to 0.375
- readout_weight: bfloat16 [240, 240], replicated, may hold values from -0.375 to 0.375
- energy_weight: float32 [240], replicated, may hold values from -0.375 to 0.375
Outputs:
- next_positions: float32 [3, 32, 4096], P(None, 'bead', 'dom')
- next_momenta: float32 [3, 32, 4096], P(None, 'bead', 'dom')
- next_forces: float32 [3, 32, 4096], P(None, 'bead', 'dom')
The draws below stay inside these ranges and needn't reach their ends.
Inputs may be any that keep to these rules, and one draw needn't show every extreme that they name: `wavevectors`: no component is zero.
All inputs are finite; a program needn't handle non-finite values.
Results may differ from the reference program's by a relative error of at most 0.0065.
Values may be sent and summed in bfloat16 or wider, within the bound.
A program may use at most 64 MiB of HBM per device.

```python
import math
import jax
import jax.numpy as jnp
from jax import lax

BEADS = 32
ATOM_DEV = 512
GHOST = 192
NEIGH = 8
FEAT = 240
BASIS = 16
LAYERS = 2
KVEC = 16384
STEPS = 1
ATOMS = 4096
EXT = 896
N_DOM = 8


def draw_positions(key, part):
    first_key, second_key = jax.random.split(jax.random.fold_in(key, 11))
    centre = jax.random.uniform(first_key, (3, 1, ATOMS), jnp.float32, -2.0, 2.0)
    spread = jnp.clip(0.15 * jax.random.normal(second_key, (3, BEADS, ATOMS), jnp.float32), -0.45, 0.45)
    return (centre + spread).astype(jnp.float32)


def draw_wavevectors(key, part):
    first_key, second_key = jax.random.split(jax.random.fold_in(key, 23))
    magnitude = jax.random.randint(first_key, (3, KVEC), 1, 13)
    signs = 2 * jax.random.randint(second_key, (3, KVEC), 0, 2) - 1
    values = (magnitude * signs).at[0, 0].set(12).at[1, 0].set(-12)
    return values.astype(jnp.int32)


def touch_ends(result, key, least, high):
    shape = result.shape
    place = [jax.random.randint(jax.random.fold_in(key, axis), (), 0, shape[axis]) for axis in range(len(shape))]
    result = result.at[tuple(place)].set(least)
    longest = shape.index(max(shape))
    place[longest] = (place[longest] + 1) % shape[longest]
    return result.at[tuple(place)].set(high)


def shard_levels(own_key, shape, cuts, least, top_value):
    factor_of = 1.0
    for position, blocks in cuts:
        draws = jax.random.uniform(jax.random.fold_in(jax.random.fold_in(own_key, 6), position), (blocks,), jnp.float32, least / len(cuts), top_value / len(cuts))
        factor_of = factor_of * jnp.repeat(jnp.exp(draws), shape[position] // blocks).reshape((-1,) + (1,) * (len(shape) - 1 - position))
    return factor_of


def gaussian(stream_key, dims, scale, reach, cuts=(), kind=jnp.bfloat16):
    array = jax.random.normal(stream_key, dims, jnp.float32) * scale
    if len(cuts) > 0:
        array = shard_levels(stream_key, dims, cuts, -0.22, 0.18) * array
    return jnp.clip(array, min=-reach, max=reach).astype(kind)


def setup_inputs(seed: int = 0) -> dict:
    keys = jax.random.split(jax.random.key(seed), 15)
    return {
        "positions": draw_positions(jax.random.fold_in(keys[14], 71), 0),
        "momenta": gaussian(keys[1], (3, BEADS, ATOMS), 1.0, 6.0, ((1, 32), (2, 8)), jnp.float32),
        "forces": gaussian(keys[2], (3, BEADS, ATOMS), 1.0, 6.0, ((1, 32), (2, 8)), jnp.float32),
        "masses": jnp.clip(jnp.exp(math.log(16.0) - 2.7725887 * jax.random.uniform(keys[3], (ATOMS,), jnp.float32) ** shard_levels(keys[3], (ATOMS,), ((0, 8),), -0.2, 0.2)), 1.0, 16.0),
        "charges": jnp.clip(jax.random.uniform(keys[4], (ATOMS,), jnp.float32, -1.0, 1.0) * shard_levels(keys[4], (ATOMS,), ((0, 8),), -0.4, 0.0), -1.0, 1.0),
        "embedding": gaussian(keys[5], (ATOMS, FEAT), 1.0, 6.0, ((0, 8),)),
        "neighbours": touch_ends(jax.random.randint(keys[6], (NEIGH, ATOMS), 0, ATOM_DEV + 2 * GHOST), jax.random.fold_in(keys[6], 1), 0, (ATOM_DEV + 2 * GHOST) - 1).astype(jnp.int32),
        "send_rows": touch_ends(jax.random.randint(keys[7], (2 * GHOST * N_DOM,), 0, ATOM_DEV), jax.random.fold_in(keys[7], 1), 0, ATOM_DEV - 1).astype(jnp.int32),
        "wavevectors": draw_wavevectors(jax.random.fold_in(keys[14], 71), 0),
        "radial_weight": gaussian(keys[9], (LAYERS, BASIS, FEAT), BASIS ** -0.5, 1.5),
        "mix_weight": gaussian(keys[10], (LAYERS, FEAT, FEAT), FEAT ** -0.5, 0.375),
        "update_weight": gaussian(keys[11], (LAYERS, FEAT, FEAT), FEAT ** -0.5, 0.375),
        "readout_weight": gaussian(keys[12], (FEAT, FEAT), FEAT ** -0.5, 0.375),
        "energy_weight": gaussian(keys[13], (FEAT,), FEAT ** -0.5, 0.375, (), jnp.float32),
    }


step_dt = 0.25
omega_cycle = 1.6
box_length = 4.0
ewald_sigma = 0.002
ewald_gain = 48.0
norm_eps = 1e-06
peak_frequency = lax.Precision.HIGHEST

def mode_matrix(length):
    row_index = jnp.arange(length, dtype=jnp.int32)[:, None]
    column_index = jnp.arange(length, dtype=jnp.int32)[None, :]
    angles = 2.0 * math.pi / length * (row_index * column_index % length).astype(jnp.float32)
    single_norm = math.sqrt(1.0 / length)
    double_norm = math.sqrt(2.0 / length)
    parity = (1 - 2 * (row_index % 2)).astype(jnp.float32)
    middle = length // 2
    normal_transform = jnp.where(column_index == 0, single_norm, jnp.where(column_index < middle, double_norm * jnp.cos(angles), jnp.where(column_index == middle, single_norm * parity, double_norm * jnp.sin(angles))))
    return normal_transform.astype(jnp.float32)

def propagate(normal_mode_positions, normal_mode_momentum, masses):
    length = normal_mode_positions.shape[1]
    orders = jnp.arange(length, dtype=jnp.float32)
    omegas = 2.0 * omega_cycle * jnp.sin(math.pi * orders / length)
    cosine = jnp.cos(omegas * step_dt)[:, None]
    sines = jnp.sin(omegas * step_dt)
    omega_safe = jnp.where(orders == 0.0, 1.0, omegas)
    drift = jnp.where(orders == 0.0, step_dt, sines / omega_safe)[:, None]
    spring = (omegas * sines)[:, None]
    next_coords = cosine * normal_mode_positions + drift * normal_mode_momentum / masses
    next_moment = cosine * normal_mode_momentum - spring * masses * normal_mode_positions
    return (next_coords, next_moment)

def ewald_coef(reciprocal, atom_total):
    square = lax.optimization_barrier(jnp.sum(reciprocal * reciprocal, 0))
    return ewald_gain / math.sqrt(reciprocal.shape[1] * atom_total) * jnp.exp(-ewald_sigma * square) / square

def phase_sums(reciprocal, centre, charge):
    phases = jnp.dot(reciprocal.T, centre, precision=peak_frequency)
    return (jnp.dot(jnp.cos(phases), charge, precision=peak_frequency), jnp.dot(jnp.sin(phases), charge, precision=peak_frequency))

def ewald_force(reciprocal, centre, charge, cosine_sum, sine_sum, damping):
    phases = jnp.dot(reciprocal.T, centre, precision=peak_frequency)
    weight = (damping * cosine_sum)[:, None] * jnp.sin(phases) - (damping * sine_sum)[:, None] * jnp.cos(phases)
    return 2.0 * charge * jnp.dot(reciprocal, weight, precision=peak_frequency)

def short_energy(coords, embedding, source, radial_rates, radial_weight, mix_weight, update_weight, readout_weight, energy_weight):
    hidden = embedding.astype(jnp.float32)
    others = coords[:, source]
    offset = others - coords[:, None, :]
    distance = lax.optimization_barrier(jnp.sum(offset * offset, 0))
    basis = (1.0 / (1.0 + radial_rates[:, None, None] * distance[None])).astype(jnp.bfloat16)
    for number in range(LAYERS):
        rounded = hidden.astype(jnp.bfloat16).astype(jnp.float32)
        edge_weight = jnp.einsum('mka,mf->kaf', basis.astype(jnp.float32), radial_weight[number].astype(jnp.float32))
        message = lax.optimization_barrier(jnp.sum(edge_weight * rounded[source], 0))
        scaled = message * lax.rsqrt(lax.optimization_barrier(jnp.mean(message * message, -1, keepdims=True)) + norm_eps)
        gated = jax.nn.silu(jnp.dot(scaled.astype(jnp.bfloat16), mix_weight[number], preferred_element_type=jnp.float32)).astype(jnp.bfloat16)
        hidden = hidden + jnp.dot(gated, update_weight[number], preferred_element_type=jnp.float32)
    activation = jax.nn.silu(jnp.dot(hidden.astype(jnp.bfloat16), readout_weight, preferred_element_type=jnp.float32))
    return jnp.sum(activation * energy_weight)

def reference(positions, momenta, forces, masses, charges, embedding, neighbours, send_rows, wavevectors, radial_weight, mix_weight, update_weight, readout_weight, energy_weight):
    normal_transform = mode_matrix(BEADS)
    table = send_rows.reshape(N_DOM, 2 * GHOST)
    domain = jnp.arange(N_DOM, dtype=jnp.int32)
    prior_domain = (domain + N_DOM - 1) % N_DOM
    next_domain = (domain + 1) % N_DOM
    owned_index = domain[:, None] * ATOM_DEV + jnp.arange(ATOM_DEV, dtype=jnp.int32)[None, :]
    from_before = prior_domain[:, None] * ATOM_DEV + table[prior_domain][:, GHOST:]
    from_after = next_domain[:, None] * ATOM_DEV + table[next_domain][:, :GHOST]
    extended = jnp.concatenate([owned_index, from_before, from_after], 1).astype(jnp.int32)
    neighbour_table = neighbours.reshape(NEIGH, N_DOM, ATOM_DEV)
    source = jnp.take_along_axis(jnp.broadcast_to(extended[None], (NEIGH, N_DOM, EXT)), neighbour_table, axis=2).reshape(NEIGH, ATOMS).astype(jnp.int32)
    reciprocal = wavevectors.astype(jnp.float32) * (2.0 * math.pi / box_length)
    damping = ewald_coef(reciprocal, ATOMS)
    radial_rates = 0.125 * 2.0 ** (0.5 * jnp.arange(BASIS, dtype=jnp.float32))
    energy_grad = jax.grad(short_energy)

    def bead_force(coords):
        return -energy_grad(coords, embedding, source, radial_rates, radial_weight, mix_weight, update_weight, readout_weight, energy_weight)
    coords_now, moment_now, force_now = (positions, momenta, forces)
    for number in range(STEPS):
        kicked = moment_now + 0.5 * step_dt * force_now
        stacked_arrays = jnp.concatenate([coords_now, kicked], 0)
        normal_mode_entries = jnp.einsum('gt,ugs->uts', normal_transform, stacked_arrays, precision=peak_frequency)
        normal_mode_positions, normal_mode_momentum = propagate(normal_mode_entries[:3], normal_mode_entries[3:], masses)
        returned_to_beads = jnp.einsum('fj,qjd->qfd', normal_transform, jnp.concatenate([normal_mode_positions, normal_mode_momentum], 0), precision=peak_frequency)
        centre = normal_mode_positions[:, 0, :] / math.sqrt(BEADS)
        cosine_sum, sine_sum = phase_sums(reciprocal, centre, charges)
        long_force = ewald_force(reciprocal, centre, charges, cosine_sum, sine_sum, damping)
        coords_now = returned_to_beads[:3]
        short_force = lax.map(bead_force, jnp.moveaxis(coords_now, 1, 0))
        force_now = jnp.moveaxis(short_force, 0, 1) + long_force[:, None, :]
        moment_now = returned_to_beads[3:] + 0.5 * step_dt * force_now
    return (coords_now, moment_now, force_now)
```

```python
import math

import jax
import jax.numpy as jnp
import numpy as np
from jax import lax
from jax.experimental import pallas as pl
from jax.experimental.pallas import tpu as pltpu
from jax.sharding import PartitionSpec as P

MESH = pl.DeviceIdType.MESH
F32 = jnp.float32
BF16 = jnp.bfloat16

BEADS = 32
ATOMS = 512
TOTAL_ATOMS = 4096
GHOST = 192
SIDE = 256
EXT = ATOMS + 2 * SIDE
NEIGH = 8
FEAT = 240
BASIS = 16
KVEC = 16384
KPART = KVEC // BEADS
DT = 0.25
TWO_PI = 2.0 * math.pi

S1, EMB, PACK, MA, MB, GH, FG, DG, SK, E1, E2, XP, FO, GG, N_SEMS = np.cumsum(
    [0, 8, 1, 1, 4, 4, 8, 4, 2, 8, 8, 4, 1, 1, 2]
).tolist()


def ring_tables():
    k = np.arange(BEADS)
    b = np.arange(BEADS)[:, None]
    angle = 2.0 * np.pi / BEADS * (b * k % BEADS)
    half = BEADS // 2
    basis = np.where(k < half, np.cos(angle), np.sin(angle)) * math.sqrt(2.0 / BEADS)
    basis = np.where(k == 0, math.sqrt(1.0 / BEADS), basis)
    basis = np.where(k == half, math.sqrt(1.0 / BEADS) * (1 - 2 * (b % 2)), basis)
    omega = 3.2 * np.sin(np.pi * k / BEADS)
    cosine, sine = np.cos(omega * DT), np.sin(omega * DT)
    drift = np.where(k == 0, DT, sine / np.where(k == 0, 1.0, omega))
    rows = [(basis * value) @ basis.T for value in (cosine, drift, omega * sine)]
    return np.concatenate([row[0] for row in rows]).astype(np.float32)


def dot(a, b):
    return lax.dot_general(a, b, (((1,), (0,)), ((), ())), preferred_element_type=F32)


def dot_t(a, b):
    return lax.dot_general(a, b, (((1,), (1,)), ((), ())), preferred_element_type=F32)


def rows_of(shape):
    return lax.broadcasted_iota(jnp.int32, shape, 0)


def lanes_of(shape):
    return lax.broadcasted_iota(jnp.int32, shape, 1)


def two_parts(value):
    high = value.astype(BF16)
    return high, (value - high.astype(F32)).astype(BF16)


def stacked_parts(value):
    high = value.astype(BF16).astype(F32)
    return jnp.concatenate([high, value - high], 0).astype(BF16)


def lane_pick(tables, index):
    result = None
    for number, block in enumerate(tables):
        local = index - 128 * number
        inside = jnp.logical_and(local >= 0, local < 128)
        got = jnp.take_along_axis(block, jnp.where(inside, local, 0), axis=1, mode="promise_in_bounds")
        result = jnp.where(inside, got, 0.0 if result is None else result)
    return result


def step_kernel(
    coef,
    pos,
    mom,
    force,
    mass,
    charge,
    emb,
    neigh,
    send,
    wave,
    radial,
    mix,
    update,
    readout,
    ew,
    out_pos,
    out_mom,
    out_force,
    v_own,
    v_all,
    emb_buf,
    pack_own,
    pack_buf,
    ma_send,
    ma_buf,
    mb_send,
    mb_buf,
    gh_send,
    gh_buf,
    fg_send,
    fg_buf,
    dg_send,
    dg_buf,
    sk_buf,
    e1_buf,
    e2_buf,
    xp_send,
    xp_buf,
    fo_send,
    fo_buf,
    gg_send,
    gg_buf,
    sel,
    sel_own,
    onehot,
    ext_rows,
    picked,
    d_picked,
    basis_buf,
    slope_buf,
    dist_buf,
    ddist_buf,
    offset_buf,
    msg,
    dmsg,
    drows,
    hidden,
    pre_buf,
    normed_buf,
    inv_buf,
    mix_t,
    update_t,
    readout_t,
    radial_t,
    wave_buf,
    wave_t,
    r_buf,
    cos_buf,
    sin_buf,
    send_sem,
    recv_sem,
):
    bead = lax.axis_index("bead")
    dom = lax.axis_index("dom")
    z, x, core = bead // 8, (bead // 2) % 4, bead % 2
    y, low = dom // 2, dom % 2
    ring = 2 * y + core

    def dev(z_, x_, y_, low_, core_):
        return ((z_ * 4 + x_) * 2 + core_, y_ * 2 + low_)

    def ring_dev(z_, step):
        place = (ring + step) % 8
        return dev(z_, x, place // 2, low, place % 2)

    def swapped_ring_dev(step):
        place = (ring + step) % 8
        return dev(z, x, place // 2, place % 2, low)

    def copy(src, dst, send_at, recv_at, target):
        return pltpu.make_async_remote_copy(
            src_ref=src,
            dst_ref=dst,
            send_sem=send_sem.at[send_at],
            recv_sem=recv_sem.at[recv_at],
            device_id=target,
            device_id_type=MESH,
        )

    def arrive(dst, recv_at):
        copy(dst, dst, 0, recv_at, dev(z, x, y, low, 1 - core)).wait_recv()

    started = []

    def send_to(src, dst, send_at, recv_at, target):
        out = copy(src, dst, send_at, recv_at, target)
        out.start()
        started.append(out)

    same = low == core
    conditional = []

    def send_or_keep(src, dst, send_at, recv_at, target):
        out = copy(src, dst, send_at, recv_at, target)

        @pl.when(same)
        def _():
            pltpu.make_async_copy(src, dst, recv_sem.at[recv_at]).start()

        @pl.when(jnp.logical_not(same))
        def _():
            out.start()

        conditional.append(out)

    barrier = pltpu.get_barrier_semaphore()
    greeted = []
    for dx in range(4):
        for dl in range(2):
            for dc in range(2):
                if dx or dl or dc:
                    greeted.append(dev(z, (x + dx) % 4, y, (low + dl) % 2, (core + dc) % 2))
    for dy in range(1, 4):
        for dc in range(2):
            greeted.append(dev(z, x, (y + dy) % 4, low, (core + dc) % 2))
    for dz in range(1, 4):
        for step in (-1, 0, 1):
            greeted.append(ring_dev((z + dz) % 4, step + 8))
    greeted.append(dev(z, x, (y + jnp.where(core == 0, 3, 1)) % 4, 1 - core, low))
    greeted.append(dev(z, x, (y + jnp.where(low == 0, 3, 1)) % 4, core, 1 - low))
    for target in greeted:
        pl.semaphore_signal(barrier, inc=1, device_id=target, device_id_type=MESH)

    v_own[...] = jnp.zeros((8, ATOMS), F32)
    for c in range(3):
        v_own[c : c + 1, :] = pos[c]
        v_own[4 + c : 5 + c, :] = mom[c] + (0.5 * DT) * force[c]
    lane = lanes_of((1, 2 * SIDE))
    rows384 = jnp.concatenate([send[...], jnp.zeros((1, 128), jnp.int32)], 1)
    shifted = pltpu.roll(rows384, 64, 1)
    spread = jnp.where(
        lane < GHOST,
        rows384,
        jnp.where(jnp.logical_and(lane >= SIDE, lane < SIDE + GHOST), shifted, -1),
    ).astype(F32)
    table = neigh[...]
    pack_own[0:8, :] = jnp.where(table >= ATOMS + GHOST, table + (SIDE - GHOST), table).astype(F32)
    pack_own[8:9, :] = mass[...]
    pack_own[9:10, :] = charge[...]
    pack_own[10:11, :] = spread
    pack_own[11:16, :] = jnp.zeros((5, ATOMS), F32)
    pl.semaphore_wait(barrier, len(greeted))

    slot = x * 2 + core
    send_or_keep(v_own, v_all.at[slot], S1, S1 + slot, dev(z, x, y, low, low))
    for number in range(1, 8):
        dx, dl = number // 2, number % 2
        send_to(
            v_own,
            v_all.at[slot],
            S1 + number,
            S1 + slot,
            dev(z, (x + dx) % 4, y, (low + dl) % 2, low),
        )
    swap = dev(z, x, y, core, low)
    send_or_keep(pack_own, pack_buf, PACK, PACK, swap)
    send_or_keep(emb, emb_buf, EMB, EMB, swap)

    eye = (rows_of((FEAT, FEAT)) == lanes_of((FEAT, FEAT))).astype(F32)
    eye_b = eye.astype(BF16)
    for layer in range(2):
        mix_t[layer] = dot_t(eye_b, mix[layer]).astype(BF16)
        update_t[layer] = dot_t(eye_b, update[layer]).astype(BF16)
        radial_t[layer] = dot_t(eye_b, radial[layer]).astype(BF16)
    readout_t[...] = dot_t(eye_b, readout[...]).astype(BF16)
    ew_col = jnp.sum(eye * ew[...], axis=1, keepdims=True)
    own_spread = jnp.broadcast_to(spread, (ATOMS, 2 * SIDE))
    atom_rows = rows_of((ATOMS, 2 * SIDE)).astype(F32)
    sel_own[...] = jnp.where(own_spread == atom_rows, 1.0, 0.0).astype(BF16)
    k_first = pl.multiple_of((bead - core + low) * KPART, KPART)
    triple = wave[:, pl.ds(k_first, KPART)].astype(F32)
    wave_buf[...] = jnp.zeros((16, KPART), F32)
    for part in range(3):
        wave_buf[4 * part : 4 * part + 3, :] = triple
    wave_t[...] = jnp.transpose(wave_buf[...]).astype(BF16)

    arrive(pack_buf, PACK)
    inv_mass = 1.0 / pack_buf[8:9, :]
    charges = pack_buf[9:10, :]
    send_row = pack_buf[10:11, :]
    sel[...] = jnp.where(jnp.broadcast_to(send_row, (ATOMS, 2 * SIDE)) == atom_rows, 1.0, 0.0).astype(BF16)
    send_index = jnp.broadcast_to(send_row, (8, 2 * SIDE)).astype(jnp.int32)

    for k in range(8):
        arrive(v_all.at[k], S1 + k)
    row8 = rows_of((8, ATOMS))
    upper = row8 < 4
    scale = jnp.where(upper, inv_mass, -pack_buf[8:9, :])
    beads_in = [v_all[k] for k in range(8)]
    total = beads_in[0]
    for k in range(1, 8):
        total = total + beads_in[k]
    centre_part = (total + DT * inv_mass * pltpu.roll(total, 4, 0)) * (1.0 / BEADS)
    centre_low = pltpu.roll(centre_part, 4, 0)
    first_row = rows_of((8, 1)) < 4
    for dz in (1, 2, 3, 0):
        z_to = (z + dz) % 4
        straight = None
        for k in range(8):
            shift = (8 * (z_to - z) + 2 * x + low - k + 64) % BEADS
            same_kind = coef[shift] * beads_in[k]
            other = jnp.where(first_row, coef[2 * BEADS + shift], coef[BEADS + shift]) * beads_in[k]
            straight = same_kind if straight is None else straight + same_kind
            crossed = other if k == 0 else crossed + other
        moved = straight + scale * pltpu.roll(crossed, 4, 0)
        ma = jnp.where(upper, moved, centre_low)
        for c in range(3):
            blocks = [
                jnp.broadcast_to(moved[c : c + 1, 128 * n : 128 * n + 128], (8, 128)) for n in range(4)
            ]
            for n in range(4):
                got = lane_pick(blocks, send_index[:, 128 * n : 128 * n + 128])
                gh_send[dz, n // 2, c : c + 1, 128 * (n % 2) : 128 * (n % 2) + 128] = got[0:1]
        gh_send[dz, :, 3:4, :] = jnp.zeros((2, 1, SIDE), F32)
        if dz:
            ma_send[dz] = ma
            mb_send[dz] = moved[4:8]
            send_to(ma_send.at[dz], ma_buf.at[z], MA + dz, MA + z, ring_dev(z_to, 0))
        else:
            ma_buf[z] = ma
            mb_buf[z] = moved[4:8]
        send_to(gh_send.at[dz, 0], gh_buf.at[1, z], GH + 2 * dz, GH + 4 + z, ring_dev(z_to, 7))
        send_to(gh_send.at[dz, 1], gh_buf.at[0, z], GH + 2 * dz + 1, GH + z, ring_dev(z_to, 1))
    for dz in range(1, 4):
        send_to(mb_send.at[dz], mb_buf.at[z], MB + dz, MB + z, ring_dev((z + dz) % 4, 0))

    def send_features(layer, rounded):
        ghosts = dot(rounded, sel[...]).astype(BF16)
        fg_send[layer, 0] = ghosts[:, :SIDE]
        fg_send[layer, 1] = ghosts[:, SIDE:]
        send_to(
            fg_send.at[layer, 0], fg_buf.at[layer, 1], FG + 2 * layer, FG + 2 * layer + 1, ring_dev(z, 7)
        )
        send_to(
            fg_send.at[layer, 1], fg_buf.at[layer, 0], FG + 2 * layer + 1, FG + 2 * layer, ring_dev(z, 1)
        )

    def receive_features(layer):
        for side in range(2):
            arrive(fg_buf.at[layer, side], FG + 2 * layer + side)
            ext_rows[:, ATOMS + SIDE * side : ATOMS + SIDE * (side + 1)] = fg_buf[layer, side]

    arrive(emb_buf, EMB)
    rounded = emb_buf[...]
    hidden[...] = rounded.astype(F32)
    ext_rows[:, :ATOMS] = rounded
    send_features(0, rounded)

    group_rows = [(rows_of((16, ATOMS)) + 16 * g).astype(F32) for g in range(8)]

    def build(j, carry):
        index = pack_buf[pl.ds(j, 1), :]
        at = pl.multiple_of(j * ATOMS, ATOMS)
        for block in range(EXT // 128):
            local = jnp.broadcast_to(index - 128.0 * block, (16, ATOMS))
            for g in range(8):
                first = 128 * block + 16 * g
                onehot[first : first + 16, pl.ds(at, ATOMS)] = jnp.where(
                    local == group_rows[g], 1.0, 0.0
                ).astype(BF16)
        return carry

    lax.fori_loop(0, NEIGH, build, 0)

    def gather(layer):
        def body(j, carry):
            at = pl.multiple_of(j * ATOMS, ATOMS)
            picked[layer, j] = dot(ext_rows[...], onehot[:, pl.ds(at, ATOMS)]).astype(BF16)
            return carry

        lax.fori_loop(0, NEIGH, body, 0)

    receive_features(0)
    gather(0)

    for dz in range(1, 4):
        arrive(ma_buf.at[(z + dz) % 4], MA + (z + dz) % 4)
    for k in range(4):
        for side in range(2):
            arrive(gh_buf.at[side, k], GH + 4 * side + k)
    moved = (ma_buf[0] + ma_buf[1]) + (ma_buf[2] + ma_buf[3])
    centre = moved[4:7]
    xp_send[...] = moved
    ghosts_at = [(gh_buf[n, 0] + gh_buf[n, 1]) + (gh_buf[n, 2] + gh_buf[n, 3]) for n in range(2)]
    index8 = pack_buf[0:8, :].astype(jnp.int32)
    distance = None
    for c in range(3):
        blocks = [moved[c : c + 1, 128 * n : 128 * n + 128] for n in range(4)]
        for side in range(2):
            blocks += [ghosts_at[side][c : c + 1, 128 * n : 128 * n + 128] for n in range(2)]
        blocks = [jnp.broadcast_to(block, (8, 128)) for block in blocks]
        others = jnp.concatenate(
            [lane_pick(blocks, index8[:, 128 * n : 128 * n + 128]) for n in range(4)], 1
        )
        offset = others - moved[c : c + 1, :]
        offset_buf[c] = offset
        distance = offset * offset if c == 0 else distance + offset * offset
    dist_buf[...] = distance
    m_row = rows_of((BASIS, ATOMS))
    rates = jnp.where(m_row % 2 == 1, 0.125 * math.sqrt(2.0), 0.125) * jnp.left_shift(1, m_row // 2).astype(F32)
    for j in range(NEIGH):
        exact = 1.0 / (1.0 + rates * dist_buf[j : j + 1, :])
        basis_buf[j] = exact.astype(BF16)
        slope_buf[j] = -rates * exact * exact

    turns = centre * 0.25
    high = turns.astype(BF16).astype(F32)
    rest = turns - high
    middle = rest.astype(BF16).astype(F32)
    r_buf[...] = jnp.zeros((16, ATOMS), F32)
    for number, value in enumerate((high, middle, rest - middle)):
        r_buf[4 * number : 4 * number + 3, :] = value

    def ewald_sums():
        phase = r_buf[...].astype(BF16)

        def body(i, carry):
            at = pl.multiple_of(i * 128, 128)
            turn = dot(wave_t[pl.ds(at, 128), :], phase)
            half = (turn - jnp.round(turn)) * math.pi
            q = half * half
            s = half * (
                1.0
                + q
                * (
                    -1.6666666641e-1
                    + q * (8.3333293858e-3 + q * (-1.9840083133e-4 + q * (2.7523971075e-6 - 2.3868346521e-8 * q)))
                )
            )
            c = 1.0 + q * (
                -0.5
                + q
                * (
                    4.1666666658e-2
                    + q
                    * (
                        -1.3888888388e-3
                        + q * (2.4801544910e-5 + q * (-2.7556993055e-7 + 2.0737354e-9 * q))
                    )
                )
            )
            sin_buf[pl.ds(at, 128), :] = (2.0 * s * c).astype(BF16)
            cos_buf[pl.ds(at, 128), :] = (1.0 - 2.0 * s * s).astype(BF16)
            return carry

        lax.fori_loop(0, KPART // 128, body, 0)
        weights = stacked_parts(jnp.broadcast_to(charges, (8, ATOMS)))
        for number, ref in enumerate((cos_buf, sin_buf)):
            sums = dot_t(weights, ref[...])
            sk_buf[ring, number : number + 1, :] = sums[0:1] + sums[8:9]
        for step in range(1, 8):
            send_to(sk_buf.at[ring], sk_buf.at[ring], SK + step, SK + ring, ring_dev(z, step))

    def ewald_forces():
        for step in range(1, 8):
            place = (ring + step) % 8
            arrive(sk_buf.at[place], SK + place)
        sums = sk_buf[0]
        for k in range(1, 8):
            sums = sums + sk_buf[k]
        recip = wave_buf[0:8, :] * (TWO_PI / 4.0)
        recip = jnp.where(row8 < 3, recip, 0.0)
        square = jnp.sum(recip * recip, axis=0, keepdims=True)
        damping = 48.0 / math.sqrt(KVEC * TOTAL_ATOMS) * jnp.exp(-0.002 * square) / square
        from_sin = stacked_parts(recip * (damping * sums[0:1]))
        from_cos = stacked_parts(recip * (damping * sums[1:2]))
        part = dot(from_sin, sin_buf[...]) - dot(from_cos, cos_buf[...])
        part = 2.0 * charges * (part[0:8] + part[8:16])
        place = 2 * x + low
        e1_buf[place] = part[0:4]
        for number in range(1, 8):
            dx, dl = number // 2, number % 2
            send_to(
                e1_buf.at[place],
                e1_buf.at[place],
                E1 + number,
                E1 + place,
                dev(z, (x + dx) % 4, y, (low + dl) % 2, core),
            )

    def ewald_group_sum():
        for number in range(1, 8):
            place = 2 * ((x + number // 2) % 4) + (low + number % 2) % 2
            arrive(e1_buf.at[place], E1 + place)
        part = e1_buf[0]
        for k in range(1, 8):
            part = part + e1_buf[k]
        e2_buf[z] = part
        for dz in range(1, 4):
            send_to(e2_buf.at[z], e2_buf.at[z], E2 + dz, E2 + z, ring_dev((z + dz) % 4, 0))

    def ewald_total():
        for dz in range(1, 4):
            arrive(e2_buf.at[(z + dz) % 4], E2 + (z + dz) % 4)
        return (e2_buf[0] + e2_buf[1]) + (e2_buf[2] + e2_buf[3])

    def finish_layer(layer):
        msg[...] = jnp.zeros((FEAT, ATOMS), F32)

        def body(j, carry):
            edge = dot(radial_t[layer], basis_buf[j])
            msg[...] += edge * picked[layer, j].astype(F32)
            return carry

        lax.fori_loop(0, NEIGH, body, 0)
        message = msg[...]
        inverse = lax.rsqrt(jnp.sum(message * message, axis=0, keepdims=True) * (1.0 / FEAT) + 1e-6)
        normed = message * inverse
        normed_buf[layer] = normed
        inv_buf[layer] = jnp.broadcast_to(inverse, (8, ATOMS))
        pre = dot(mix_t[layer], normed.astype(BF16))
        pre_buf[layer] = pre
        gated = (pre * lax.logistic(pre)).astype(BF16)
        hidden[...] += dot(update_t[layer], gated)

    finish_layer(0)
    rounded = hidden[...].astype(BF16)
    ext_rows[:, :ATOMS] = rounded
    send_features(1, rounded)
    ewald_sums()
    for dz in range(1, 4):
        arrive(mb_buf.at[(z + dz) % 4], MB + (z + dz) % 4)
    xp_send[4:8, :] = (mb_buf[0] + mb_buf[1]) + (mb_buf[2] + mb_buf[3])
    send_or_keep(xp_send, xp_buf, XP, XP, swap)
    receive_features(1)
    gather(1)
    finish_layer(1)

    def silu_slope(pre):
        sig = lax.logistic(pre)
        return sig * (1.0 + pre * (1.0 - sig))

    final = dot(readout_t[...], hidden[...].astype(BF16))
    dfinal = ew_col * silu_slope(final)
    cotan = dot(readout[...], dfinal.astype(BF16)).astype(BF16)

    def message_cotan(layer, cotan_b):
        dgated = dot(update[layer], cotan_b).astype(BF16).astype(F32)
        dpre = dgated * silu_slope(pre_buf[layer])
        dnormed = dot(mix[layer], dpre.astype(BF16)).astype(BF16).astype(F32)
        normed = normed_buf[layer]
        mean = jnp.sum(dnormed * normed, axis=0, keepdims=True) * (1.0 / FEAT)
        dmsg[...] = inv_buf[layer, 0:1, :] * (dnormed - normed * mean)

    def distance_cotan(layer):
        def body(j, carry):
            dedge = (picked[layer, j].astype(F32) * dmsg[...]).astype(BF16)
            dbasis = dot(radial[layer], dedge).astype(BF16).astype(F32)
            part = jnp.sum(dbasis * slope_buf[j], axis=0, keepdims=True)
            if layer == 1:
                ddist_buf[pl.ds(j, 1), :] = part
            else:
                ddist_buf[pl.ds(j, 1), :] += part
            return carry

        lax.fori_loop(0, NEIGH, body, 0)

    message_cotan(1, cotan)

    def row_cotan(j, carry):
        at = pl.multiple_of(j * ATOMS, ATOMS)
        edge = dot(radial_t[1], basis_buf[j])
        d_picked[:, pl.ds(at, ATOMS)] = (edge * dmsg[...]).astype(BF16)
        return carry

    lax.fori_loop(0, NEIGH, row_cotan, 0)
    for side in range(2):
        first = ATOMS + SIDE * side
        dg_send[side] = dot_t(d_picked[...], onehot[first : first + SIDE, :]).astype(BF16)
        send_to(dg_send.at[side], dg_buf.at[1 - side], DG + side, DG + 1 - side, ring_dev(z, 7 if side == 0 else 1))
    for half in range(2):
        drows[:, SIDE * half : SIDE * half + SIDE] = dot_t(
            d_picked[...], onehot[SIDE * half : SIDE * half + SIDE, :]
        )
    distance_cotan(1)
    ewald_forces()
    for side in range(2):
        arrive(dg_buf.at[side], DG + side)
    returned = dot_t(dg_buf[0], sel[:, :SIDE]) + dot_t(dg_buf[1], sel[:, SIDE:])
    owned = (drows[...] + returned).astype(BF16).astype(F32)
    ewald_group_sum()
    message_cotan(0, (cotan.astype(F32) + owned).astype(BF16))
    distance_cotan(0)

    ddist = 2.0 * ddist_buf[...]
    edge_force = [offset_buf[c] * ddist for c in range(3)]
    for c in range(3):
        own = jnp.sum(edge_force[c], axis=0, keepdims=True)
        fo_send[c : c + 1, :] = own
    fo_send[3:4, :] = jnp.zeros((1, ATOMS), F32)

    parts = []
    zero_row = jnp.zeros((1, ATOMS), F32)
    for j in range(NEIGH):
        rows = [edge_force[c][j : j + 1, :] for c in range(3)] + [zero_row] * 5
        parts.append(stacked_parts(jnp.concatenate(rows, 0)))
    force_rows = jnp.concatenate(parts, 1)
    for side in range(2):
        first = ATOMS + SIDE * side
        both = dot_t(force_rows, onehot[first : first + SIDE, :])
        gg_send[side] = both[0:4] + both[8:12]
        send_to(
            gg_send.at[side], gg_buf.at[1 - side], GG + side, GG + 1 - side, swapped_ring_dev(7 if side == 0 else 1)
        )
    both = dot_t(force_rows, onehot[:ATOMS, :])
    fo_send[...] = (fo_send[...] - (both[0:4] + both[8:12])) + ewald_total()
    send_or_keep(fo_send, fo_buf, FO, FO, swap)

    arrive(xp_buf, XP)
    for side in range(2):
        arrive(gg_buf.at[side], GG + side)
    zero4 = jnp.zeros((4, SIDE), F32)
    returned = None
    for side in range(2):
        rows = stacked_parts(jnp.concatenate([gg_buf[side], zero4], 0))
        both = dot_t(rows, sel_own[:, SIDE * side : SIDE * side + SIDE])
        both = both[0:4] + both[8:12]
        returned = both if side == 0 else returned + both
    arrive(fo_buf, FO)
    result = fo_buf[...] - returned
    for c in range(3):
        out_pos[c] = xp_buf[c : c + 1, :]
        out_mom[c] = xp_buf[4 + c : 5 + c, :] + (0.5 * DT) * result[c : c + 1, :]
        out_force[c] = result[c : c + 1, :]

    for out in started:
        out.wait_send()

    @pl.when(jnp.logical_not(same))
    def _():
        for out in conditional:
            out.wait_send()


def local(
    positions,
    momenta,
    forces,
    masses,
    charges,
    embedding,
    neighbours,
    send_rows,
    wavevectors,
    radial_weight,
    mix_weight,
    update_weight,
    readout_weight,
    energy_weight,
):
    vmem = pl.BlockSpec(memory_space=pltpu.VMEM)
    piece = jax.ShapeDtypeStruct((3, 1, ATOMS), F32)
    scratch = [
        ((8, ATOMS), F32),
        ((8, 8, ATOMS), F32),
        ((FEAT, ATOMS), BF16),
        ((16, ATOMS), F32),
        ((16, ATOMS), F32),
        ((4, 8, ATOMS), F32),
        ((4, 8, ATOMS), F32),
        ((4, 4, ATOMS), F32),
        ((4, 4, ATOMS), F32),
        ((4, 2, 4, SIDE), F32),
        ((2, 4, 4, SIDE), F32),
        ((2, 2, FEAT, SIDE), BF16),
        ((2, 2, FEAT, SIDE), BF16),
        ((2, FEAT, SIDE), BF16),
        ((2, FEAT, SIDE), BF16),
        ((8, 2, KPART), F32),
        ((8, 4, ATOMS), F32),
        ((4, 4, ATOMS), F32),
        ((8, ATOMS), F32),
        ((8, ATOMS), F32),
        ((4, ATOMS), F32),
        ((4, ATOMS), F32),
        ((2, 4, SIDE), F32),
        ((2, 4, SIDE), F32),
        ((ATOMS, 2 * SIDE), BF16),
        ((ATOMS, 2 * SIDE), BF16),
        ((EXT, NEIGH * ATOMS), BF16),
        ((FEAT, EXT), BF16),
        ((2, NEIGH, FEAT, ATOMS), BF16),
        ((FEAT, NEIGH * ATOMS), BF16),
        ((NEIGH, BASIS, ATOMS), BF16),
        ((NEIGH, BASIS, ATOMS), F32),
        ((NEIGH, ATOMS), F32),
        ((NEIGH, ATOMS), F32),
        ((3, NEIGH, ATOMS), F32),
        ((FEAT, ATOMS), F32),
        ((FEAT, ATOMS), F32),
        ((FEAT, ATOMS), F32),
        ((FEAT, ATOMS), F32),
        ((2, FEAT, ATOMS), F32),
        ((2, FEAT, ATOMS), F32),
        ((2, 8, ATOMS), F32),
        ((2, FEAT, FEAT), BF16),
        ((2, FEAT, FEAT), BF16),
        ((FEAT, FEAT), BF16),
        ((2, FEAT, BASIS), BF16),
        ((16, KPART), F32),
        ((KPART, 16), BF16),
        ((16, ATOMS), F32),
        ((KPART, ATOMS), BF16),
        ((KPART, ATOMS), BF16),
    ]
    return pl.pallas_call(
        step_kernel,
        out_shape=(piece, piece, piece),
        in_specs=[pl.BlockSpec(memory_space=pltpu.SMEM)] + [vmem] * 14,
        out_specs=(vmem, vmem, vmem),
        scratch_shapes=[pltpu.VMEM(shape, kind) for shape, kind in scratch]
        + [pltpu.SemaphoreType.DMA((N_SEMS,)), pltpu.SemaphoreType.DMA((N_SEMS,))],
        compiler_params=pltpu.CompilerParams(
            collective_id=0, has_side_effects=True, vmem_limit_bytes=48 * 1024 * 1024
        ),
        cost_estimate=pl.CostEstimate(flops=16_000_000_000, bytes_accessed=2_000_000, transcendentals=1_000_000),
    )(
        jnp.asarray(ring_tables()),
        positions,
        momenta,
        forces,
        masses.reshape(1, ATOMS),
        charges.reshape(1, ATOMS),
        embedding.T,
        neighbours,
        send_rows.reshape(1, 2 * GHOST),
        wavevectors,
        radial_weight,
        mix_weight,
        update_weight,
        readout_weight,
        energy_weight.reshape(1, FEAT),
    )


def solution(mesh):
    own = P(None, "bead", "dom")
    placed = (
        own,
        own,
        own,
        P("dom"),
        P("dom"),
        P("dom", None),
        P(None, "dom"),
        P("dom"),
        P(),
        P(),
        P(),
        P(),
        P(),
        P(),
    )
    return jax.shard_map(local, mesh=mesh, in_specs=placed, out_specs=(own, own, own), check_vma=False)
```

```python
import math

import jax
import jax.numpy as jnp
import numpy as np
from jax import lax
from jax.experimental import pallas as pl
from jax.experimental.pallas import tpu as pltpu
from jax.sharding import PartitionSpec as P

MESH = pl.DeviceIdType.MESH
F32 = jnp.float32
BF16 = jnp.bfloat16

BEADS = 32
ATOMS = 512
TOTAL_ATOMS = 4096
GHOST = 192
SIDE = 256
EXT = ATOMS + 2 * SIDE
NEIGH = 8
FEAT = 240
BASIS = 16
KVEC = 16384
KPART = KVEC // BEADS
DT = 0.25
TWO_PI = 2.0 * math.pi

S1, EMB, PACK, MA, MB, GH, FG, DG, SA, SB, E1, E2, XP, FO, GG, N_SEMS = np.cumsum(
    [0, 8, 1, 1, 4, 4, 2, 4, 2, 1, 4, 8, 4, 1, 1, 2]
).tolist()


def ring_tables():
    k = np.arange(BEADS)
    b = np.arange(BEADS)[:, None]
    angle = 2.0 * np.pi / BEADS * (b * k % BEADS)
    half = BEADS // 2
    basis = np.where(k < half, np.cos(angle), np.sin(angle)) * math.sqrt(2.0 / BEADS)
    basis = np.where(k == 0, math.sqrt(1.0 / BEADS), basis)
    basis = np.where(k == half, math.sqrt(1.0 / BEADS) * (1 - 2 * (b % 2)), basis)
    omega = 3.2 * np.sin(np.pi * k / BEADS)
    cosine, sine = np.cos(omega * DT), np.sin(omega * DT)
    drift = np.where(k == 0, DT, sine / np.where(k == 0, 1.0, omega))
    rows = [(basis * value) @ basis.T for value in (cosine, drift, omega * sine)]
    return np.concatenate([row[0] for row in rows]).astype(np.float32)


def dot(a, b):
    return lax.dot_general(a, b, (((1,), (0,)), ((), ())), preferred_element_type=F32)


def dot_t(a, b):
    return lax.dot_general(a, b, (((1,), (1,)), ((), ())), preferred_element_type=F32)


def rows_of(shape):
    return lax.broadcasted_iota(jnp.int32, shape, 0)


def lanes_of(shape):
    return lax.broadcasted_iota(jnp.int32, shape, 1)


def two_parts(value):
    high = value.astype(BF16)
    return high, (value - high.astype(F32)).astype(BF16)


def stacked_parts(value):
    high = value.astype(BF16).astype(F32)
    return jnp.concatenate([high, value - high], 0).astype(BF16)


def lane_pick(tables, index):
    result = None
    for number, block in enumerate(tables):
        local = index - 128 * number
        inside = jnp.logical_and(local >= 0, local < 128)
        got = jnp.take_along_axis(block, jnp.where(inside, local, 0), axis=1, mode="promise_in_bounds")
        result = jnp.where(inside, got, 0.0 if result is None else result)
    return result


def step_kernel(
    coef_in,
    pos_in,
    mom_in,
    force_in,
    mass_in,
    charge_in,
    emb,
    neigh_in,
    send_in,
    wave_in,
    radial_in,
    mix_in,
    update_in,
    readout_in,
    ew_in,
    out,
    coef,
    pos,
    mom,
    force,
    mass,
    charge,
    neigh,
    send,
    wave,
    radial,
    mix,
    update,
    readout,
    ew,
    v_own,
    v_all,
    emb_buf,
    pack_own,
    pack_buf,
    ma_send,
    ma_buf,
    mb_send,
    mb_buf,
    gh_send,
    gh_buf,
    fg_send,
    fg_buf,
    dg_send,
    dg_buf,
    sa_buf,
    sb_buf,
    e1_buf,
    e2_buf,
    xp_send,
    xp_buf,
    fo_send,
    fo_buf,
    gg_send,
    gg_buf,
    sel,
    sel_own,
    onehot,
    ext_rows,
    picked,
    d_picked,
    basis_buf,
    slope_buf,
    dist_buf,
    ddist_buf,
    offset_buf,
    msg,
    dmsg,
    drows,
    hidden,
    pre_buf,
    normed_buf,
    inv_buf,
    mix_t,
    update_t,
    readout_t,
    radial_t,
    wave_buf,
    wave_t,
    r_buf,
    cos_buf,
    sin_buf,
    send_sem,
    recv_sem,
    load_sem,
):
    bead = lax.axis_index("bead")
    dom = lax.axis_index("dom")
    z, x, core = bead // 8, (bead // 2) % 4, bead % 2
    y, low = dom // 2, dom % 2
    ring = 2 * y + core

    def dev(z_, x_, y_, low_, core_):
        return ((z_ * 4 + x_) * 2 + core_, y_ * 2 + low_)

    def ring_dev(z_, step):
        place = (ring + step) % 8
        return dev(z_, x, place // 2, low, place % 2)

    def swapped_ring_dev(step):
        place = (ring + step) % 8
        return dev(z, x, place // 2, place % 2, low)

    def copy(src, dst, send_at, recv_at, target):
        return pltpu.make_async_remote_copy(
            src_ref=src,
            dst_ref=dst,
            send_sem=send_sem.at[send_at],
            recv_sem=recv_sem.at[recv_at],
            device_id=target,
            device_id_type=MESH,
        )

    def arrive(dst, recv_at):
        copy(dst, dst, 0, recv_at, dev(z, x, y, low, 1 - core)).wait_recv()

    started = []

    def send_to(src, dst, send_at, recv_at, target):
        sent = copy(src, dst, send_at, recv_at, target)
        sent.start()
        started.append(sent)

    k_first = pl.multiple_of((bead - core + low) * KPART, KPART)
    loads = {}
    for number, (src, dst) in enumerate(
        (
            (pos_in, pos),
            (mom_in, mom),
            (force_in, force),
            (mass_in, mass),
            (charge_in, charge),
            (neigh_in, neigh),
            (send_in, send),
            (coef_in, coef),
            (radial_in, radial),
            (mix_in, mix),
            (update_in, update),
            (readout_in, readout),
            (ew_in, ew),
            (wave_in.at[:, pl.ds(k_first, KPART)], wave),
        )
    ):
        loads[number] = pltpu.make_async_copy(src, dst, load_sem.at[number])
        loads[number].start()

    same = low == core
    conditional = []

    def send_or_keep(src, dst, send_at, recv_at, target):
        sent = copy(src, dst, send_at, recv_at, target)

        @pl.when(same)
        def _():
            pltpu.make_async_copy(src, dst, recv_sem.at[recv_at]).start()

        @pl.when(jnp.logical_not(same))
        def _():
            sent.start()

        conditional.append(sent)

    barrier = pltpu.get_barrier_semaphore()

    def greet(target):
        pl.semaphore_signal(barrier, inc=1, device_id=target, device_id_type=MESH)

    far = dev((z + 3 + 2 * low) % 4, x, y, 1 - low, low)
    for number in range(1, 8):
        greet(dev(z, (x + number // 2) % 4, y, core, (low + number % 2) % 2))
    for dz in range(1, 4):
        greet(dev((z + dz) % 4, x, y, low, core))
    for step in (1, 7, 4):
        greet(ring_dev(z, step))

    @pl.when(jnp.logical_not(same))
    def _():
        greet(dev(z, x, y, core, low))
        greet(far)

    for number in range(7):
        loads[number].wait()
    v_own[...] = jnp.zeros((8, ATOMS), F32)
    for c in range(3):
        v_own[c : c + 1, :] = pos[c]
        v_own[4 + c : 5 + c, :] = mom[c] + (0.5 * DT) * force[c]
    lane = lanes_of((1, 2 * SIDE))
    rows384 = jnp.concatenate(
        [send[0:1, :], send[1:2, :], send[2:3, :], jnp.zeros((1, 128), jnp.int32)], 1
    )
    shifted = pltpu.roll(rows384, 64, 1)
    spread = jnp.where(
        lane < GHOST,
        rows384,
        jnp.where(jnp.logical_and(lane >= SIDE, lane < SIDE + GHOST), shifted, -1),
    ).astype(F32)
    table = neigh[...]
    pack_own[0:8, :] = jnp.where(table >= ATOMS + GHOST, table + (SIDE - GHOST), table).astype(F32)
    pack_own[8:9, :] = mass[...]
    pack_own[9:10, :] = charge[...]
    pack_own[10:11, :] = spread
    pack_own[11:16, :] = jnp.zeros((5, ATOMS), F32)
    pl.semaphore_wait(barrier, 13 + 2 * jnp.where(same, 0, 1))

    slot = x * 2 + core
    send_or_keep(v_own, v_all.at[slot], S1, S1 + slot, dev(z, x, y, low, low))
    for number in range(1, 8):
        dx, dl = number // 2, number % 2
        send_to(
            v_own,
            v_all.at[slot],
            S1 + number,
            S1 + slot,
            dev(z, (x + dx) % 4, y, (low + dl) % 2, low),
        )
    swap = dev(z, x, y, core, low)
    send_or_keep(pack_own, pack_buf, PACK, PACK, far)
    send_or_keep(emb, emb_buf, EMB, EMB, far)

    for number in range(7, 14):
        loads[number].wait()

    eye = (rows_of((FEAT, FEAT)) == lanes_of((FEAT, FEAT))).astype(F32)
    eye_b = eye.astype(BF16)
    for layer in range(2):
        mix_t[layer] = dot_t(eye_b, mix[layer]).astype(BF16)
        update_t[layer] = dot_t(eye_b, update[layer]).astype(BF16)
        radial_t[layer] = dot_t(eye_b, radial[layer]).astype(BF16)
    readout_t[...] = dot_t(eye_b, readout[...]).astype(BF16)
    ew_col = jnp.sum(eye * ew[...], axis=1, keepdims=True)
    own_spread = jnp.broadcast_to(spread, (ATOMS, 2 * SIDE))
    atom_rows = rows_of((ATOMS, 2 * SIDE)).astype(F32)
    sel_own[...] = jnp.where(own_spread == atom_rows, 1.0, 0.0).astype(BF16)
    triple = wave[...].astype(F32)
    wave_buf[...] = jnp.zeros((16, KPART), F32)
    for part in range(3):
        wave_buf[4 * part : 4 * part + 3, :] = triple
    wave_t[...] = jnp.transpose(wave_buf[...]).astype(BF16)

    arrive(pack_buf, PACK)
    inv_mass = 1.0 / pack_buf[8:9, :]
    charges = pack_buf[9:10, :]
    send_row = pack_buf[10:11, :]
    sel[...] = jnp.where(jnp.broadcast_to(send_row, (ATOMS, 2 * SIDE)) == atom_rows, 1.0, 0.0).astype(BF16)
    send_index = jnp.broadcast_to(send_row, (8, 2 * SIDE)).astype(jnp.int32)

    for k in range(8):
        arrive(v_all.at[k], S1 + k)
    row8 = rows_of((8, ATOMS))
    upper = row8 < 4
    scale = jnp.where(upper, inv_mass, -pack_buf[8:9, :])
    beads_in = [v_all[k] for k in range(8)]
    total = beads_in[0]
    for k in range(1, 8):
        total = total + beads_in[k]
    centre_part = (total + DT * inv_mass * pltpu.roll(total, 4, 0)) * (1.0 / BEADS)
    centre_low = pltpu.roll(centre_part, 4, 0)
    first_row = rows_of((8, 1)) < 4
    for dz in (1, 2, 3, 0):
        z_to = (z + dz) % 4
        straight = None
        for k in range(8):
            shift = (8 * (z_to - z) + 2 * x + low - k + 64) % BEADS
            same_kind = coef[shift] * beads_in[k]
            other = jnp.where(first_row, coef[2 * BEADS + shift], coef[BEADS + shift]) * beads_in[k]
            straight = same_kind if straight is None else straight + same_kind
            crossed = other if k == 0 else crossed + other
        moved = straight + scale * pltpu.roll(crossed, 4, 0)
        ma = jnp.where(upper, moved, centre_low)
        if dz:
            ma_send[dz] = ma
            mb_send[dz] = moved[4:8]
            send_to(ma_send.at[dz], ma_buf.at[z], MA + dz, MA + z, ring_dev(z_to, 0))
        else:
            ma_buf[z] = ma
            mb_buf[z] = moved[4:8]

    def send_features(layer, rounded):
        ghosts = dot(rounded, sel[...]).astype(BF16)
        fg_send[layer, 0] = ghosts[:, :SIDE]
        fg_send[layer, 1] = ghosts[:, SIDE:]
        send_to(
            fg_send.at[layer, 0], fg_buf.at[layer, 1], FG + 2 * layer, FG + 2 * layer + 1, ring_dev(z, 7)
        )
        send_to(
            fg_send.at[layer, 1], fg_buf.at[layer, 0], FG + 2 * layer + 1, FG + 2 * layer, ring_dev(z, 1)
        )

    def receive_features(layer):
        for side in range(2):
            arrive(fg_buf.at[layer, side], FG + 2 * layer + side)
            ext_rows[:, ATOMS + SIDE * side : ATOMS + SIDE * (side + 1)] = fg_buf[layer, side]

    arrive(emb_buf, EMB)
    rounded = emb_buf[...]
    hidden[...] = rounded.astype(F32)
    ext_rows[:, :ATOMS] = rounded
    send_features(0, rounded)
    for dz in range(1, 4):
        send_to(mb_send.at[dz], mb_buf.at[z], MB + dz, MB + z, ring_dev((z + dz) % 4, 0))

    group_rows = [(rows_of((16, ATOMS)) + 16 * g).astype(F32) for g in range(8)]

    def build(j, carry):
        index = pack_buf[pl.ds(j, 1), :]
        at = pl.multiple_of(j * ATOMS, ATOMS)
        for block in range(EXT // 128):
            local = jnp.broadcast_to(index - 128.0 * block, (16, ATOMS))
            for g in range(8):
                first = 128 * block + 16 * g
                onehot[first : first + 16, pl.ds(at, ATOMS)] = jnp.where(
                    local == group_rows[g], 1.0, 0.0
                ).astype(BF16)
        return carry

    lax.fori_loop(0, NEIGH, build, 0)

    def gather_part(layer, first, last, fresh):
        def body(j, carry):
            at = pl.multiple_of(j * ATOMS, ATOMS)
            part = dot(ext_rows[:, first:last], onehot[first:last, pl.ds(at, ATOMS)])
            if not fresh:
                part = part + picked[layer, j].astype(F32)
            picked[layer, j] = part.astype(BF16)
            return carry

        lax.fori_loop(0, NEIGH, body, 0, unroll=True)

    receive_features(0)
    gather_part(0, 0, EXT, True)

    for dz in range(1, 4):
        arrive(ma_buf.at[(z + dz) % 4], MA + (z + dz) % 4)
    moved = (ma_buf[0] + ma_buf[1]) + (ma_buf[2] + ma_buf[3])
    centre = moved[4:7]
    xp_send[...] = moved
    for c in range(3):
        blocks = [
            jnp.broadcast_to(moved[c : c + 1, 128 * n : 128 * n + 128], (8, 128)) for n in range(4)
        ]
        for n in range(4):
            got = lane_pick(blocks, send_index[:, 128 * n : 128 * n + 128])
            gh_send[n // 2, c : c + 1, 128 * (n % 2) : 128 * (n % 2) + 128] = got[0:1]
    gh_send[:, 3:4, :] = jnp.zeros((2, 1, SIDE), F32)
    send_to(gh_send.at[0], gh_buf.at[1], GH, GH + 1, ring_dev(z, 7))
    send_to(gh_send.at[1], gh_buf.at[0], GH + 1, GH, ring_dev(z, 1))
    turns = centre * 0.25
    high = turns.astype(BF16).astype(F32)
    rest = turns - high
    middle = rest.astype(BF16).astype(F32)
    r_buf[...] = jnp.zeros((16, ATOMS), F32)
    for number, value in enumerate((high, middle, rest - middle)):
        r_buf[4 * number : 4 * number + 3, :] = value

    def ewald_sums():
        phase = r_buf[...].astype(BF16)

        def body(i, carry):
            at = pl.multiple_of(i * 128, 128)
            turn = dot(wave_t[pl.ds(at, 128), :], phase)
            half = (turn - jnp.round(turn)) * math.pi
            q = half * half
            s = half * (
                1.0
                + q
                * (
                    -1.6666666641e-1
                    + q * (8.3333293858e-3 + q * (-1.9840083133e-4 + q * (2.7523971075e-6 - 2.3868346521e-8 * q)))
                )
            )
            c = 1.0 + q * (
                -0.5
                + q
                * (
                    4.1666666658e-2
                    + q
                    * (
                        -1.3888888388e-3
                        + q * (2.4801544910e-5 + q * (-2.7556993055e-7 + 2.0737354e-9 * q))
                    )
                )
            )
            sin_buf[pl.ds(at, 128), :] = (2.0 * s * c).astype(BF16)
            cos_buf[pl.ds(at, 128), :] = (1.0 - 2.0 * s * s).astype(BF16)
            return carry

        lax.fori_loop(0, KPART // 128, body, 0)
        weights = stacked_parts(jnp.broadcast_to(charges, (8, ATOMS)))
        for number, ref in enumerate((cos_buf, sin_buf)):
            sums = dot_t(weights, ref[...])
            sa_buf[core, number : number + 1, :] = sums[0:1] + sums[8:9]
        send_to(sa_buf.at[core], sa_buf.at[core], SA, SA, dev(z, x, y, low, 1 - core))

    def ewald_ring():
        arrive(sa_buf.at[1 - core], SA)
        sb_buf[y] = sa_buf[0] + sa_buf[1]
        for dy in range(1, 4):
            send_to(sb_buf.at[y], sb_buf.at[y], SB + dy, SB + y, dev(z, x, (y + dy) % 4, low, core))

    ewald_sums()
    ghosts_at = []
    for side in range(2):
        arrive(gh_buf.at[side], GH + side)
        ghosts_at.append(gh_buf[side])
    index8 = pack_buf[0:8, :].astype(jnp.int32)
    distance = None
    for c in range(3):
        blocks = [moved[c : c + 1, 128 * n : 128 * n + 128] for n in range(4)]
        for side in range(2):
            blocks += [ghosts_at[side][c : c + 1, 128 * n : 128 * n + 128] for n in range(2)]
        blocks = [jnp.broadcast_to(block, (8, 128)) for block in blocks]
        others = jnp.concatenate(
            [lane_pick(blocks, index8[:, 128 * n : 128 * n + 128]) for n in range(4)], 1
        )
        offset = others - moved[c : c + 1, :]
        offset_buf[c] = offset
        distance = offset * offset if c == 0 else distance + offset * offset
    dist_buf[...] = distance
    m_row = rows_of((BASIS, ATOMS))
    rates = jnp.where(m_row % 2 == 1, 0.125 * math.sqrt(2.0), 0.125) * jnp.left_shift(1, m_row // 2).astype(F32)
    for j in range(NEIGH):
        exact = 1.0 / (1.0 + rates * dist_buf[j : j + 1, :])
        basis_buf[j] = exact.astype(BF16)
        slope_buf[j] = -rates * exact * exact

    def ewald_forces():
        for dy in range(1, 4):
            arrive(sb_buf.at[(y + dy) % 4], SB + (y + dy) % 4)
        sums = (sb_buf[0] + sb_buf[1]) + (sb_buf[2] + sb_buf[3])
        recip = wave_buf[0:8, :] * (TWO_PI / 4.0)
        recip = jnp.where(row8 < 3, recip, 0.0)
        square = jnp.sum(recip * recip, axis=0, keepdims=True)
        damping = 48.0 / math.sqrt(KVEC * TOTAL_ATOMS) * jnp.exp(-0.002 * square) / square
        from_sin = stacked_parts(recip * (damping * sums[0:1]))
        from_cos = stacked_parts(recip * (damping * sums[1:2]))
        part = dot(from_sin, sin_buf[...]) - dot(from_cos, cos_buf[...])
        part = 2.0 * charges * (part[0:8] + part[8:16])
        place = 2 * x + low
        e1_buf[place] = part[0:4]
        for number in range(1, 8):
            dx, dl = number // 2, number % 2
            send_to(
                e1_buf.at[place],
                e1_buf.at[place],
                E1 + number,
                E1 + place,
                dev(z, (x + dx) % 4, y, (low + dl) % 2, core),
            )

    def ewald_group_sum():
        for number in range(1, 8):
            place = 2 * ((x + number // 2) % 4) + (low + number % 2) % 2
            arrive(e1_buf.at[place], E1 + place)
        part = e1_buf[0]
        for k in range(1, 8):
            part = part + e1_buf[k]
        e2_buf[z] = part
        for dz in range(1, 4):
            send_to(e2_buf.at[z], e2_buf.at[z], E2 + dz, E2 + z, ring_dev((z + dz) % 4, 0))

    def ewald_total():
        for dz in range(1, 4):
            arrive(e2_buf.at[(z + dz) % 4], E2 + (z + dz) % 4)
        return (e2_buf[0] + e2_buf[1]) + (e2_buf[2] + e2_buf[3])

    def finish_layer(layer):
        msg[...] = jnp.zeros((FEAT, ATOMS), F32)

        def body(j, carry):
            edge = dot(radial_t[layer], basis_buf[j])
            msg[...] += edge * picked[layer, j].astype(F32)
            return carry

        lax.fori_loop(0, NEIGH, body, 0, unroll=True)
        message = msg[...]
        inverse = lax.rsqrt(jnp.sum(message * message, axis=0, keepdims=True) * (1.0 / FEAT) + 1e-6)
        normed = message * inverse
        normed_buf[layer] = normed
        inv_buf[layer] = jnp.broadcast_to(inverse, (8, ATOMS))
        pre = dot(mix_t[layer], normed.astype(BF16))
        pre_buf[layer] = pre
        gated = (pre * lax.logistic(pre)).astype(BF16)
        hidden[...] += dot(update_t[layer], gated)

    ewald_ring()
    finish_layer(0)
    rounded = hidden[...].astype(BF16)
    ext_rows[:, :ATOMS] = rounded
    send_features(1, rounded)
    gather_part(1, 0, ATOMS, True)
    for dz in range(1, 4):
        arrive(mb_buf.at[(z + dz) % 4], MB + (z + dz) % 4)
    xp_send[4:8, :] = (mb_buf[0] + mb_buf[1]) + (mb_buf[2] + mb_buf[3])
    send_or_keep(xp_send, xp_buf, XP, XP, swap)
    ewald_forces()
    receive_features(1)
    gather_part(1, ATOMS, EXT, False)
    finish_layer(1)

    def silu_slope(pre):
        sig = lax.logistic(pre)
        return sig * (1.0 + pre * (1.0 - sig))

    final = dot(readout_t[...], hidden[...].astype(BF16))
    dfinal = ew_col * silu_slope(final)
    cotan = dot(readout[...], dfinal.astype(BF16)).astype(BF16)

    def message_cotan(layer, cotan_b):
        dgated = dot(update[layer], cotan_b).astype(BF16).astype(F32)
        dpre = dgated * silu_slope(pre_buf[layer])
        dnormed = dot(mix[layer], dpre.astype(BF16)).astype(BF16).astype(F32)
        normed = normed_buf[layer]
        mean = jnp.sum(dnormed * normed, axis=0, keepdims=True) * (1.0 / FEAT)
        dmsg[...] = inv_buf[layer, 0:1, :] * (dnormed - normed * mean)

    def distance_cotan(layer):
        def body(j, carry):
            dedge = (picked[layer, j].astype(F32) * dmsg[...]).astype(BF16)
            dbasis = dot(radial[layer], dedge).astype(BF16).astype(F32)
            part = jnp.sum(dbasis * slope_buf[j], axis=0, keepdims=True)
            if layer == 1:
                ddist_buf[pl.ds(j, 1), :] = part
            else:
                ddist_buf[pl.ds(j, 1), :] += part
            return carry

        lax.fori_loop(0, NEIGH, body, 0, unroll=True)

    message_cotan(1, cotan)

    def row_cotan(j, carry):
        at = pl.multiple_of(j * ATOMS, ATOMS)
        edge = dot(radial_t[1], basis_buf[j])
        d_picked[:, pl.ds(at, ATOMS)] = (edge * dmsg[...]).astype(BF16)
        return carry

    lax.fori_loop(0, NEIGH, row_cotan, 0, unroll=True)
    for side in range(2):
        first = ATOMS + SIDE * side
        dg_send[side] = dot_t(d_picked[...], onehot[first : first + SIDE, :]).astype(BF16)
        send_to(dg_send.at[side], dg_buf.at[1 - side], DG + side, DG + 1 - side, ring_dev(z, 7 if side == 0 else 1))
    for half in range(2):
        drows[:, SIDE * half : SIDE * half + SIDE] = dot_t(
            d_picked[...], onehot[SIDE * half : SIDE * half + SIDE, :]
        )
    distance_cotan(1)
    ewald_group_sum()
    for side in range(2):
        arrive(dg_buf.at[side], DG + side)
    returned = dot_t(dg_buf[0], sel[:, :SIDE]) + dot_t(dg_buf[1], sel[:, SIDE:])
    owned = (drows[...] + returned).astype(BF16).astype(F32)
    message_cotan(0, (cotan.astype(F32) + owned).astype(BF16))
    distance_cotan(0)

    ddist = 2.0 * ddist_buf[...]
    edge_force = [offset_buf[c] * ddist for c in range(3)]
    for c in range(3):
        own = jnp.sum(edge_force[c], axis=0, keepdims=True)
        fo_send[c : c + 1, :] = own
    fo_send[3:4, :] = jnp.zeros((1, ATOMS), F32)

    parts = []
    zero_row = jnp.zeros((1, ATOMS), F32)
    for j in range(NEIGH):
        rows = [edge_force[c][j : j + 1, :] for c in range(3)] + [zero_row] * 5
        parts.append(stacked_parts(jnp.concatenate(rows, 0)))
    force_rows = jnp.concatenate(parts, 1)
    for side in range(2):
        first = ATOMS + SIDE * side
        both = dot_t(force_rows, onehot[first : first + SIDE, :])
        gg_send[side] = both[0:4] + both[8:12]
        send_to(
            gg_send.at[side], gg_buf.at[1 - side], GG + side, GG + 1 - side, swapped_ring_dev(7 if side == 0 else 1)
        )
    both = dot_t(force_rows, onehot[:ATOMS, :])
    fo_send[...] = (fo_send[...] - (both[0:4] + both[8:12])) + ewald_total()
    send_or_keep(fo_send, fo_buf, FO, FO, swap)

    arrive(xp_buf, XP)
    for side in range(2):
        arrive(gg_buf.at[side], GG + side)
    zero4 = jnp.zeros((4, SIDE), F32)
    returned = None
    for side in range(2):
        rows = stacked_parts(jnp.concatenate([gg_buf[side], zero4], 0))
        both = dot_t(rows, sel_own[:, SIDE * side : SIDE * side + SIDE])
        both = both[0:4] + both[8:12]
        returned = both if side == 0 else returned + both
    arrive(fo_buf, FO)
    result = fo_buf[...] - returned
    for c in range(3):
        out[c] = xp_buf[c : c + 1, :]
        out[3 + c] = xp_buf[4 + c : 5 + c, :] + (0.5 * DT) * result[c : c + 1, :]
        out[6 + c] = result[c : c + 1, :]

    for sent in started:
        sent.wait_send()

    @pl.when(jnp.logical_not(same))
    def _():
        for sent in conditional:
            sent.wait_send()


def local(
    positions,
    momenta,
    forces,
    masses,
    charges,
    embedding,
    neighbours,
    send_rows,
    wavevectors,
    radial_weight,
    mix_weight,
    update_weight,
    readout_weight,
    energy_weight,
):
    piece = (3, 1, ATOMS)
    scratch = [
        (piece, F32),
        (piece, F32),
        (piece, F32),
        ((1, ATOMS), F32),
        ((1, ATOMS), F32),
        ((NEIGH, ATOMS), jnp.int32),
        ((3, 128), jnp.int32),
        ((3, KPART), jnp.int32),
        ((2, BASIS, FEAT), BF16),
        ((2, FEAT, FEAT), BF16),
        ((2, FEAT, FEAT), BF16),
        ((FEAT, FEAT), BF16),
        ((1, FEAT), F32),
        ((8, ATOMS), F32),
        ((8, 8, ATOMS), F32),
        ((FEAT, ATOMS), BF16),
        ((16, ATOMS), F32),
        ((16, ATOMS), F32),
        ((4, 8, ATOMS), F32),
        ((4, 8, ATOMS), F32),
        ((4, 4, ATOMS), F32),
        ((4, 4, ATOMS), F32),
        ((2, 4, SIDE), F32),
        ((2, 4, SIDE), F32),
        ((2, 2, FEAT, SIDE), BF16),
        ((2, 2, FEAT, SIDE), BF16),
        ((2, FEAT, SIDE), BF16),
        ((2, FEAT, SIDE), BF16),
        ((2, 2, KPART), F32),
        ((4, 2, KPART), F32),
        ((8, 4, ATOMS), F32),
        ((4, 4, ATOMS), F32),
        ((8, ATOMS), F32),
        ((8, ATOMS), F32),
        ((4, ATOMS), F32),
        ((4, ATOMS), F32),
        ((2, 4, SIDE), F32),
        ((2, 4, SIDE), F32),
        ((ATOMS, 2 * SIDE), BF16),
        ((ATOMS, 2 * SIDE), BF16),
        ((EXT, NEIGH * ATOMS), BF16),
        ((FEAT, EXT), BF16),
        ((2, NEIGH, FEAT, ATOMS), BF16),
        ((FEAT, NEIGH * ATOMS), BF16),
        ((NEIGH, BASIS, ATOMS), BF16),
        ((NEIGH, BASIS, ATOMS), F32),
        ((NEIGH, ATOMS), F32),
        ((NEIGH, ATOMS), F32),
        ((3, NEIGH, ATOMS), F32),
        ((FEAT, ATOMS), F32),
        ((FEAT, ATOMS), F32),
        ((FEAT, ATOMS), F32),
        ((FEAT, ATOMS), F32),
        ((2, FEAT, ATOMS), F32),
        ((2, FEAT, ATOMS), F32),
        ((2, 8, ATOMS), F32),
        ((2, FEAT, FEAT), BF16),
        ((2, FEAT, FEAT), BF16),
        ((FEAT, FEAT), BF16),
        ((2, FEAT, BASIS), BF16),
        ((16, KPART), F32),
        ((KPART, 16), BF16),
        ((16, ATOMS), F32),
        ((KPART, ATOMS), BF16),
        ((KPART, ATOMS), BF16),
    ]
    out = pl.pallas_call(
        step_kernel,
        out_shape=jax.ShapeDtypeStruct((9, 1, ATOMS), F32),
        in_specs=[pl.BlockSpec(memory_space=pltpu.HBM)] * 15,
        out_specs=pl.BlockSpec(memory_space=pltpu.VMEM),
        scratch_shapes=[pltpu.SMEM((3 * BEADS,), F32)]
        + [pltpu.VMEM(shape, kind) for shape, kind in scratch]
        + [
            pltpu.SemaphoreType.DMA((N_SEMS,)),
            pltpu.SemaphoreType.DMA((N_SEMS,)),
            pltpu.SemaphoreType.DMA((14,)),
        ],
        compiler_params=pltpu.CompilerParams(
            collective_id=0, has_side_effects=True, vmem_limit_bytes=60 * 1024 * 1024
        ),
        cost_estimate=pl.CostEstimate(flops=16_000_000_000, bytes_accessed=2_000_000, transcendentals=1_000_000),
    )(
        jnp.asarray(ring_tables()),
        positions,
        momenta,
        forces,
        masses.reshape(1, ATOMS),
        charges.reshape(1, ATOMS),
        embedding.T,
        neighbours,
        send_rows.reshape(3, 128),
        wavevectors,
        radial_weight,
        mix_weight,
        update_weight,
        readout_weight,
        energy_weight.reshape(1, FEAT),
    )
    return out[0:3], out[3:6], out[6:9]


def solution(mesh):
    own = P(None, "bead", "dom")
    placed = (
        own,
        own,
        own,
        P("dom"),
        P("dom"),
        P("dom", None),
        P(None, "dom"),
        P("dom"),
        P(),
        P(),
        P(),
        P(),
        P(),
        P(),
    )
    return jax.shard_map(local, mesh=mesh, in_specs=placed, out_specs=(own, own, own), check_vma=False)
```

```python
import math

import jax
import jax.numpy as jnp
import numpy as np
from jax import lax
from jax.experimental import pallas as pl
from jax.experimental.pallas import tpu as pltpu
from jax.sharding import PartitionSpec as P

MESH = pl.DeviceIdType.MESH
F32 = jnp.float32
BF16 = jnp.bfloat16

BEADS = 32
ATOMS = 512
TOTAL_ATOMS = 4096
GHOST = 192
SIDE = 256
EXT = ATOMS + 2 * SIDE
NEIGH = 8
FEAT = 240
BASIS = 16
KVEC = 16384
KPART = KVEC // BEADS
DT = 0.25
TWO_PI = 2.0 * math.pi
PACKED = FEAT + 128

S1, EMB, PACK, MA, MB, GH, FG, DG, SA, SB, E1, E2, XP, FO, GG, N_SEMS = np.cumsum(
    [0, 8, 1, 1, 4, 4, 2, 4, 2, 1, 4, 8, 4, 1, 1, 2]
).tolist()


def ring_tables():
    k = np.arange(BEADS)
    b = np.arange(BEADS)[:, None]
    angle = 2.0 * np.pi / BEADS * (b * k % BEADS)
    half = BEADS // 2
    basis = np.where(k < half, np.cos(angle), np.sin(angle)) * math.sqrt(2.0 / BEADS)
    basis = np.where(k == 0, math.sqrt(1.0 / BEADS), basis)
    basis = np.where(k == half, math.sqrt(1.0 / BEADS) * (1 - 2 * (b % 2)), basis)
    omega = 3.2 * np.sin(np.pi * k / BEADS)
    cosine, sine = np.cos(omega * DT), np.sin(omega * DT)
    drift = np.where(k == 0, DT, sine / np.where(k == 0, 1.0, omega))
    rows = [(basis * value) @ basis.T for value in (cosine, drift, omega * sine)]
    return np.concatenate([row[0] for row in rows]).astype(np.float32)


def dot(a, b):
    return lax.dot_general(a, b, (((1,), (0,)), ((), ())), preferred_element_type=F32)


def dot_t(a, b):
    return lax.dot_general(a, b, (((1,), (1,)), ((), ())), preferred_element_type=F32)


def rows_of(shape):
    return lax.broadcasted_iota(jnp.int32, shape, 0)


def lanes_of(shape):
    return lax.broadcasted_iota(jnp.int32, shape, 1)


def two_parts(value):
    high = value.astype(BF16)
    return high, (value - high.astype(F32)).astype(BF16)


def stacked_parts(value):
    high = value.astype(BF16).astype(F32)
    return jnp.concatenate([high, value - high], 0).astype(BF16)


def lane_pick(tables, index):
    result = None
    for number, block in enumerate(tables):
        local = index - 128 * number
        inside = jnp.logical_and(local >= 0, local < 128)
        got = jnp.take_along_axis(block, jnp.where(inside, local, 0), axis=1, mode="promise_in_bounds")
        result = jnp.where(inside, got, 0.0 if result is None else result)
    return result


def step_kernel(
    coef_in,
    pos_in,
    mom_in,
    force_in,
    mass_in,
    charge_in,
    emb,
    neigh_in,
    send_in,
    wave_in,
    radial_in,
    mix_in,
    update_in,
    readout_in,
    ew_in,
    out,
    coef,
    pos,
    mom,
    force,
    mass,
    charge,
    neigh,
    send,
    wave,
    radial,
    mix,
    update,
    readout,
    ew,
    v_own,
    v_all,
    emb_buf,
    pack_own,
    pack_buf,
    ma_send,
    ma_buf,
    mb_send,
    mb_buf,
    gh_send,
    gh_buf,
    fg_send,
    fg_buf,
    dg_send,
    dg_buf,
    dg_rows,
    sa_buf,
    sb_buf,
    e1_buf,
    e2_buf,
    xp_send,
    xp_buf,
    fo_send,
    fo_buf,
    gg_send,
    gg_buf,
    sel,
    sel_own,
    onehot,
    ext_rows,
    picked,
    d_picked,
    basis_buf,
    slope_buf,
    dist_buf,
    ddist_buf,
    offset_buf,
    msg,
    dmsg,
    drows,
    hidden,
    pre_buf,
    normed_buf,
    inv_buf,
    mix_t,
    update_t,
    readout_t,
    radial_t,
    wave_buf,
    wave_t,
    r_buf,
    cos_buf,
    sin_buf,
    send_sem,
    recv_sem,
    load_sem,
):
    bead = lax.axis_index("bead")
    dom = lax.axis_index("dom")
    z, x, core = bead // 8, (bead // 2) % 4, bead % 2
    y, low = dom // 2, dom % 2
    ring = 2 * y + core

    def dev(z_, x_, y_, low_, core_):
        return ((z_ * 4 + x_) * 2 + core_, y_ * 2 + low_)

    def ring_dev(z_, step):
        place = (ring + step) % 8
        return dev(z_, x, place // 2, low, place % 2)

    def swapped_ring_dev(step):
        place = (ring + step) % 8
        return dev(z, x, place // 2, place % 2, low)

    def copy(src, dst, send_at, recv_at, target):
        return pltpu.make_async_remote_copy(
            src_ref=src,
            dst_ref=dst,
            send_sem=send_sem.at[send_at],
            recv_sem=recv_sem.at[recv_at],
            device_id=target,
            device_id_type=MESH,
        )

    def arrive(dst, recv_at):
        copy(dst, dst, 0, recv_at, dev(z, x, y, low, 1 - core)).wait_recv()

    started = []

    def send_to(src, dst, send_at, recv_at, target):
        sent = copy(src, dst, send_at, recv_at, target)
        sent.start()
        started.append(sent)

    k_first = pl.multiple_of((bead - core + low) * KPART, KPART)
    loads = {}
    for number, (src, dst) in enumerate(
        (
            (pos_in, pos),
            (mom_in, mom),
            (force_in, force),
            (mass_in, mass),
            (charge_in, charge),
            (neigh_in, neigh),
            (send_in, send),
            (coef_in, coef),
            (radial_in, radial),
            (mix_in, mix),
            (update_in, update),
            (readout_in, readout),
            (ew_in, ew),
            (wave_in.at[:, pl.ds(k_first, KPART)], wave),
        )
    ):
        loads[number] = pltpu.make_async_copy(src, dst, load_sem.at[number])
        loads[number].start()

    same = low == core
    conditional = []

    def send_or_keep(src, dst, send_at, recv_at, target):
        sent = copy(src, dst, send_at, recv_at, target)

        @pl.when(same)
        def _():
            pltpu.make_async_copy(src, dst, recv_sem.at[recv_at]).start()

        @pl.when(jnp.logical_not(same))
        def _():
            sent.start()

        conditional.append(sent)

    barrier = pltpu.get_barrier_semaphore()

    def greet(target):
        pl.semaphore_signal(barrier, inc=1, device_id=target, device_id_type=MESH)

    far = dev((z + 3 + 2 * low) % 4, x, y, 1 - low, low)
    for dz in (2, 1, 3):
        greet(dev((z + dz) % 4, x, y, low, core))
    greet(ring_dev(z, 4))
    for dx, flip in ((2, 1), (2, 0), (1, 1), (3, 1), (1, 0), (3, 0)):
        greet(dev(z, (x + dx) % 4, y, core, (low + flip) % 2))

    @pl.when(jnp.logical_not(same))
    def _():
        greet(far)
        greet(dev(z, x, y, core, low))

    greet(ring_dev(z, 7 - 6 * core))
    greet(dev(z, x, y, core, 1 - low))
    greet(ring_dev(z, 1 + 6 * core))

    for number in range(7):
        loads[number].wait()
    v_own[...] = jnp.zeros((8, ATOMS), F32)
    for c in range(3):
        v_own[c : c + 1, :] = pos[c]
        v_own[4 + c : 5 + c, :] = mom[c] + (0.5 * DT) * force[c]
    lane = lanes_of((1, 2 * SIDE))
    rows384 = jnp.concatenate(
        [send[0:1, :], send[1:2, :], send[2:3, :], jnp.zeros((1, 128), jnp.int32)], 1
    )
    shifted = pltpu.roll(rows384, 64, 1)
    spread = jnp.where(
        lane < GHOST,
        rows384,
        jnp.where(jnp.logical_and(lane >= SIDE, lane < SIDE + GHOST), shifted, -1),
    ).astype(F32)
    table = neigh[...]
    pack_own[0:8, :] = jnp.where(table >= ATOMS + GHOST, table + (SIDE - GHOST), table).astype(F32)
    pack_own[8:9, :] = mass[...]
    pack_own[9:10, :] = charge[...]
    pack_own[10:11, :] = spread
    pack_own[11:16, :] = jnp.zeros((5, ATOMS), F32)
    pl.semaphore_wait(barrier, 13 + 2 * jnp.where(same, 0, 1))

    slot = x * 2 + core
    for dx, dl in ((2, 1), (2, 0), (1, 1), (3, 1), (1, 0), (3, 0), (0, 1)):
        send_to(
            v_own,
            v_all.at[slot],
            S1 + 2 * dx + dl,
            S1 + slot,
            dev(z, (x + dx) % 4, y, (low + dl) % 2, low),
        )
    send_or_keep(v_own, v_all.at[slot], S1, S1 + slot, dev(z, x, y, low, low))
    swap = dev(z, x, y, core, low)
    send_or_keep(pack_own, pack_buf, PACK, PACK, far)
    send_or_keep(emb, emb_buf, EMB, EMB, far)

    for number in range(7, 14):
        loads[number].wait()

    eye = (rows_of((FEAT, FEAT)) == lanes_of((FEAT, FEAT))).astype(F32)
    eye_b = eye.astype(BF16)
    for layer in range(2):
        mix_t[layer] = dot_t(eye_b, mix[layer]).astype(BF16)
        update_t[layer] = dot_t(eye_b, update[layer]).astype(BF16)
        radial_t[layer] = dot_t(eye_b, radial[layer]).astype(BF16)
    readout_t[...] = dot_t(eye_b, readout[...]).astype(BF16)
    ew_col = jnp.sum(eye * ew[...], axis=1, keepdims=True)
    own_spread = jnp.broadcast_to(spread, (ATOMS, 2 * SIDE))
    atom_rows = rows_of((ATOMS, 2 * SIDE)).astype(F32)
    sel_own[...] = jnp.where(own_spread == atom_rows, 1.0, 0.0).astype(BF16)
    triple = wave[...].astype(F32)
    wave_buf[...] = jnp.zeros((16, KPART), F32)
    for part in range(3):
        wave_buf[4 * part : 4 * part + 3, :] = triple
    wave_t[...] = jnp.transpose(wave_buf[...]).astype(BF16)

    arrive(pack_buf, PACK)
    inv_mass = 1.0 / pack_buf[8:9, :]
    charges = pack_buf[9:10, :]
    send_row = pack_buf[10:11, :]
    sel[...] = jnp.where(jnp.broadcast_to(send_row, (ATOMS, 2 * SIDE)) == atom_rows, 1.0, 0.0).astype(BF16)
    send_index = jnp.broadcast_to(send_row, (8, 2 * SIDE)).astype(jnp.int32)

    for k in range(8):
        arrive(v_all.at[k], S1 + k)
    row8 = rows_of((8, ATOMS))
    upper = row8 < 4
    scale = jnp.where(upper, inv_mass, -pack_buf[8:9, :])
    beads_in = [v_all[k] for k in range(8)]
    total = beads_in[0]
    for k in range(1, 8):
        total = total + beads_in[k]
    centre_part = (total + DT * inv_mass * pltpu.roll(total, 4, 0)) * (1.0 / BEADS)
    centre_low = pltpu.roll(centre_part, 4, 0)
    first_row = rows_of((8, 1)) < 4
    for dz in (2, 1, 3, 0):
        z_to = (z + dz) % 4
        straight = None
        for k in range(8):
            shift = (8 * (z_to - z) + 2 * x + low - k + 64) % BEADS
            same_kind = coef[shift] * beads_in[k]
            other = jnp.where(first_row, coef[2 * BEADS + shift], coef[BEADS + shift]) * beads_in[k]
            straight = same_kind if straight is None else straight + same_kind
            crossed = other if k == 0 else crossed + other
        moved = straight + scale * pltpu.roll(crossed, 4, 0)
        ma = jnp.where(upper, moved, centre_low)
        if dz:
            ma_send[dz] = ma
            mb_send[dz] = moved[4:8]
            send_to(ma_send.at[dz], ma_buf.at[z], MA + dz, MA + z, ring_dev(z_to, 0))
        else:
            ma_buf[z] = ma
            mb_buf[z] = moved[4:8]

    def pack_side(ref, value):
        ref[0:FEAT, :] = value[:, 0:128].astype(BF16)
        rest = jnp.concatenate([value[128:FEAT, 128:SIDE], jnp.zeros((256 - FEAT, 128), F32)], 0)
        ref[FEAT:PACKED, :] = (value[0:128, 128:SIDE] + pltpu.roll(rest, 64, 1)).astype(BF16)

    def unpack_side(ref, packed, first):
        ref[:, first : first + 128] = packed[0:FEAT, :]
        rest = packed[FEAT:PACKED, :].astype(F32)
        ref[0:128, first + 128 : first + SIDE] = rest.astype(BF16)
        ref[128:FEAT, first + 128 : first + SIDE] = pltpu.roll(rest, 64, 1)[0 : FEAT - 128].astype(BF16)

    def send_sides(src, dst, first_sem):
        for near in range(2):
            side = core if near == 0 else 1 - core
            send_to(
                src.at[side], dst.at[1 - side], first_sem + side, first_sem + 1 - side, ring_dev(z, 7 - 6 * side)
            )

    def send_features(layer, rounded):
        ghosts = dot(rounded, sel[...])
        for side in range(2):
            pack_side(fg_send.at[layer, side], ghosts[:, SIDE * side : SIDE * (side + 1)])
        send_sides(fg_send.at[layer], fg_buf.at[layer], FG + 2 * layer)

    def receive_features(layer):
        for side in range(2):
            arrive(fg_buf.at[layer, side], FG + 2 * layer + side)
            unpack_side(ext_rows, fg_buf.at[layer, side], ATOMS + SIDE * side)

    arrive(emb_buf, EMB)
    rounded = emb_buf[...]
    hidden[...] = rounded.astype(F32)
    ext_rows[:, :ATOMS] = rounded
    send_features(0, rounded)
    for dz in range(1, 4):
        send_to(mb_send.at[dz], mb_buf.at[z], MB + dz, MB + z, ring_dev((z + dz) % 4, 0))

    group_rows = [(rows_of((16, ATOMS)) + 16 * g).astype(F32) for g in range(8)]

    def build(j, carry):
        index = pack_buf[pl.ds(j, 1), :]
        at = pl.multiple_of(j * ATOMS, ATOMS)
        for block in range(EXT // 128):
            local = jnp.broadcast_to(index - 128.0 * block, (16, ATOMS))
            for g in range(8):
                first = 128 * block + 16 * g
                onehot[first : first + 16, pl.ds(at, ATOMS)] = jnp.where(
                    local == group_rows[g], 1.0, 0.0
                ).astype(BF16)
        return carry

    lax.fori_loop(0, NEIGH, build, 0)

    def gather_part(layer, first, last, fresh):
        def body(j, carry):
            at = pl.multiple_of(j * ATOMS, ATOMS)
            part = dot(ext_rows[:, first:last], onehot[first:last, pl.ds(at, ATOMS)])
            if not fresh:
                part = part + picked[layer, j].astype(F32)
            picked[layer, j] = part.astype(BF16)
            return carry

        lax.fori_loop(0, NEIGH, body, 0, unroll=True)

    gather_part(0, 0, ATOMS, True)

    for dz in range(1, 4):
        arrive(ma_buf.at[(z + dz) % 4], MA + (z + dz) % 4)
    moved = (ma_buf[0] + ma_buf[1]) + (ma_buf[2] + ma_buf[3])
    centre = moved[4:7]
    xp_send[...] = moved
    for c in range(3):
        blocks = [
            jnp.broadcast_to(moved[c : c + 1, 128 * n : 128 * n + 128], (8, 128)) for n in range(4)
        ]
        for n in range(4):
            got = lane_pick(blocks, send_index[:, 128 * n : 128 * n + 128])
            gh_send[n // 2, c : c + 1, 128 * (n % 2) : 128 * (n % 2) + 128] = got[0:1]
    gh_send[:, 3:4, :] = jnp.zeros((2, 1, SIDE), F32)
    send_sides(gh_send, gh_buf, GH)
    receive_features(0)
    gather_part(0, ATOMS, EXT, False)
    turns = centre * 0.25
    high = turns.astype(BF16).astype(F32)
    rest = turns - high
    middle = rest.astype(BF16).astype(F32)
    r_buf[...] = jnp.zeros((16, ATOMS), F32)
    for number, value in enumerate((high, middle, rest - middle)):
        r_buf[4 * number : 4 * number + 3, :] = value

    def ewald_sums():
        phase = r_buf[...].astype(BF16)

        def body(i, carry):
            at = pl.multiple_of(i * 128, 128)
            turn = dot(wave_t[pl.ds(at, 128), :], phase)
            half = (turn - jnp.round(turn)) * math.pi
            q = half * half
            s = half * (
                1.0
                + q
                * (
                    -1.6666666641e-1
                    + q * (8.3333293858e-3 + q * (-1.9840083133e-4 + q * (2.7523971075e-6 - 2.3868346521e-8 * q)))
                )
            )
            c = 1.0 + q * (
                -0.5
                + q
                * (
                    4.1666666658e-2
                    + q
                    * (
                        -1.3888888388e-3
                        + q * (2.4801544910e-5 + q * (-2.7556993055e-7 + 2.0737354e-9 * q))
                    )
                )
            )
            sin_buf[pl.ds(at, 128), :] = (2.0 * s * c).astype(BF16)
            cos_buf[pl.ds(at, 128), :] = (1.0 - 2.0 * s * s).astype(BF16)
            return carry

        lax.fori_loop(0, KPART // 128, body, 0, unroll=True)
        weights = stacked_parts(jnp.broadcast_to(charges, (8, ATOMS)))
        for number, ref in enumerate((cos_buf, sin_buf)):
            sums = dot_t(weights, ref[...])
            sa_buf[core, number : number + 1, :] = sums[0:1] + sums[8:9]

    def ewald_ring():
        arrive(sa_buf.at[1 - core], SA)
        sb_buf[y] = sa_buf[0] + sa_buf[1]
        for dy in range(1, 4):
            send_to(sb_buf.at[y], sb_buf.at[y], SB + dy, SB + y, dev(z, x, (y + dy) % 4, low, core))

    ewald_sums()
    ghosts_at = []
    for side in range(2):
        arrive(gh_buf.at[side], GH + side)
        ghosts_at.append(gh_buf[side])
    send_to(sa_buf.at[core], sa_buf.at[core], SA, SA, dev(z, x, y, low, 1 - core))
    index8 = pack_buf[0:8, :].astype(jnp.int32)
    distance = None
    for c in range(3):
        blocks = [moved[c : c + 1, 128 * n : 128 * n + 128] for n in range(4)]
        for side in range(2):
            blocks += [ghosts_at[side][c : c + 1, 128 * n : 128 * n + 128] for n in range(2)]
        blocks = [jnp.broadcast_to(block, (8, 128)) for block in blocks]
        others = jnp.concatenate(
            [lane_pick(blocks, index8[:, 128 * n : 128 * n + 128]) for n in range(4)], 1
        )
        offset = others - moved[c : c + 1, :]
        offset_buf[c] = offset
        distance = offset * offset if c == 0 else distance + offset * offset
    dist_buf[...] = distance
    m_row = rows_of((BASIS, ATOMS))
    rates = jnp.where(m_row % 2 == 1, 0.125 * math.sqrt(2.0), 0.125) * jnp.left_shift(1, m_row // 2).astype(F32)
    for j in range(NEIGH):
        exact = 1.0 / (1.0 + rates * dist_buf[j : j + 1, :])
        basis_buf[j] = exact.astype(BF16)
        slope_buf[j] = -rates * exact * exact

    def ewald_forces():
        for dy in range(1, 4):
            arrive(sb_buf.at[(y + dy) % 4], SB + (y + dy) % 4)
        sums = (sb_buf[0] + sb_buf[1]) + (sb_buf[2] + sb_buf[3])
        recip = wave_buf[0:8, :] * (TWO_PI / 4.0)
        recip = jnp.where(row8 < 3, recip, 0.0)
        square = jnp.sum(recip * recip, axis=0, keepdims=True)
        damping = 48.0 / math.sqrt(KVEC * TOTAL_ATOMS) * jnp.exp(-0.002 * square) / square
        from_sin = stacked_parts(recip * (damping * sums[0:1]))
        from_cos = stacked_parts(recip * (damping * sums[1:2]))
        part = dot(from_sin, sin_buf[...]) - dot(from_cos, cos_buf[...])
        part = 2.0 * charges * (part[0:8] + part[8:16])
        place = 2 * x + low
        e1_buf[place] = part[0:4]
        for number in range(1, 8):
            dx, dl = number // 2, number % 2
            send_to(
                e1_buf.at[place],
                e1_buf.at[place],
                E1 + number,
                E1 + place,
                dev(z, (x + dx) % 4, y, (low + dl) % 2, core),
            )

    def ewald_group_sum():
        for number in range(1, 8):
            place = 2 * ((x + number // 2) % 4) + (low + number % 2) % 2
            arrive(e1_buf.at[place], E1 + place)
        part = e1_buf[0]
        for k in range(1, 8):
            part = part + e1_buf[k]
        e2_buf[z] = part
        for dz in range(1, 4):
            send_to(e2_buf.at[z], e2_buf.at[z], E2 + dz, E2 + z, ring_dev((z + dz) % 4, 0))

    def ewald_total():
        for dz in range(1, 4):
            arrive(e2_buf.at[(z + dz) % 4], E2 + (z + dz) % 4)
        return (e2_buf[0] + e2_buf[1]) + (e2_buf[2] + e2_buf[3])

    def finish_layer(layer):
        msg[...] = jnp.zeros((FEAT, ATOMS), F32)

        def body(j, carry):
            edge = dot(radial_t[layer], basis_buf[j])
            msg[...] += edge * picked[layer, j].astype(F32)
            return carry

        lax.fori_loop(0, NEIGH, body, 0, unroll=True)
        message = msg[...]
        inverse = lax.rsqrt(jnp.sum(message * message, axis=0, keepdims=True) * (1.0 / FEAT) + 1e-6)
        normed = message * inverse
        normed_buf[layer] = normed
        inv_buf[layer] = jnp.broadcast_to(inverse, (8, ATOMS))
        pre = dot(mix_t[layer], normed.astype(BF16))
        pre_buf[layer] = pre
        gated = (pre * lax.logistic(pre)).astype(BF16)
        hidden[...] += dot(update_t[layer], gated)

    ewald_ring()
    finish_layer(0)
    rounded = hidden[...].astype(BF16)
    ext_rows[:, :ATOMS] = rounded
    send_features(1, rounded)
    gather_part(1, 0, ATOMS, True)
    for dz in range(1, 4):
        arrive(mb_buf.at[(z + dz) % 4], MB + (z + dz) % 4)
    xp_send[4:8, :] = (mb_buf[0] + mb_buf[1]) + (mb_buf[2] + mb_buf[3])
    send_or_keep(xp_send, xp_buf, XP, XP, swap)
    ewald_forces()
    receive_features(1)
    gather_part(1, ATOMS, EXT, False)
    finish_layer(1)

    def silu_slope(pre):
        sig = lax.logistic(pre)
        return sig * (1.0 + pre * (1.0 - sig))

    final = dot(readout_t[...], hidden[...].astype(BF16))
    dfinal = ew_col * silu_slope(final)
    cotan = dot(readout[...], dfinal.astype(BF16)).astype(BF16)

    def message_cotan(layer, cotan_b):
        dgated = dot(update[layer], cotan_b).astype(BF16).astype(F32)
        dpre = dgated * silu_slope(pre_buf[layer])
        dnormed = dot(mix[layer], dpre.astype(BF16)).astype(BF16).astype(F32)
        normed = normed_buf[layer]
        mean = jnp.sum(dnormed * normed, axis=0, keepdims=True) * (1.0 / FEAT)
        dmsg[...] = inv_buf[layer, 0:1, :] * (dnormed - normed * mean)

    def distance_cotan(layer):
        def body(j, carry):
            dedge = (picked[layer, j].astype(F32) * dmsg[...]).astype(BF16)
            dbasis = dot(radial[layer], dedge).astype(BF16).astype(F32)
            part = jnp.sum(dbasis * slope_buf[j], axis=0, keepdims=True)
            if layer == 1:
                ddist_buf[pl.ds(j, 1), :] = part
            else:
                ddist_buf[pl.ds(j, 1), :] += part
            return carry

        lax.fori_loop(0, NEIGH, body, 0, unroll=True)

    message_cotan(1, cotan)

    def row_cotan(j, carry):
        at = pl.multiple_of(j * ATOMS, ATOMS)
        edge = dot(radial_t[1], basis_buf[j])
        d_picked[:, pl.ds(at, ATOMS)] = (edge * dmsg[...]).astype(BF16)
        return carry

    lax.fori_loop(0, NEIGH, row_cotan, 0, unroll=True)
    for near in range(2):
        side = core if near == 0 else 1 - core
        first = pl.multiple_of(ATOMS + SIDE * side, SIDE)
        pack_side(dg_send.at[side], dot_t(d_picked[...], onehot[pl.ds(first, SIDE), :]))
        send_to(dg_send.at[side], dg_buf.at[1 - side], DG + side, DG + 1 - side, ring_dev(z, 7 - 6 * side))
    for half in range(2):
        drows[:, SIDE * half : SIDE * half + SIDE] = dot_t(
            d_picked[...], onehot[SIDE * half : SIDE * half + SIDE, :]
        )
    distance_cotan(1)
    ewald_group_sum()
    for near in (1, 0):
        side = core if near == 0 else 1 - core
        arrive(dg_buf.at[side], DG + side)
    for side in range(2):
        unpack_side(dg_rows, dg_buf.at[side], SIDE * side)
    returned = dot_t(dg_rows[...], sel[...])
    owned = (drows[...] + returned).astype(BF16).astype(F32)
    message_cotan(0, (cotan.astype(F32) + owned).astype(BF16))
    distance_cotan(0)

    ddist = 2.0 * ddist_buf[...]
    edge_force = [offset_buf[c] * ddist for c in range(3)]
    for c in range(3):
        own = jnp.sum(edge_force[c], axis=0, keepdims=True)
        fo_send[c : c + 1, :] = own
    fo_send[3:4, :] = jnp.zeros((1, ATOMS), F32)

    parts = []
    zero_row = jnp.zeros((1, ATOMS), F32)
    for j in range(NEIGH):
        rows = [edge_force[c][j : j + 1, :] for c in range(3)] + [zero_row] * 5
        parts.append(stacked_parts(jnp.concatenate(rows, 0)))
    force_rows = jnp.concatenate(parts, 1)
    for side in range(2):
        first = ATOMS + SIDE * side
        both = dot_t(force_rows, onehot[first : first + SIDE, :])
        gg_send[side] = both[0:4] + both[8:12]
        send_to(
            gg_send.at[side], gg_buf.at[1 - side], GG + side, GG + 1 - side, swapped_ring_dev(7 if side == 0 else 1)
        )
    both = dot_t(force_rows, onehot[:ATOMS, :])
    fo_send[...] = (fo_send[...] - (both[0:4] + both[8:12])) + ewald_total()
    send_or_keep(fo_send, fo_buf, FO, FO, swap)

    arrive(xp_buf, XP)
    for side in range(2):
        arrive(gg_buf.at[side], GG + side)
    zero4 = jnp.zeros((4, SIDE), F32)
    returned = None
    for side in range(2):
        rows = stacked_parts(jnp.concatenate([gg_buf[side], zero4], 0))
        both = dot_t(rows, sel_own[:, SIDE * side : SIDE * side + SIDE])
        both = both[0:4] + both[8:12]
        returned = both if side == 0 else returned + both
    arrive(fo_buf, FO)
    result = fo_buf[...] - returned
    for c in range(3):
        out[c] = xp_buf[c : c + 1, :]
        out[3 + c] = xp_buf[4 + c : 5 + c, :] + (0.5 * DT) * result[c : c + 1, :]
        out[6 + c] = result[c : c + 1, :]

    for sent in started:
        sent.wait_send()

    @pl.when(jnp.logical_not(same))
    def _():
        for sent in conditional:
            sent.wait_send()


def local(
    positions,
    momenta,
    forces,
    masses,
    charges,
    embedding,
    neighbours,
    send_rows,
    wavevectors,
    radial_weight,
    mix_weight,
    update_weight,
    readout_weight,
    energy_weight,
):
    piece = (3, 1, ATOMS)
    scratch = [
        (piece, F32),
        (piece, F32),
        (piece, F32),
        ((1, ATOMS), F32),
        ((1, ATOMS), F32),
        ((NEIGH, ATOMS), jnp.int32),
        ((3, 128), jnp.int32),
        ((3, KPART), jnp.int32),
        ((2, BASIS, FEAT), BF16),
        ((2, FEAT, FEAT), BF16),
        ((2, FEAT, FEAT), BF16),
        ((FEAT, FEAT), BF16),
        ((1, FEAT), F32),
        ((8, ATOMS), F32),
        ((8, 8, ATOMS), F32),
        ((FEAT, ATOMS), BF16),
        ((16, ATOMS), F32),
        ((16, ATOMS), F32),
        ((4, 8, ATOMS), F32),
        ((4, 8, ATOMS), F32),
        ((4, 4, ATOMS), F32),
        ((4, 4, ATOMS), F32),
        ((2, 4, SIDE), F32),
        ((2, 4, SIDE), F32),
        ((2, 2, PACKED, 128), BF16),
        ((2, 2, PACKED, 128), BF16),
        ((2, PACKED, 128), BF16),
        ((2, PACKED, 128), BF16),
        ((FEAT, 2 * SIDE), BF16),
        ((2, 2, KPART), F32),
        ((4, 2, KPART), F32),
        ((8, 4, ATOMS), F32),
        ((4, 4, ATOMS), F32),
        ((8, ATOMS), F32),
        ((8, ATOMS), F32),
        ((4, ATOMS), F32),
        ((4, ATOMS), F32),
        ((2, 4, SIDE), F32),
        ((2, 4, SIDE), F32),
        ((ATOMS, 2 * SIDE), BF16),
        ((ATOMS, 2 * SIDE), BF16),
        ((EXT, NEIGH * ATOMS), BF16),
        ((FEAT, EXT), BF16),
        ((2, NEIGH, FEAT, ATOMS), BF16),
        ((FEAT, NEIGH * ATOMS), BF16),
        ((NEIGH, BASIS, ATOMS), BF16),
        ((NEIGH, BASIS, ATOMS), F32),
        ((NEIGH, ATOMS), F32),
        ((NEIGH, ATOMS), F32),
        ((3, NEIGH, ATOMS), F32),
        ((FEAT, ATOMS), F32),
        ((FEAT, ATOMS), F32),
        ((FEAT, ATOMS), F32),
        ((FEAT, ATOMS), F32),
        ((2, FEAT, ATOMS), F32),
        ((2, FEAT, ATOMS), F32),
        ((2, 8, ATOMS), F32),
        ((2, FEAT, FEAT), BF16),
        ((2, FEAT, FEAT), BF16),
        ((FEAT, FEAT), BF16),
        ((2, FEAT, BASIS), BF16),
        ((16, KPART), F32),
        ((KPART, 16), BF16),
        ((16, ATOMS), F32),
        ((KPART, ATOMS), BF16),
        ((KPART, ATOMS), BF16),
    ]
    out = pl.pallas_call(
        step_kernel,
        out_shape=jax.ShapeDtypeStruct((9, 1, ATOMS), F32),
        in_specs=[pl.BlockSpec(memory_space=pltpu.HBM)] * 15,
        out_specs=pl.BlockSpec(memory_space=pltpu.VMEM),
        scratch_shapes=[pltpu.SMEM((3 * BEADS,), F32)]
        + [pltpu.VMEM(shape, kind) for shape, kind in scratch]
        + [
            pltpu.SemaphoreType.DMA((N_SEMS,)),
            pltpu.SemaphoreType.DMA((N_SEMS,)),
            pltpu.SemaphoreType.DMA((14,)),
        ],
        compiler_params=pltpu.CompilerParams(
            collective_id=0, has_side_effects=True, vmem_limit_bytes=60 * 1024 * 1024
        ),
        cost_estimate=pl.CostEstimate(flops=16_000_000_000, bytes_accessed=2_000_000, transcendentals=1_000_000),
    )(
        jnp.asarray(ring_tables()),
        positions,
        momenta,
        forces,
        masses.reshape(1, ATOMS),
        charges.reshape(1, ATOMS),
        embedding.T,
        neighbours,
        send_rows.reshape(3, 128),
        wavevectors,
        radial_weight,
        mix_weight,
        update_weight,
        readout_weight,
        energy_weight.reshape(1, FEAT),
    )
    return out[0:3], out[3:6], out[6:9]


def solution(mesh):
    own = P(None, "bead", "dom")
    placed = (
        own,
        own,
        own,
        P("dom"),
        P("dom"),
        P("dom", None),
        P(None, "dom"),
        P("dom"),
        P(),
        P(),
        P(),
        P(),
        P(),
        P(),
    )
    return jax.shard_map(local, mesh=mesh, in_specs=placed, out_specs=(own, own, own), check_vma=False)
```

```python
import math

import jax
import jax.numpy as jnp
import numpy as np
from jax import lax
from jax.experimental import pallas as pl
from jax.experimental.pallas import tpu as pltpu
from jax.sharding import PartitionSpec as P

MESH = pl.DeviceIdType.MESH
F32 = jnp.float32
BF16 = jnp.bfloat16

BEADS = 32
ATOMS = 512
TOTAL_ATOMS = 4096
GHOST = 192
SIDE = 256
EXT = ATOMS + 2 * SIDE
NEIGH = 8
FEAT = 240
BASIS = 16
KVEC = 16384
KPART = KVEC // BEADS
DT = 0.25
TWO_PI = 2.0 * math.pi
PACKED = FEAT + 128

S1, EMB, PACK, MA, MB, GH, FG, DG, SA, SB, E1, E2, XP, FO, GG, N_SEMS = np.cumsum(
    [0, 8, 1, 1, 4, 4, 2, 4, 2, 1, 4, 4, 8, 1, 1, 2]
).tolist()


def ring_tables():
    k = np.arange(BEADS)
    b = np.arange(BEADS)[:, None]
    angle = 2.0 * np.pi / BEADS * (b * k % BEADS)
    half = BEADS // 2
    basis = np.where(k < half, np.cos(angle), np.sin(angle)) * math.sqrt(2.0 / BEADS)
    basis = np.where(k == 0, math.sqrt(1.0 / BEADS), basis)
    basis = np.where(k == half, math.sqrt(1.0 / BEADS) * (1 - 2 * (b % 2)), basis)
    omega = 3.2 * np.sin(np.pi * k / BEADS)
    cosine, sine = np.cos(omega * DT), np.sin(omega * DT)
    drift = np.where(k == 0, DT, sine / np.where(k == 0, 1.0, omega))
    rows = [(basis * value) @ basis.T for value in (cosine, drift, omega * sine)]
    return np.concatenate([row[0] for row in rows]).astype(np.float32)


def dot(a, b):
    return lax.dot_general(a, b, (((1,), (0,)), ((), ())), preferred_element_type=F32)


def dot_t(a, b):
    return lax.dot_general(a, b, (((1,), (1,)), ((), ())), preferred_element_type=F32)


def rows_of(shape):
    return lax.broadcasted_iota(jnp.int32, shape, 0)


def lanes_of(shape):
    return lax.broadcasted_iota(jnp.int32, shape, 1)


def two_parts(value):
    high = value.astype(BF16)
    return high, (value - high.astype(F32)).astype(BF16)


def stacked_parts(value):
    high = value.astype(BF16).astype(F32)
    return jnp.concatenate([high, value - high], 0).astype(BF16)


def lane_pick(tables, index):
    result = None
    for number, block in enumerate(tables):
        local = index - 128 * number
        inside = jnp.logical_and(local >= 0, local < 128)
        got = jnp.take_along_axis(block, jnp.where(inside, local, 0), axis=1, mode="promise_in_bounds")
        result = jnp.where(inside, got, 0.0 if result is None else result)
    return result


def step_kernel(
    coef_in,
    pos_in,
    mom_in,
    force_in,
    mass_in,
    charge_in,
    emb,
    neigh_in,
    send_in,
    wave_in,
    radial_in,
    mix_in,
    update_in,
    readout_in,
    ew_in,
    out,
    coef,
    pos,
    mom,
    force,
    mass,
    charge,
    neigh,
    send,
    wave,
    radial,
    mix,
    update,
    readout,
    ew,
    v_own,
    v_all,
    emb_buf,
    pack_own,
    pack_buf,
    ma_send,
    ma_buf,
    mb_send,
    mb_buf,
    gh_send,
    gh_buf,
    fg_send,
    fg_buf,
    dg_send,
    dg_buf,
    dg_rows,
    sa_buf,
    sb_buf,
    e1_buf,
    e2_send,
    e2_buf,
    xp_send,
    xp_buf,
    fo_send,
    fo_buf,
    gg_send,
    gg_buf,
    sel,
    sel_own,
    onehot,
    ext_rows,
    picked,
    d_picked,
    basis_buf,
    slope_buf,
    dist_buf,
    ddist_buf,
    offset_buf,
    msg,
    dmsg,
    drows,
    hidden,
    pre_buf,
    normed_buf,
    inv_buf,
    mix_t,
    update_t,
    readout_t,
    radial_t,
    wave_buf,
    wave_t,
    r_buf,
    cos_buf,
    sin_buf,
    send_sem,
    recv_sem,
    load_sem,
):
    bead = lax.axis_index("bead")
    dom = lax.axis_index("dom")
    z, x, core = bead // 8, (bead // 2) % 4, bead % 2
    y, low = dom // 2, dom % 2
    ring = 2 * y + core

    def dev(z_, x_, y_, low_, core_):
        return ((z_ * 4 + x_) * 2 + core_, y_ * 2 + low_)

    def ring_dev(z_, step):
        place = (ring + step) % 8
        return dev(z_, x, place // 2, low, place % 2)

    def swapped_ring_dev(step):
        place = (ring + step) % 8
        return dev(z, x, place // 2, place % 2, low)

    def copy(src, dst, send_at, recv_at, target):
        return pltpu.make_async_remote_copy(
            src_ref=src,
            dst_ref=dst,
            send_sem=send_sem.at[send_at],
            recv_sem=recv_sem.at[recv_at],
            device_id=target,
            device_id_type=MESH,
        )

    def arrive(dst, recv_at):
        copy(dst, dst, 0, recv_at, dev(z, x, y, low, 1 - core)).wait_recv()

    started = []

    def send_to(src, dst, send_at, recv_at, target):
        sent = copy(src, dst, send_at, recv_at, target)
        sent.start()
        started.append(sent)

    k_first = pl.multiple_of((bead - core + low) * KPART, KPART)
    loads = {}
    for number, (src, dst) in enumerate(
        (
            (pos_in, pos),
            (mom_in, mom),
            (force_in, force),
            (mass_in, mass),
            (charge_in, charge),
            (neigh_in, neigh),
            (send_in, send),
            (coef_in, coef),
            (radial_in, radial),
            (mix_in, mix),
            (update_in, update),
            (readout_in, readout),
            (ew_in, ew),
            (wave_in.at[:, pl.ds(k_first, KPART)], wave),
        )
    ):
        loads[number] = pltpu.make_async_copy(src, dst, load_sem.at[number])
        if number < 7:
            loads[number].start()

    same = low == core
    conditional = []

    def send_or_keep(src, dst, send_at, recv_at, target):
        sent = copy(src, dst, send_at, recv_at, target)

        @pl.when(same)
        def _():
            pltpu.make_async_copy(src, dst, recv_sem.at[recv_at]).start()

        @pl.when(jnp.logical_not(same))
        def _():
            sent.start()

        conditional.append(sent)

    barrier = pltpu.get_barrier_semaphore()

    def greet(target):
        pl.semaphore_signal(barrier, inc=1, device_id=target, device_id_type=MESH)

    far = dev((z + 3 + 2 * low) % 4, x, y, 1 - low, low)
    for dz in (2, 1, 3):
        greet(dev((z + dz) % 4, x, y, low, core))
    greet(ring_dev(z, 4))
    for dx, flip in ((2, 1), (2, 0), (1, 1), (3, 1), (1, 0), (3, 0)):
        greet(dev(z, (x + dx) % 4, y, core, (low + flip) % 2))

    @pl.when(jnp.logical_not(same))
    def _():
        greet(far)
        greet(dev(z, x, y, core, low))

    greet(ring_dev(z, 7 - 6 * core))
    greet(dev(z, x, y, core, 1 - low))
    greet(ring_dev(z, 1 + 6 * core))

    for number in range(7, 14):
        loads[number].start()

    for number in range(7):
        loads[number].wait()
    v_own[...] = jnp.zeros((8, ATOMS), F32)
    for c in range(3):
        v_own[c : c + 1, :] = pos[c]
        v_own[4 + c : 5 + c, :] = mom[c] + (0.5 * DT) * force[c]
    lane = lanes_of((1, 2 * SIDE))
    rows384 = jnp.concatenate(
        [send[0:1, :], send[1:2, :], send[2:3, :], jnp.zeros((1, 128), jnp.int32)], 1
    )
    shifted = pltpu.roll(rows384, 64, 1)
    spread = jnp.where(
        lane < GHOST,
        rows384,
        jnp.where(jnp.logical_and(lane >= SIDE, lane < SIDE + GHOST), shifted, -1),
    ).astype(F32)
    table = neigh[...]
    pack_own[0:8, :] = jnp.where(table >= ATOMS + GHOST, table + (SIDE - GHOST), table).astype(F32)
    pack_own[8:9, :] = mass[...]
    pack_own[9:10, :] = charge[...]
    pack_own[10:11, :] = spread
    pack_own[11:16, :] = jnp.zeros((5, ATOMS), F32)
    pl.semaphore_wait(barrier, 13 + 2 * jnp.where(same, 0, 1))

    slot = x * 2 + core
    for dx, dl in ((2, 1), (2, 0), (1, 1), (3, 1), (1, 0), (3, 0), (0, 1)):
        send_to(
            v_own,
            v_all.at[slot],
            S1 + 2 * dx + dl,
            S1 + slot,
            dev(z, (x + dx) % 4, y, (low + dl) % 2, low),
        )
    send_or_keep(v_own, v_all.at[slot], S1, S1 + slot, dev(z, x, y, low, low))
    swap = dev(z, x, y, core, low)
    send_or_keep(pack_own, pack_buf, PACK, PACK, far)
    send_or_keep(emb, emb_buf, EMB, EMB, far)

    for number in range(7, 14):
        loads[number].wait()

    eye = (rows_of((FEAT, FEAT)) == lanes_of((FEAT, FEAT))).astype(F32)
    eye_b = eye.astype(BF16)
    for layer in range(2):
        mix_t[layer] = dot_t(eye_b, mix[layer]).astype(BF16)
        update_t[layer] = dot_t(eye_b, update[layer]).astype(BF16)
        radial_t[layer] = dot_t(eye_b, radial[layer]).astype(BF16)
    readout_t[...] = dot_t(eye_b, readout[...]).astype(BF16)
    ew_col = jnp.sum(eye * ew[...], axis=1, keepdims=True)
    own_spread = jnp.broadcast_to(spread, (ATOMS, 2 * SIDE))
    atom_rows = rows_of((ATOMS, 2 * SIDE)).astype(F32)
    sel_own[...] = jnp.where(own_spread == atom_rows, 1.0, 0.0).astype(BF16)
    triple = wave[...].astype(F32)
    wave_buf[...] = jnp.zeros((16, KPART), F32)
    for part in range(3):
        wave_buf[4 * part : 4 * part + 3, :] = triple
    wave_t[...] = jnp.transpose(wave_buf[...]).astype(BF16)

    arrive(pack_buf, PACK)
    inv_mass = 1.0 / pack_buf[8:9, :]
    charges = pack_buf[9:10, :]
    send_row = pack_buf[10:11, :]
    sel[...] = jnp.where(jnp.broadcast_to(send_row, (ATOMS, 2 * SIDE)) == atom_rows, 1.0, 0.0).astype(BF16)
    send_index = jnp.broadcast_to(send_row, (8, 2 * SIDE)).astype(jnp.int32)

    for k in range(8):
        arrive(v_all.at[k], S1 + k)
    row8 = rows_of((8, ATOMS))
    upper = row8 < 4
    scale = jnp.where(upper, inv_mass, -pack_buf[8:9, :])
    beads_in = [v_all[k] for k in range(8)]
    total = beads_in[0]
    for k in range(1, 8):
        total = total + beads_in[k]
    centre_part = (total + DT * inv_mass * pltpu.roll(total, 4, 0)) * (1.0 / BEADS)
    centre_low = pltpu.roll(centre_part, 4, 0)
    first_row = rows_of((8, 1)) < 4
    for dz in (2, 1, 3, 0):
        z_to = (z + dz) % 4
        straight = None
        for k in range(8):
            shift = (8 * (z_to - z) + 2 * x + low - k + 64) % BEADS
            same_kind = coef[shift] * beads_in[k]
            other = jnp.where(first_row, coef[2 * BEADS + shift], coef[BEADS + shift]) * beads_in[k]
            straight = same_kind if straight is None else straight + same_kind
            crossed = other if k == 0 else crossed + other
        moved = straight + scale * pltpu.roll(crossed, 4, 0)
        ma = jnp.where(upper, moved, centre_low)
        if dz:
            ma_send[dz] = ma
            mb_send[dz] = moved[4:8]
            send_to(ma_send.at[dz], ma_buf.at[z], MA + dz, MA + z, ring_dev(z_to, 0))
        else:
            ma_buf[z] = ma
            mb_buf[z] = moved[4:8]

    def pack_side(ref, value):
        ref[0:FEAT, :] = value[:, 0:128].astype(BF16)
        rest = jnp.concatenate([value[128:FEAT, 128:SIDE], jnp.zeros((256 - FEAT, 128), F32)], 0)
        ref[FEAT:PACKED, :] = (value[0:128, 128:SIDE] + pltpu.roll(rest, 64, 1)).astype(BF16)

    def unpack_side(ref, packed, first):
        ref[:, first : first + 128] = packed[0:FEAT, :]
        rest = packed[FEAT:PACKED, :].astype(F32)
        ref[0:128, first + 128 : first + SIDE] = rest.astype(BF16)
        ref[128:FEAT, first + 128 : first + SIDE] = pltpu.roll(rest, 64, 1)[0 : FEAT - 128].astype(BF16)

    def send_sides(src, dst, first_sem):
        for near in range(2):
            side = core if near == 0 else 1 - core
            send_to(
                src.at[side], dst.at[1 - side], first_sem + side, first_sem + 1 - side, ring_dev(z, 7 - 6 * side)
            )

    def send_features(layer, rounded):
        ghosts = dot(rounded, sel[...])
        for side in range(2):
            pack_side(fg_send.at[layer, side], ghosts[:, SIDE * side : SIDE * (side + 1)])
        send_sides(fg_send.at[layer], fg_buf.at[layer], FG + 2 * layer)

    def receive_features(layer):
        for side in range(2):
            arrive(fg_buf.at[layer, side], FG + 2 * layer + side)
            unpack_side(ext_rows, fg_buf.at[layer, side], ATOMS + SIDE * side)

    arrive(emb_buf, EMB)
    rounded = emb_buf[...]
    hidden[...] = rounded.astype(F32)
    ext_rows[:, :ATOMS] = rounded
    send_features(0, rounded)
    for dz in range(1, 4):
        send_to(mb_send.at[dz], mb_buf.at[z], MB + dz, MB + z, ring_dev((z + dz) % 4, 0))

    group_rows = [(rows_of((16, ATOMS)) + 16 * g).astype(F32) for g in range(8)]

    def build(j, carry):
        index = pack_buf[pl.ds(j, 1), :]
        at = pl.multiple_of(j * ATOMS, ATOMS)
        for block in range(EXT // 128):
            local = jnp.broadcast_to(index - 128.0 * block, (16, ATOMS))
            for g in range(8):
                first = 128 * block + 16 * g
                onehot[first : first + 16, pl.ds(at, ATOMS)] = jnp.where(
                    local == group_rows[g], 1.0, 0.0
                ).astype(BF16)
        return carry

    lax.fori_loop(0, NEIGH, build, 0)

    def gather_part(layer, first, last, fresh):
        def body(j, carry):
            at = pl.multiple_of(j * ATOMS, ATOMS)
            part = dot(ext_rows[:, first:last], onehot[first:last, pl.ds(at, ATOMS)])
            if not fresh:
                part = part + picked[layer, j].astype(F32)
            picked[layer, j] = part.astype(BF16)
            return carry

        lax.fori_loop(0, NEIGH, body, 0, unroll=True)

    gather_part(0, 0, ATOMS, True)

    for dz in range(1, 4):
        arrive(ma_buf.at[(z + dz) % 4], MA + (z + dz) % 4)
    moved = (ma_buf[0] + ma_buf[1]) + (ma_buf[2] + ma_buf[3])
    centre = moved[4:7]
    xp_send[...] = moved
    for c in range(3):
        blocks = [
            jnp.broadcast_to(moved[c : c + 1, 128 * n : 128 * n + 128], (8, 128)) for n in range(4)
        ]
        for n in range(4):
            got = lane_pick(blocks, send_index[:, 128 * n : 128 * n + 128])
            gh_send[n // 2, c : c + 1, 128 * (n % 2) : 128 * (n % 2) + 128] = got[0:1]
    gh_send[:, 3:4, :] = jnp.zeros((2, 1, SIDE), F32)
    send_sides(gh_send, gh_buf, GH)
    receive_features(0)
    gather_part(0, ATOMS, EXT, False)
    turns = centre * 0.25
    high = turns.astype(BF16).astype(F32)
    rest = turns - high
    middle = rest.astype(BF16).astype(F32)
    r_buf[...] = jnp.zeros((16, ATOMS), F32)
    for number, value in enumerate((high, middle, rest - middle)):
        r_buf[4 * number : 4 * number + 3, :] = value

    def ewald_sums():
        phase = r_buf[...].astype(BF16)

        def body(i, carry):
            at = pl.multiple_of(i * 128, 128)
            turn = dot(wave_t[pl.ds(at, 128), :], phase)
            half = (turn - jnp.round(turn)) * math.pi
            q = half * half
            s = half * (
                1.0
                + q
                * (
                    -1.6666666641e-1
                    + q * (8.3333293858e-3 + q * (-1.9840083133e-4 + q * (2.7523971075e-6 - 2.3868346521e-8 * q)))
                )
            )
            c = 1.0 + q * (
                -0.5
                + q
                * (
                    4.1666666658e-2
                    + q
                    * (
                        -1.3888888388e-3
                        + q * (2.4801544910e-5 + q * (-2.7556993055e-7 + 2.0737354e-9 * q))
                    )
                )
            )
            sin_buf[pl.ds(at, 128), :] = (2.0 * s * c).astype(BF16)
            cos_buf[pl.ds(at, 128), :] = (1.0 - 2.0 * s * s).astype(BF16)
            return carry

        lax.fori_loop(0, KPART // 128, body, 0, unroll=True)
        weights = stacked_parts(jnp.broadcast_to(charges, (8, ATOMS)))
        for number, ref in enumerate((cos_buf, sin_buf)):
            sums = dot_t(weights, ref[...])
            sa_buf[core, number : number + 1, :] = sums[0:1] + sums[8:9]
        send_to(sa_buf.at[core], sa_buf.at[core], SA, SA, dev(z, x, y, low, 1 - core))

    def ewald_ring():
        arrive(sa_buf.at[1 - core], SA)
        sb_buf[y] = sa_buf[0] + sa_buf[1]
        for dy in range(1, 4):
            send_to(sb_buf.at[y], sb_buf.at[y], SB + dy, SB + y, dev(z, x, (y + dy) % 4, low, core))

    ghosts_at = []
    for side in range(2):
        arrive(gh_buf.at[side], GH + side)
        ghosts_at.append(gh_buf[side])
    index8 = pack_buf[0:8, :].astype(jnp.int32)
    distance = None
    for c in range(3):
        blocks = [moved[c : c + 1, 128 * n : 128 * n + 128] for n in range(4)]
        for side in range(2):
            blocks += [ghosts_at[side][c : c + 1, 128 * n : 128 * n + 128] for n in range(2)]
        blocks = [jnp.broadcast_to(block, (8, 128)) for block in blocks]
        others = jnp.concatenate(
            [lane_pick(blocks, index8[:, 128 * n : 128 * n + 128]) for n in range(4)], 1
        )
        offset = others - moved[c : c + 1, :]
        offset_buf[c] = offset
        distance = offset * offset if c == 0 else distance + offset * offset
    dist_buf[...] = distance
    m_row = rows_of((BASIS, ATOMS))
    rates = jnp.where(m_row % 2 == 1, 0.125 * math.sqrt(2.0), 0.125) * jnp.left_shift(1, m_row // 2).astype(F32)
    for j in range(NEIGH):
        exact = 1.0 / (1.0 + rates * dist_buf[j : j + 1, :])
        basis_buf[j] = exact.astype(BF16)
        slope_buf[j] = -rates * exact * exact

    def ewald_forces():
        for dy in range(1, 4):
            arrive(sb_buf.at[(y + dy) % 4], SB + (y + dy) % 4)
        sums = (sb_buf[0] + sb_buf[1]) + (sb_buf[2] + sb_buf[3])
        recip = wave_buf[0:8, :] * (TWO_PI / 4.0)
        recip = jnp.where(row8 < 3, recip, 0.0)
        square = jnp.sum(recip * recip, axis=0, keepdims=True)
        damping = 48.0 / math.sqrt(KVEC * TOTAL_ATOMS) * jnp.exp(-0.002 * square) / square
        from_sin = stacked_parts(recip * (damping * sums[0:1]))
        from_cos = stacked_parts(recip * (damping * sums[1:2]))
        part = dot(from_sin, sin_buf[...]) - dot(from_cos, cos_buf[...])
        part = 2.0 * charges * (part[0:8] + part[8:16])
        e1_buf[x] = part[0:4]
        for dx in (2, 1, 3):
            send_to(e1_buf.at[x], e1_buf.at[x], E1 + dx, E1 + x, dev(z, (x + dx) % 4, y, low, core))

    def ewald_group_sum():
        for dx in (1, 3, 2):
            arrive(e1_buf.at[(x + dx) % 4], E1 + (x + dx) % 4)
        e2_send[...] = (e1_buf[0] + e1_buf[1]) + (e1_buf[2] + e1_buf[3])
        place = 2 * z + low
        for dz in (2, 1, 3, 0):
            for flip in (1, 0):
                if dz or flip:
                    send_to(
                        e2_send,
                        e2_buf.at[place],
                        E2 + 2 * dz + flip,
                        E2 + place,
                        dev((z + dz) % 4, x, y, core, (low + flip) % 2),
                    )
        send_or_keep(e2_send, e2_buf.at[place], E2, E2 + place, swap)

    def finish_layer(layer):
        msg[...] = jnp.zeros((FEAT, ATOMS), F32)

        def body(j, carry):
            edge = dot(radial_t[layer], basis_buf[j])
            msg[...] += edge * picked[layer, j].astype(F32)
            return carry

        lax.fori_loop(0, NEIGH, body, 0, unroll=True)
        message = msg[...]
        inverse = lax.rsqrt(jnp.sum(message * message, axis=0, keepdims=True) * (1.0 / FEAT) + 1e-6)
        normed = message * inverse
        normed_buf[layer] = normed
        inv_buf[layer] = jnp.broadcast_to(inverse, (8, ATOMS))
        pre = dot(mix_t[layer], normed.astype(BF16))
        pre_buf[layer] = pre
        gated = (pre * lax.logistic(pre)).astype(BF16)
        hidden[...] += dot(update_t[layer], gated)

    finish_layer(0)
    rounded = hidden[...].astype(BF16)
    ext_rows[:, :ATOMS] = rounded
    send_features(1, rounded)
    ewald_sums()
    gather_part(1, 0, ATOMS, True)
    ewald_ring()
    for dz in range(1, 4):
        arrive(mb_buf.at[(z + dz) % 4], MB + (z + dz) % 4)
    xp_send[4:8, :] = (mb_buf[0] + mb_buf[1]) + (mb_buf[2] + mb_buf[3])
    send_or_keep(xp_send, xp_buf, XP, XP, swap)
    receive_features(1)
    gather_part(1, ATOMS, EXT, False)
    finish_layer(1)

    def silu_slope(pre):
        sig = lax.logistic(pre)
        return sig * (1.0 + pre * (1.0 - sig))

    final = dot(readout_t[...], hidden[...].astype(BF16))
    dfinal = ew_col * silu_slope(final)
    cotan = dot(readout[...], dfinal.astype(BF16)).astype(BF16)

    def message_cotan(layer, cotan_b):
        dgated = dot(update[layer], cotan_b).astype(BF16).astype(F32)
        dpre = dgated * silu_slope(pre_buf[layer])
        dnormed = dot(mix[layer], dpre.astype(BF16)).astype(BF16).astype(F32)
        normed = normed_buf[layer]
        mean = jnp.sum(dnormed * normed, axis=0, keepdims=True) * (1.0 / FEAT)
        dmsg[...] = inv_buf[layer, 0:1, :] * (dnormed - normed * mean)

    def distance_cotan(layer):
        def body(j, carry):
            dedge = (picked[layer, j].astype(F32) * dmsg[...]).astype(BF16)
            dbasis = dot(radial[layer], dedge).astype(BF16).astype(F32)
            part = jnp.sum(dbasis * slope_buf[j], axis=0, keepdims=True)
            if layer == 1:
                ddist_buf[pl.ds(j, 1), :] = part
            else:
                ddist_buf[pl.ds(j, 1), :] += part
            return carry

        lax.fori_loop(0, NEIGH, body, 0, unroll=True)

    message_cotan(1, cotan)

    def row_cotan(j, carry):
        at = pl.multiple_of(j * ATOMS, ATOMS)
        edge = dot(radial_t[1], basis_buf[j])
        d_picked[:, pl.ds(at, ATOMS)] = (edge * dmsg[...]).astype(BF16)
        return carry

    lax.fori_loop(0, NEIGH, row_cotan, 0, unroll=True)
    for near in range(2):
        side = core if near == 0 else 1 - core
        first = pl.multiple_of(ATOMS + SIDE * side, SIDE)
        pack_side(dg_send.at[side], dot_t(d_picked[...], onehot[pl.ds(first, SIDE), :]))
        send_to(dg_send.at[side], dg_buf.at[1 - side], DG + side, DG + 1 - side, ring_dev(z, 7 - 6 * side))
    ewald_forces()
    for half in range(2):
        drows[:, SIDE * half : SIDE * half + SIDE] = dot_t(
            d_picked[...], onehot[SIDE * half : SIDE * half + SIDE, :]
        )
    distance_cotan(1)
    for near in (1, 0):
        side = core if near == 0 else 1 - core
        arrive(dg_buf.at[side], DG + side)
    for side in range(2):
        unpack_side(dg_rows, dg_buf.at[side], SIDE * side)
    returned = dot_t(dg_rows[...], sel[...])
    owned = (drows[...] + returned).astype(BF16).astype(F32)
    message_cotan(0, (cotan.astype(F32) + owned).astype(BF16))
    distance_cotan(0)
    ewald_group_sum()

    ddist = 2.0 * ddist_buf[...]
    edge_force = [offset_buf[c] * ddist for c in range(3)]
    for c in range(3):
        own = jnp.sum(edge_force[c], axis=0, keepdims=True)
        fo_send[c : c + 1, :] = own
    fo_send[3:4, :] = jnp.zeros((1, ATOMS), F32)

    parts = []
    zero_row = jnp.zeros((1, ATOMS), F32)
    for j in range(NEIGH):
        rows = [edge_force[c][j : j + 1, :] for c in range(3)] + [zero_row] * 5
        parts.append(stacked_parts(jnp.concatenate(rows, 0)))
    force_rows = jnp.concatenate(parts, 1)
    for near in range(2):
        side = core if near == 0 else 1 - core
        first = pl.multiple_of(ATOMS + SIDE * side, SIDE)
        both = dot_t(force_rows, onehot[pl.ds(first, SIDE), :])
        gg_send[side] = both[0:4] + both[8:12]
        send_to(
            gg_send.at[side], gg_buf.at[1 - side], GG + side, GG + 1 - side, swapped_ring_dev(7 - 6 * side)
        )
    both = dot_t(force_rows, onehot[:ATOMS, :])
    fo_send[...] = fo_send[...] - (both[0:4] + both[8:12])
    send_or_keep(fo_send, fo_buf, FO, FO, swap)

    arrive(xp_buf, XP)
    for side in range(2):
        arrive(gg_buf.at[side], GG + side)
    zero4 = jnp.zeros((4, SIDE), F32)
    returned = None
    for side in range(2):
        rows = stacked_parts(jnp.concatenate([gg_buf[side], zero4], 0))
        both = dot_t(rows, sel_own[:, SIDE * side : SIDE * side + SIDE])
        both = both[0:4] + both[8:12]
        returned = both if side == 0 else returned + both
    arrive(fo_buf, FO)
    for place in range(8):
        arrive(e2_buf.at[place], E2 + place)
    long_range = e2_buf[0]
    for place in range(1, 8):
        long_range = long_range + e2_buf[place]
    result = (fo_buf[...] - returned) + long_range
    for c in range(3):
        out[c] = xp_buf[c : c + 1, :]
        out[3 + c] = xp_buf[4 + c : 5 + c, :] + (0.5 * DT) * result[c : c + 1, :]
        out[6 + c] = result[c : c + 1, :]

    for sent in started:
        sent.wait_send()

    @pl.when(jnp.logical_not(same))
    def _():
        for sent in conditional:
            sent.wait_send()


def local(
    positions,
    momenta,
    forces,
    masses,
    charges,
    embedding,
    neighbours,
    send_rows,
    wavevectors,
    radial_weight,
    mix_weight,
    update_weight,
    readout_weight,
    energy_weight,
):
    piece = (3, 1, ATOMS)
    scratch = [
        (piece, F32),
        (piece, F32),
        (piece, F32),
        ((1, ATOMS), F32),
        ((1, ATOMS), F32),
        ((NEIGH, ATOMS), jnp.int32),
        ((3, 128), jnp.int32),
        ((3, KPART), jnp.int32),
        ((2, BASIS, FEAT), BF16),
        ((2, FEAT, FEAT), BF16),
        ((2, FEAT, FEAT), BF16),
        ((FEAT, FEAT), BF16),
        ((1, FEAT), F32),
        ((8, ATOMS), F32),
        ((8, 8, ATOMS), F32),
        ((FEAT, ATOMS), BF16),
        ((16, ATOMS), F32),
        ((16, ATOMS), F32),
        ((4, 8, ATOMS), F32),
        ((4, 8, ATOMS), F32),
        ((4, 4, ATOMS), F32),
        ((4, 4, ATOMS), F32),
        ((2, 4, SIDE), F32),
        ((2, 4, SIDE), F32),
        ((2, 2, PACKED, 128), BF16),
        ((2, 2, PACKED, 128), BF16),
        ((2, PACKED, 128), BF16),
        ((2, PACKED, 128), BF16),
        ((FEAT, 2 * SIDE), BF16),
        ((2, 2, KPART), F32),
        ((4, 2, KPART), F32),
        ((4, 4, ATOMS), F32),
        ((4, ATOMS), F32),
        ((8, 4, ATOMS), F32),
        ((8, ATOMS), F32),
        ((8, ATOMS), F32),
        ((4, ATOMS), F32),
        ((4, ATOMS), F32),
        ((2, 4, SIDE), F32),
        ((2, 4, SIDE), F32),
        ((ATOMS, 2 * SIDE), BF16),
        ((ATOMS, 2 * SIDE), BF16),
        ((EXT, NEIGH * ATOMS), BF16),
        ((FEAT, EXT), BF16),
        ((2, NEIGH, FEAT, ATOMS), BF16),
        ((FEAT, NEIGH * ATOMS), BF16),
        ((NEIGH, BASIS, ATOMS), BF16),
        ((NEIGH, BASIS, ATOMS), F32),
        ((NEIGH, ATOMS), F32),
        ((NEIGH, ATOMS), F32),
        ((3, NEIGH, ATOMS), F32),
        ((FEAT, ATOMS), F32),
        ((FEAT, ATOMS), F32),
        ((FEAT, ATOMS), F32),
        ((FEAT, ATOMS), F32),
        ((2, FEAT, ATOMS), F32),
        ((2, FEAT, ATOMS), F32),
        ((2, 8, ATOMS), F32),
        ((2, FEAT, FEAT), BF16),
        ((2, FEAT, FEAT), BF16),
        ((FEAT, FEAT), BF16),
        ((2, FEAT, BASIS), BF16),
        ((16, KPART), F32),
        ((KPART, 16), BF16),
        ((16, ATOMS), F32),
        ((KPART, ATOMS), BF16),
        ((KPART, ATOMS), BF16),
    ]
    out = pl.pallas_call(
        step_kernel,
        out_shape=jax.ShapeDtypeStruct((9, 1, ATOMS), F32),
        in_specs=[pl.BlockSpec(memory_space=pltpu.HBM)] * 15,
        out_specs=pl.BlockSpec(memory_space=pltpu.VMEM),
        scratch_shapes=[pltpu.SMEM((3 * BEADS,), F32)]
        + [pltpu.VMEM(shape, kind) for shape, kind in scratch]
        + [
            pltpu.SemaphoreType.DMA((N_SEMS,)),
            pltpu.SemaphoreType.DMA((N_SEMS,)),
            pltpu.SemaphoreType.DMA((14,)),
        ],
        compiler_params=pltpu.CompilerParams(
            collective_id=0, has_side_effects=True, vmem_limit_bytes=60 * 1024 * 1024
        ),
        cost_estimate=pl.CostEstimate(flops=16_000_000_000, bytes_accessed=2_000_000, transcendentals=1_000_000),
    )(
        jnp.asarray(ring_tables()),
        positions,
        momenta,
        forces,
        masses.reshape(1, ATOMS),
        charges.reshape(1, ATOMS),
        embedding.T,
        neighbours,
        send_rows.reshape(3, 128),
        wavevectors,
        radial_weight,
        mix_weight,
        update_weight,
        readout_weight,
        energy_weight.reshape(1, FEAT),
    )
    return out[0:3], out[3:6], out[6:9]


def solution(mesh):
    own = P(None, "bead", "dom")
    placed = (
        own,
        own,
        own,
        P("dom"),
        P("dom"),
        P("dom", None),
        P(None, "dom"),
        P("dom"),
        P(),
        P(),
        P(),
        P(),
        P(),
        P(),
    )
    return jax.shard_map(local, mesh=mesh, in_specs=placed, out_specs=(own, own, own), check_vma=False)
```

```python
import math

import jax
import jax.numpy as jnp
import numpy as np
from jax import lax
from jax.experimental import pallas as pl
from jax.experimental.pallas import tpu as pltpu
from jax.sharding import PartitionSpec as P

MESH = pl.DeviceIdType.MESH
F32 = jnp.float32
BF16 = jnp.bfloat16

BEADS = 32
ATOMS = 512
TOTAL_ATOMS = 4096
GHOST = 192
SIDE = 256
EXT = ATOMS + 2 * SIDE
NEIGH = 8
FEAT = 240
BASIS = 16
KVEC = 16384
KPART = KVEC // BEADS
DT = 0.25
TWO_PI = 2.0 * math.pi
PACKED = FEAT + 128

S1, EMB, PACK, MA, MB, GH, FG, DG, SA, SB, E1, E2, XP, FO, GG, N_SEMS = np.cumsum(
    [0, 8, 1, 1, 8, 8, 2, 4, 2, 1, 4, 4, 8, 1, 1, 2]
).tolist()


def ring_tables():
    k = np.arange(BEADS)
    b = np.arange(BEADS)[:, None]
    angle = 2.0 * np.pi / BEADS * (b * k % BEADS)
    half = BEADS // 2
    basis = np.where(k < half, np.cos(angle), np.sin(angle)) * math.sqrt(2.0 / BEADS)
    basis = np.where(k == 0, math.sqrt(1.0 / BEADS), basis)
    basis = np.where(k == half, math.sqrt(1.0 / BEADS) * (1 - 2 * (b % 2)), basis)
    omega = 3.2 * np.sin(np.pi * k / BEADS)
    cosine, sine = np.cos(omega * DT), np.sin(omega * DT)
    drift = np.where(k == 0, DT, sine / np.where(k == 0, 1.0, omega))
    rows = [(basis * value) @ basis.T for value in (cosine, drift, omega * sine)]
    return np.concatenate([row[0] for row in rows]).astype(np.float32)


def dot(a, b):
    return lax.dot_general(a, b, (((1,), (0,)), ((), ())), preferred_element_type=F32)


def dot_t(a, b):
    return lax.dot_general(a, b, (((1,), (1,)), ((), ())), preferred_element_type=F32)


def rows_of(shape):
    return lax.broadcasted_iota(jnp.int32, shape, 0)


def lanes_of(shape):
    return lax.broadcasted_iota(jnp.int32, shape, 1)


def two_parts(value):
    high = value.astype(BF16)
    return high, (value - high.astype(F32)).astype(BF16)


def stacked_parts(value):
    high = value.astype(BF16).astype(F32)
    return jnp.concatenate([high, value - high], 0).astype(BF16)


def lane_pick(tables, index):
    result = None
    for number, block in enumerate(tables):
        local = index - 128 * number
        inside = jnp.logical_and(local >= 0, local < 128)
        got = jnp.take_along_axis(block, jnp.where(inside, local, 0), axis=1, mode="promise_in_bounds")
        result = jnp.where(inside, got, 0.0 if result is None else result)
    return result


def step_kernel(
    coef_in,
    pos_in,
    mom_in,
    force_in,
    mass_in,
    charge_in,
    emb,
    neigh_in,
    send_in,
    wave_in,
    radial_in,
    mix_in,
    update_in,
    readout_in,
    ew_in,
    out,
    coef,
    pos,
    mom,
    force,
    mass,
    charge,
    neigh,
    send,
    wave,
    radial,
    mix,
    update,
    readout,
    ew,
    v_own,
    v_all,
    emb_buf,
    pack_own,
    pack_buf,
    ma_send,
    ma_buf,
    mb_send,
    mb_buf,
    gh_send,
    gh_buf,
    fg_send,
    fg_buf,
    dg_send,
    dg_buf,
    dg_rows,
    sa_buf,
    sb_buf,
    e1_buf,
    e2_send,
    e2_buf,
    xp_send,
    xp_buf,
    fo_send,
    fo_buf,
    gg_send,
    gg_buf,
    sel,
    sel_own,
    onehot,
    ext_rows,
    picked,
    d_picked,
    basis_buf,
    slope_buf,
    dist_buf,
    ddist_buf,
    offset_buf,
    msg,
    dmsg,
    drows,
    hidden,
    pre_buf,
    normed_buf,
    inv_buf,
    mix_t,
    update_t,
    readout_t,
    radial_t,
    wave_buf,
    wave_t,
    r_buf,
    cos_buf,
    sin_buf,
    send_sem,
    recv_sem,
    load_sem,
):
    bead = lax.axis_index("bead")
    dom = lax.axis_index("dom")
    z, x, core = bead // 8, (bead // 2) % 4, bead % 2
    y, low = dom // 2, dom % 2
    ring = 2 * y + core

    def dev(z_, x_, y_, low_, core_):
        return ((z_ * 4 + x_) * 2 + core_, y_ * 2 + low_)

    def ring_dev(z_, step):
        place = (ring + step) % 8
        return dev(z_, x, place // 2, low, place % 2)

    def swapped_ring_dev(step):
        place = (ring + step) % 8
        return dev(z, x, place // 2, place % 2, low)

    def copy(src, dst, send_at, recv_at, target):
        return pltpu.make_async_remote_copy(
            src_ref=src,
            dst_ref=dst,
            send_sem=send_sem.at[send_at],
            recv_sem=recv_sem.at[recv_at],
            device_id=target,
            device_id_type=MESH,
        )

    def arrive(dst, recv_at):
        copy(dst, dst, 0, recv_at, dev(z, x, y, low, 1 - core)).wait_recv()

    started = []

    def send_to(src, dst, send_at, recv_at, target):
        sent = copy(src, dst, send_at, recv_at, target)
        sent.start()
        started.append(sent)

    k_first = pl.multiple_of((bead - core + low) * KPART, KPART)
    loads = {}
    for number, (src, dst) in enumerate(
        (
            (pos_in, pos),
            (mom_in, mom),
            (force_in, force),
            (mass_in, mass),
            (charge_in, charge),
            (neigh_in, neigh),
            (send_in, send),
            (coef_in, coef),
            (radial_in, radial),
            (mix_in, mix),
            (update_in, update),
            (readout_in, readout),
            (ew_in, ew),
            (wave_in.at[:, pl.ds(k_first, KPART)], wave),
        )
    ):
        loads[number] = pltpu.make_async_copy(src, dst, load_sem.at[number])
        if number < 7:
            loads[number].start()

    same = low == core
    conditional = []

    def send_or_keep(src, dst, send_at, recv_at, target):
        sent = copy(src, dst, send_at, recv_at, target)

        @pl.when(same)
        def _():
            pltpu.make_async_copy(src, dst, recv_sem.at[recv_at]).start()

        @pl.when(jnp.logical_not(same))
        def _():
            sent.start()

        conditional.append(sent)

    barrier = pltpu.get_barrier_semaphore()

    def greet(target):
        pl.semaphore_signal(barrier, inc=1, device_id=target, device_id_type=MESH)

    far = dev((z + 3 + 2 * low) % 4, x, y, 1 - low, low)
    for dz in (2, 1, 3):
        greet(dev((z + dz) % 4, x, y, core, core))
    greet(ring_dev(z, 4))

    @pl.when(same)
    def _():
        for dx, flip in ((2, 1), (2, 0), (1, 1), (3, 1), (1, 0), (3, 0), (0, 1)):
            greet(dev(z, (x + dx) % 4, y, core, (low + flip) % 2))

    @pl.when(jnp.logical_not(same))
    def _():
        greet(far)
        greet(dev(z, x, y, core, core))

    greet(ring_dev(z, 7 - 6 * core))
    greet(ring_dev(z, 1 + 6 * core))

    for number in range(7, 14):
        loads[number].start()

    for number in range(7):
        loads[number].wait()
    v_own[...] = jnp.zeros((8, ATOMS), F32)
    for c in range(3):
        v_own[c : c + 1, :] = pos[c]
        v_own[4 + c : 5 + c, :] = mom[c] + (0.5 * DT) * force[c]
    lane = lanes_of((1, 2 * SIDE))
    rows384 = jnp.concatenate(
        [send[0:1, :], send[1:2, :], send[2:3, :], jnp.zeros((1, 128), jnp.int32)], 1
    )
    shifted = pltpu.roll(rows384, 64, 1)
    spread = jnp.where(
        lane < GHOST,
        rows384,
        jnp.where(jnp.logical_and(lane >= SIDE, lane < SIDE + GHOST), shifted, -1),
    ).astype(F32)
    table = neigh[...]
    pack_own[0:8, :] = jnp.where(table >= ATOMS + GHOST, table + (SIDE - GHOST), table).astype(F32)
    pack_own[8:9, :] = mass[...]
    pack_own[9:10, :] = charge[...]
    pack_own[10:11, :] = spread
    pack_own[11:16, :] = jnp.zeros((5, ATOMS), F32)
    pl.semaphore_wait(barrier, jnp.where(same, 13, 8))

    slot = x * 2 + core
    for dx in (2, 1, 3):
        send_to(v_own, v_all.at[slot], S1 + dx, S1 + slot, dev(z, (x + dx) % 4, y, low, low))
    send_or_keep(v_own, v_all.at[slot], S1, S1 + slot, dev(z, x, y, low, low))
    swap = dev(z, x, y, core, low)
    send_or_keep(pack_own, pack_buf, PACK, PACK, far)
    send_or_keep(emb, emb_buf, EMB, EMB, far)

    for number in range(7, 14):
        loads[number].wait()

    eye = (rows_of((FEAT, FEAT)) == lanes_of((FEAT, FEAT))).astype(F32)
    eye_b = eye.astype(BF16)
    for layer in range(2):
        mix_t[layer] = dot_t(eye_b, mix[layer]).astype(BF16)
        update_t[layer] = dot_t(eye_b, update[layer]).astype(BF16)
        radial_t[layer] = dot_t(eye_b, radial[layer]).astype(BF16)
    readout_t[...] = dot_t(eye_b, readout[...]).astype(BF16)
    ew_col = jnp.sum(eye * ew[...], axis=1, keepdims=True)
    own_spread = jnp.broadcast_to(spread, (ATOMS, 2 * SIDE))
    atom_rows = rows_of((ATOMS, 2 * SIDE)).astype(F32)
    sel_own[...] = jnp.where(own_spread == atom_rows, 1.0, 0.0).astype(BF16)
    triple = wave[...].astype(F32)
    wave_buf[...] = jnp.zeros((16, KPART), F32)
    for part in range(3):
        wave_buf[4 * part : 4 * part + 3, :] = triple
    wave_t[...] = jnp.transpose(wave_buf[...]).astype(BF16)

    arrive(pack_buf, PACK)
    charges = pack_buf[9:10, :]
    send_row = pack_buf[10:11, :]
    sel[...] = jnp.where(jnp.broadcast_to(send_row, (ATOMS, 2 * SIDE)) == atom_rows, 1.0, 0.0).astype(BF16)
    send_index = jnp.broadcast_to(send_row, (8, 2 * SIDE)).astype(jnp.int32)

    row8 = rows_of((8, ATOMS))
    targets = [(2, 0), (2, 1), (1, 0), (3, 0), (1, 1), (3, 1), (0, 1), (0, 0)]

    def sums_copy(number, src, dst, first_sem):
        target = dev((z + number // 2) % 4, x, y, (low + number % 2) % 2, core)
        return copy(src.at[number], dst.at[z], first_sem + number, first_sem + z, target)

    @pl.when(same)
    def _():
        for k in range(8):
            arrive(v_all.at[k], S1 + k)
        upper = row8 < 4
        inv_mass = 1.0 / mass[...]
        scale = jnp.where(upper, inv_mass, -mass[...])
        beads_in = [v_all[k] for k in range(8)]
        total = beads_in[0]
        for k in range(1, 8):
            total = total + beads_in[k]
        centre_part = (total + DT * inv_mass * pltpu.roll(total, 4, 0)) * (1.0 / BEADS)
        centre_low = pltpu.roll(centre_part, 4, 0)
        first_row = rows_of((8, 1)) < 4
        for dz, flip in targets:
            z_to, low_to, number = (z + dz) % 4, (low + flip) % 2, 2 * dz + flip
            straight = None
            for k in range(8):
                shift = (8 * (z_to - z) + 2 * x + low_to - k + 64) % BEADS
                same_kind = coef[shift] * beads_in[k]
                other = jnp.where(first_row, coef[2 * BEADS + shift], coef[BEADS + shift]) * beads_in[k]
                straight = same_kind if k == 0 else straight + same_kind
                crossed = other if k == 0 else crossed + other
            moved = straight + scale * pltpu.roll(crossed, 4, 0)
            ma = jnp.where(upper, moved, centre_low)
            if number:
                ma_send[number] = ma
                mb_send[number] = moved[4:8]
                sums_copy(number, ma_send, ma_buf, MA).start()
            else:
                ma_buf[z] = ma
                mb_buf[z] = moved[4:8]

    def arrive_sums(buf, first_sem):
        @pl.when(jnp.logical_not(same))
        def _():
            arrive(buf.at[z], first_sem + z)

        for dz in (1, 3, 2):
            arrive(buf.at[(z + dz) % 4], first_sem + (z + dz) % 4)

    def pack_side(ref, value):
        ref[0:FEAT, :] = value[:, 0:128].astype(BF16)
        rest = jnp.concatenate([value[128:FEAT, 128:SIDE], jnp.zeros((256 - FEAT, 128), F32)], 0)
        ref[FEAT:PACKED, :] = (value[0:128, 128:SIDE] + pltpu.roll(rest, 64, 1)).astype(BF16)

    def unpack_side(ref, packed, first):
        ref[:, first : first + 128] = packed[0:FEAT, :]
        rest = packed[FEAT:PACKED, :].astype(F32)
        ref[0:128, first + 128 : first + SIDE] = rest.astype(BF16)
        ref[128:FEAT, first + 128 : first + SIDE] = pltpu.roll(rest, 64, 1)[0 : FEAT - 128].astype(BF16)

    def send_sides(src, dst, first_sem):
        for near in range(2):
            side = core if near == 0 else 1 - core
            send_to(
                src.at[side], dst.at[1 - side], first_sem + side, first_sem + 1 - side, ring_dev(z, 7 - 6 * side)
            )

    def send_features(layer, rounded):
        ghosts = dot(rounded, sel[...])
        for side in range(2):
            pack_side(fg_send.at[layer, side], ghosts[:, SIDE * side : SIDE * (side + 1)])
        send_sides(fg_send.at[layer], fg_buf.at[layer], FG + 2 * layer)

    def receive_features(layer):
        for side in range(2):
            arrive(fg_buf.at[layer, side], FG + 2 * layer + side)
            unpack_side(ext_rows, fg_buf.at[layer, side], ATOMS + SIDE * side)

    arrive(emb_buf, EMB)
    rounded = emb_buf[...]
    hidden[...] = rounded.astype(F32)
    ext_rows[:, :ATOMS] = rounded
    send_features(0, rounded)

    @pl.when(same)
    def _():
        for dz, flip in targets[:7]:
            sums_copy(2 * dz + flip, mb_send, mb_buf, MB).start()

    group_rows = [(rows_of((16, ATOMS)) + 16 * g).astype(F32) for g in range(8)]

    def build(j, carry):
        index = pack_buf[pl.ds(j, 1), :]
        at = pl.multiple_of(j * ATOMS, ATOMS)
        for block in range(EXT // 128):
            local = jnp.broadcast_to(index - 128.0 * block, (16, ATOMS))
            for g in range(8):
                first = 128 * block + 16 * g
                onehot[first : first + 16, pl.ds(at, ATOMS)] = jnp.where(
                    local == group_rows[g], 1.0, 0.0
                ).astype(BF16)
        return carry

    lax.fori_loop(0, NEIGH, build, 0)

    def gather_part(layer, first, last, fresh):
        def body(j, carry):
            at = pl.multiple_of(j * ATOMS, ATOMS)
            part = dot(ext_rows[:, first:last], onehot[first:last, pl.ds(at, ATOMS)])
            if not fresh:
                part = part + picked[layer, j].astype(F32)
            picked[layer, j] = part.astype(BF16)
            return carry

        lax.fori_loop(0, NEIGH, body, 0, unroll=True)

    gather_part(0, 0, ATOMS, True)

    arrive_sums(ma_buf, MA)
    moved = (ma_buf[0] + ma_buf[1]) + (ma_buf[2] + ma_buf[3])
    centre = moved[4:7]
    xp_send[...] = moved
    for c in range(3):
        blocks = [
            jnp.broadcast_to(moved[c : c + 1, 128 * n : 128 * n + 128], (8, 128)) for n in range(4)
        ]
        for n in range(4):
            got = lane_pick(blocks, send_index[:, 128 * n : 128 * n + 128])
            gh_send[n // 2, c : c + 1, 128 * (n % 2) : 128 * (n % 2) + 128] = got[0:1]
    gh_send[:, 3:4, :] = jnp.zeros((2, 1, SIDE), F32)
    send_sides(gh_send, gh_buf, GH)
    receive_features(0)
    gather_part(0, ATOMS, EXT, False)
    turns = centre * 0.25
    high = turns.astype(BF16).astype(F32)
    rest = turns - high
    middle = rest.astype(BF16).astype(F32)
    r_buf[...] = jnp.zeros((16, ATOMS), F32)
    for number, value in enumerate((high, middle, rest - middle)):
        r_buf[4 * number : 4 * number + 3, :] = value

    def ewald_sums():
        phase = r_buf[...].astype(BF16)

        def body(i, carry):
            at = pl.multiple_of(i * 128, 128)
            turn = dot(wave_t[pl.ds(at, 128), :], phase)
            half = (turn - jnp.round(turn)) * math.pi
            q = half * half
            s = half * (
                1.0
                + q
                * (
                    -1.6666666641e-1
                    + q * (8.3333293858e-3 + q * (-1.9840083133e-4 + q * (2.7523971075e-6 - 2.3868346521e-8 * q)))
                )
            )
            c = 1.0 + q * (
                -0.5
                + q
                * (
                    4.1666666658e-2
                    + q
                    * (
                        -1.3888888388e-3
                        + q * (2.4801544910e-5 + q * (-2.7556993055e-7 + 2.0737354e-9 * q))
                    )
                )
            )
            sin_buf[pl.ds(at, 128), :] = (2.0 * s * c).astype(BF16)
            cos_buf[pl.ds(at, 128), :] = (1.0 - 2.0 * s * s).astype(BF16)
            return carry

        lax.fori_loop(0, KPART // 128, body, 0, unroll=True)
        weights = stacked_parts(jnp.broadcast_to(charges, (8, ATOMS)))
        for number, ref in enumerate((cos_buf, sin_buf)):
            sums = dot_t(weights, ref[...])
            sa_buf[core, number : number + 1, :] = sums[0:1] + sums[8:9]
        send_to(sa_buf.at[core], sa_buf.at[core], SA, SA, dev(z, x, y, low, 1 - core))

    def ewald_ring():
        arrive(sa_buf.at[1 - core], SA)
        sb_buf[y] = sa_buf[0] + sa_buf[1]
        for dy in range(1, 4):
            send_to(sb_buf.at[y], sb_buf.at[y], SB + dy, SB + y, dev(z, x, (y + dy) % 4, low, core))

    ghosts_at = []
    for side in range(2):
        arrive(gh_buf.at[side], GH + side)
        ghosts_at.append(gh_buf[side])
    index8 = pack_buf[0:8, :].astype(jnp.int32)
    distance = None
    for c in range(3):
        blocks = [moved[c : c + 1, 128 * n : 128 * n + 128] for n in range(4)]
        for side in range(2):
            blocks += [ghosts_at[side][c : c + 1, 128 * n : 128 * n + 128] for n in range(2)]
        blocks = [jnp.broadcast_to(block, (8, 128)) for block in blocks]
        others = jnp.concatenate(
            [lane_pick(blocks, index8[:, 128 * n : 128 * n + 128]) for n in range(4)], 1
        )
        offset = others - moved[c : c + 1, :]
        offset_buf[c] = offset
        distance = offset * offset if c == 0 else distance + offset * offset
    dist_buf[...] = distance
    m_row = rows_of((BASIS, ATOMS))
    rates = jnp.where(m_row % 2 == 1, 0.125 * math.sqrt(2.0), 0.125) * jnp.left_shift(1, m_row // 2).astype(F32)
    for j in range(NEIGH):
        exact = 1.0 / (1.0 + rates * dist_buf[j : j + 1, :])
        basis_buf[j] = exact.astype(BF16)
        slope_buf[j] = -rates * exact * exact

    def ewald_forces():
        for dy in range(1, 4):
            arrive(sb_buf.at[(y + dy) % 4], SB + (y + dy) % 4)
        sums = (sb_buf[0] + sb_buf[1]) + (sb_buf[2] + sb_buf[3])
        recip = wave_buf[0:8, :] * (TWO_PI / 4.0)
        recip = jnp.where(row8 < 3, recip, 0.0)
        square = jnp.sum(recip * recip, axis=0, keepdims=True)
        damping = 48.0 / math.sqrt(KVEC * TOTAL_ATOMS) * jnp.exp(-0.002 * square) / square
        from_sin = stacked_parts(recip * (damping * sums[0:1]))
        from_cos = stacked_parts(recip * (damping * sums[1:2]))
        part = dot(from_sin, sin_buf[...]) - dot(from_cos, cos_buf[...])
        part = 2.0 * charges * (part[0:8] + part[8:16])
        e1_buf[x] = part[0:4]
        for dx in (2, 1, 3):
            send_to(e1_buf.at[x], e1_buf.at[x], E1 + dx, E1 + x, dev(z, (x + dx) % 4, y, low, core))

    def ewald_group_sum():
        for dx in (1, 3, 2):
            arrive(e1_buf.at[(x + dx) % 4], E1 + (x + dx) % 4)
        e2_send[...] = (e1_buf[0] + e1_buf[1]) + (e1_buf[2] + e1_buf[3])
        place = 2 * z + low
        for dz in (2, 1, 3, 0):
            for flip in (1, 0):
                if dz or flip:
                    send_to(
                        e2_send,
                        e2_buf.at[place],
                        E2 + 2 * dz + flip,
                        E2 + place,
                        dev((z + dz) % 4, x, y, core, (low + flip) % 2),
                    )
        send_or_keep(e2_send, e2_buf.at[place], E2, E2 + place, swap)

    def finish_layer(layer):
        msg[...] = jnp.zeros((FEAT, ATOMS), F32)

        def body(j, carry):
            edge = dot(radial_t[layer], basis_buf[j])
            msg[...] += edge * picked[layer, j].astype(F32)
            return carry

        lax.fori_loop(0, NEIGH, body, 0, unroll=True)
        message = msg[...]
        inverse = lax.rsqrt(jnp.sum(message * message, axis=0, keepdims=True) * (1.0 / FEAT) + 1e-6)
        normed = message * inverse
        normed_buf[layer] = normed
        inv_buf[layer] = jnp.broadcast_to(inverse, (8, ATOMS))
        pre = dot(mix_t[layer], normed.astype(BF16))
        pre_buf[layer] = pre
        gated = (pre * lax.logistic(pre)).astype(BF16)
        hidden[...] += dot(update_t[layer], gated)

    finish_layer(0)
    rounded = hidden[...].astype(BF16)
    ext_rows[:, :ATOMS] = rounded
    send_features(1, rounded)
    ewald_sums()
    gather_part(1, 0, ATOMS, True)
    ewald_ring()
    arrive_sums(mb_buf, MB)
    xp_send[4:8, :] = (mb_buf[0] + mb_buf[1]) + (mb_buf[2] + mb_buf[3])
    send_or_keep(xp_send, xp_buf, XP, XP, swap)
    receive_features(1)
    gather_part(1, ATOMS, EXT, False)
    finish_layer(1)

    def silu_slope(pre):
        sig = lax.logistic(pre)
        return sig * (1.0 + pre * (1.0 - sig))

    final = dot(readout_t[...], hidden[...].astype(BF16))
    dfinal = ew_col * silu_slope(final)
    cotan = dot(readout[...], dfinal.astype(BF16)).astype(BF16)

    def message_cotan(layer, cotan_b):
        dgated = dot(update[layer], cotan_b).astype(BF16).astype(F32)
        dpre = dgated * silu_slope(pre_buf[layer])
        dnormed = dot(mix[layer], dpre.astype(BF16)).astype(BF16).astype(F32)
        normed = normed_buf[layer]
        mean = jnp.sum(dnormed * normed, axis=0, keepdims=True) * (1.0 / FEAT)
        dmsg[...] = inv_buf[layer, 0:1, :] * (dnormed - normed * mean)

    def distance_cotan(layer):
        def body(j, carry):
            dedge = (picked[layer, j].astype(F32) * dmsg[...]).astype(BF16)
            dbasis = dot(radial[layer], dedge).astype(BF16).astype(F32)
            part = jnp.sum(dbasis * slope_buf[j], axis=0, keepdims=True)
            if layer == 1:
                ddist_buf[pl.ds(j, 1), :] = part
            else:
                ddist_buf[pl.ds(j, 1), :] += part
            return carry

        lax.fori_loop(0, NEIGH, body, 0, unroll=True)

    message_cotan(1, cotan)

    def row_cotan(j, carry):
        at = pl.multiple_of(j * ATOMS, ATOMS)
        edge = dot(radial_t[1], basis_buf[j])
        d_picked[:, pl.ds(at, ATOMS)] = (edge * dmsg[...]).astype(BF16)
        return carry

    lax.fori_loop(0, NEIGH, row_cotan, 0, unroll=True)
    for near in range(2):
        side = core if near == 0 else 1 - core
        first = pl.multiple_of(ATOMS + SIDE * side, SIDE)
        pack_side(dg_send.at[side], dot_t(d_picked[...], onehot[pl.ds(first, SIDE), :]))
        send_to(dg_send.at[side], dg_buf.at[1 - side], DG + side, DG + 1 - side, ring_dev(z, 7 - 6 * side))
    ewald_forces()
    for half in range(2):
        drows[:, SIDE * half : SIDE * half + SIDE] = dot_t(
            d_picked[...], onehot[SIDE * half : SIDE * half + SIDE, :]
        )
    distance_cotan(1)
    for near in (1, 0):
        side = core if near == 0 else 1 - core
        arrive(dg_buf.at[side], DG + side)
    for side in range(2):
        unpack_side(dg_rows, dg_buf.at[side], SIDE * side)
    returned = dot_t(dg_rows[...], sel[...])
    owned = (drows[...] + returned).astype(BF16).astype(F32)
    message_cotan(0, (cotan.astype(F32) + owned).astype(BF16))
    distance_cotan(0)
    ewald_group_sum()

    ddist = 2.0 * ddist_buf[...]
    edge_force = [offset_buf[c] * ddist for c in range(3)]
    for c in range(3):
        own = jnp.sum(edge_force[c], axis=0, keepdims=True)
        fo_send[c : c + 1, :] = own
    fo_send[3:4, :] = jnp.zeros((1, ATOMS), F32)

    parts = []
    zero_row = jnp.zeros((1, ATOMS), F32)
    for j in range(NEIGH):
        rows = [edge_force[c][j : j + 1, :] for c in range(3)] + [zero_row] * 5
        parts.append(stacked_parts(jnp.concatenate(rows, 0)))
    force_rows = jnp.concatenate(parts, 1)
    for near in range(2):
        side = core if near == 0 else 1 - core
        first = pl.multiple_of(ATOMS + SIDE * side, SIDE)
        both = dot_t(force_rows, onehot[pl.ds(first, SIDE), :])
        gg_send[side] = both[0:4] + both[8:12]
        send_to(
            gg_send.at[side], gg_buf.at[1 - side], GG + side, GG + 1 - side, swapped_ring_dev(7 - 6 * side)
        )
    both = dot_t(force_rows, onehot[:ATOMS, :])
    fo_send[...] = fo_send[...] - (both[0:4] + both[8:12])
    send_or_keep(fo_send, fo_buf, FO, FO, swap)

    arrive(xp_buf, XP)
    for side in range(2):
        arrive(gg_buf.at[side], GG + side)
    zero4 = jnp.zeros((4, SIDE), F32)
    returned = None
    for side in range(2):
        rows = stacked_parts(jnp.concatenate([gg_buf[side], zero4], 0))
        both = dot_t(rows, sel_own[:, SIDE * side : SIDE * side + SIDE])
        both = both[0:4] + both[8:12]
        returned = both if side == 0 else returned + both
    arrive(fo_buf, FO)
    for place in range(8):
        arrive(e2_buf.at[place], E2 + place)
    long_range = e2_buf[0]
    for place in range(1, 8):
        long_range = long_range + e2_buf[place]
    result = (fo_buf[...] - returned) + long_range
    for c in range(3):
        out[c] = xp_buf[c : c + 1, :]
        out[3 + c] = xp_buf[4 + c : 5 + c, :] + (0.5 * DT) * result[c : c + 1, :]
        out[6 + c] = result[c : c + 1, :]

    for sent in started:
        sent.wait_send()

    @pl.when(jnp.logical_not(same))
    def _():
        for sent in conditional:
            sent.wait_send()

    @pl.when(same)
    def _():
        for dz, flip in targets[:7]:
            sums_copy(2 * dz + flip, ma_send, ma_buf, MA).wait_send()
            sums_copy(2 * dz + flip, mb_send, mb_buf, MB).wait_send()


def local(
    positions,
    momenta,
    forces,
    masses,
    charges,
    embedding,
    neighbours,
    send_rows,
    wavevectors,
    radial_weight,
    mix_weight,
    update_weight,
    readout_weight,
    energy_weight,
):
    piece = (3, 1, ATOMS)
    scratch = [
        (piece, F32),
        (piece, F32),
        (piece, F32),
        ((1, ATOMS), F32),
        ((1, ATOMS), F32),
        ((NEIGH, ATOMS), jnp.int32),
        ((3, 128), jnp.int32),
        ((3, KPART), jnp.int32),
        ((2, BASIS, FEAT), BF16),
        ((2, FEAT, FEAT), BF16),
        ((2, FEAT, FEAT), BF16),
        ((FEAT, FEAT), BF16),
        ((1, FEAT), F32),
        ((8, ATOMS), F32),
        ((8, 8, ATOMS), F32),
        ((FEAT, ATOMS), BF16),
        ((16, ATOMS), F32),
        ((16, ATOMS), F32),
        ((8, 8, ATOMS), F32),
        ((4, 8, ATOMS), F32),
        ((8, 4, ATOMS), F32),
        ((4, 4, ATOMS), F32),
        ((2, 4, SIDE), F32),
        ((2, 4, SIDE), F32),
        ((2, 2, PACKED, 128), BF16),
        ((2, 2, PACKED, 128), BF16),
        ((2, PACKED, 128), BF16),
        ((2, PACKED, 128), BF16),
        ((FEAT, 2 * SIDE), BF16),
        ((2, 2, KPART), F32),
        ((4, 2, KPART), F32),
        ((4, 4, ATOMS), F32),
        ((4, ATOMS), F32),
        ((8, 4, ATOMS), F32),
        ((8, ATOMS), F32),
        ((8, ATOMS), F32),
        ((4, ATOMS), F32),
        ((4, ATOMS), F32),
        ((2, 4, SIDE), F32),
        ((2, 4, SIDE), F32),
        ((ATOMS, 2 * SIDE), BF16),
        ((ATOMS, 2 * SIDE), BF16),
        ((EXT, NEIGH * ATOMS), BF16),
        ((FEAT, EXT), BF16),
        ((2, NEIGH, FEAT, ATOMS), BF16),
        ((FEAT, NEIGH * ATOMS), BF16),
        ((NEIGH, BASIS, ATOMS), BF16),
        ((NEIGH, BASIS, ATOMS), F32),
        ((NEIGH, ATOMS), F32),
        ((NEIGH, ATOMS), F32),
        ((3, NEIGH, ATOMS), F32),
        ((FEAT, ATOMS), F32),
        ((FEAT, ATOMS), F32),
        ((FEAT, ATOMS), F32),
        ((FEAT, ATOMS), F32),
        ((2, FEAT, ATOMS), F32),
        ((2, FEAT, ATOMS), F32),
        ((2, 8, ATOMS), F32),
        ((2, FEAT, FEAT), BF16),
        ((2, FEAT, FEAT), BF16),
        ((FEAT, FEAT), BF16),
        ((2, FEAT, BASIS), BF16),
        ((16, KPART), F32),
        ((KPART, 16), BF16),
        ((16, ATOMS), F32),
        ((KPART, ATOMS), BF16),
        ((KPART, ATOMS), BF16),
    ]
    out = pl.pallas_call(
        step_kernel,
        out_shape=jax.ShapeDtypeStruct((9, 1, ATOMS), F32),
        in_specs=[pl.BlockSpec(memory_space=pltpu.HBM)] * 15,
        out_specs=pl.BlockSpec(memory_space=pltpu.VMEM),
        scratch_shapes=[pltpu.SMEM((3 * BEADS,), F32)]
        + [pltpu.VMEM(shape, kind) for shape, kind in scratch]
        + [
            pltpu.SemaphoreType.DMA((N_SEMS,)),
            pltpu.SemaphoreType.DMA((N_SEMS,)),
            pltpu.SemaphoreType.DMA((14,)),
        ],
        compiler_params=pltpu.CompilerParams(
            collective_id=0, has_side_effects=True, vmem_limit_bytes=60 * 1024 * 1024
        ),
        cost_estimate=pl.CostEstimate(flops=16_000_000_000, bytes_accessed=2_000_000, transcendentals=1_000_000),
    )(
        jnp.asarray(ring_tables()),
        positions,
        momenta,
        forces,
        masses.reshape(1, ATOMS),
        charges.reshape(1, ATOMS),
        embedding.T,
        neighbours,
        send_rows.reshape(3, 128),
        wavevectors,
        radial_weight,
        mix_weight,
        update_weight,
        readout_weight,
        energy_weight.reshape(1, FEAT),
    )
    return out[0:3], out[3:6], out[6:9]


def solution(mesh):
    own = P(None, "bead", "dom")
    placed = (
        own,
        own,
        own,
        P("dom"),
        P("dom"),
        P("dom", None),
        P(None, "dom"),
        P("dom"),
        P(),
        P(),
        P(),
        P(),
        P(),
        P(),
    )
    return jax.shard_map(local, mesh=mesh, in_specs=placed, out_specs=(own, own, own), check_vma=False)
```

```python
import math

import jax
import jax.numpy as jnp
import numpy as np
from jax import lax
from jax.experimental import pallas as pl
from jax.experimental.pallas import tpu as pltpu
from jax.sharding import PartitionSpec as P

MESH = pl.DeviceIdType.MESH
F32 = jnp.float32
BF16 = jnp.bfloat16

BEADS = 32
ATOMS = 512
TOTAL_ATOMS = 4096
GHOST = 192
SIDE = 256
EXT = ATOMS + 2 * SIDE
NEIGH = 8
FEAT = 240
BASIS = 16
KVEC = 16384
KPART = KVEC // BEADS
DT = 0.25
TWO_PI = 2.0 * math.pi
PACKED = FEAT + 128

S1, EMB, PACK, MA, MB, GH, FG, DG, SA, SB, E1, E2, XP, FO, GG, N_SEMS = np.cumsum(
    [0, 8, 1, 1, 8, 8, 2, 4, 2, 1, 4, 4, 8, 1, 1, 2]
).tolist()


def ring_tables():
    k = np.arange(BEADS)
    b = np.arange(BEADS)[:, None]
    angle = 2.0 * np.pi / BEADS * (b * k % BEADS)
    half = BEADS // 2
    basis = np.where(k < half, np.cos(angle), np.sin(angle)) * math.sqrt(2.0 / BEADS)
    basis = np.where(k == 0, math.sqrt(1.0 / BEADS), basis)
    basis = np.where(k == half, math.sqrt(1.0 / BEADS) * (1 - 2 * (b % 2)), basis)
    omega = 3.2 * np.sin(np.pi * k / BEADS)
    cosine, sine = np.cos(omega * DT), np.sin(omega * DT)
    drift = np.where(k == 0, DT, sine / np.where(k == 0, 1.0, omega))
    rows = [(basis * value) @ basis.T for value in (cosine, drift, omega * sine)]
    return np.concatenate([row[0] for row in rows]).astype(np.float32)


def dot(a, b):
    return lax.dot_general(a, b, (((1,), (0,)), ((), ())), preferred_element_type=F32)


def dot_t(a, b):
    return lax.dot_general(a, b, (((1,), (1,)), ((), ())), preferred_element_type=F32)


def rows_of(shape):
    return lax.broadcasted_iota(jnp.int32, shape, 0)


def lanes_of(shape):
    return lax.broadcasted_iota(jnp.int32, shape, 1)


def two_parts(value):
    high = value.astype(BF16)
    return high, (value - high.astype(F32)).astype(BF16)


def stacked_parts(value):
    high = value.astype(BF16).astype(F32)
    return jnp.concatenate([high, value - high], 0).astype(BF16)


def lane_pick(tables, index):
    result = None
    for number, block in enumerate(tables):
        local = index - 128 * number
        inside = jnp.logical_and(local >= 0, local < 128)
        got = jnp.take_along_axis(block, jnp.where(inside, local, 0), axis=1, mode="promise_in_bounds")
        result = jnp.where(inside, got, 0.0 if result is None else result)
    return result


def step_kernel(
    coef_in,
    pos_in,
    mom_in,
    force_in,
    mass_in,
    charge_in,
    emb,
    neigh_in,
    send_in,
    wave_in,
    radial_in,
    mix_in,
    update_in,
    readout_in,
    ew_in,
    out,
    coef,
    pos,
    mom,
    force,
    mass,
    charge,
    neigh,
    send,
    wave,
    radial,
    mix,
    update,
    readout,
    ew,
    v_own,
    v_all,
    emb_buf,
    pack_own,
    pack_buf,
    ma_send,
    ma_buf,
    mb_send,
    mb_buf,
    gh_send,
    gh_buf,
    fg_send,
    fg_buf,
    dg_send,
    dg_buf,
    dg_rows,
    sa_buf,
    sb_buf,
    e1_buf,
    e2_send,
    e2_buf,
    xp_send,
    xp_buf,
    fo_send,
    fo_buf,
    gg_send,
    gg_buf,
    sel,
    sel_own,
    onehot,
    ext_rows,
    picked,
    d_picked,
    basis_buf,
    slope_buf,
    dist_buf,
    ddist_buf,
    offset_buf,
    msg,
    dmsg,
    drows,
    hidden,
    pre_buf,
    normed_buf,
    inv_buf,
    mix_t,
    update_t,
    readout_t,
    radial_t,
    wave_buf,
    wave_t,
    r_buf,
    cos_buf,
    sin_buf,
    send_sem,
    recv_sem,
    load_sem,
):
    bead = lax.axis_index("bead")
    dom = lax.axis_index("dom")
    z, x, core = bead // 8, (bead // 2) % 4, bead % 2
    y, low = dom // 2, dom % 2
    ring = 2 * y + core

    def dev(z_, x_, y_, low_, core_):
        return ((z_ * 4 + x_) * 2 + core_, y_ * 2 + low_)

    def ring_dev(z_, step):
        place = (ring + step) % 8
        return dev(z_, x, place // 2, low, place % 2)

    def swapped_ring_dev(step):
        place = (ring + step) % 8
        return dev(z, x, place // 2, place % 2, low)

    def copy(src, dst, send_at, recv_at, target):
        return pltpu.make_async_remote_copy(
            src_ref=src,
            dst_ref=dst,
            send_sem=send_sem.at[send_at],
            recv_sem=recv_sem.at[recv_at],
            device_id=target,
            device_id_type=MESH,
        )

    def arrive(dst, recv_at):
        copy(dst, dst, 0, recv_at, dev(z, x, y, low, 1 - core)).wait_recv()

    started = []

    def send_to(src, dst, send_at, recv_at, target):
        sent = copy(src, dst, send_at, recv_at, target)
        sent.start()
        started.append(sent)

    k_first = pl.multiple_of((bead - core + low) * KPART, KPART)
    loads = {}
    for number, (src, dst) in enumerate(
        (
            (pos_in, pos),
            (mom_in, mom),
            (force_in, force),
            (mass_in, mass),
            (charge_in, charge),
            (neigh_in, neigh),
            (send_in, send),
            (coef_in, coef),
            (radial_in, radial),
            (mix_in, mix),
            (update_in, update),
            (readout_in, readout),
            (ew_in, ew),
            (wave_in.at[:, pl.ds(k_first, KPART)], wave),
        )
    ):
        loads[number] = pltpu.make_async_copy(src, dst, load_sem.at[number])
        if number < 3:
            loads[number].start()

    same = low == core
    conditional = []

    def send_or_keep(src, dst, send_at, recv_at, target):
        sent = copy(src, dst, send_at, recv_at, target)

        @pl.when(same)
        def _():
            pltpu.make_async_copy(src, dst, recv_sem.at[recv_at]).start()

        @pl.when(jnp.logical_not(same))
        def _():
            sent.start()

        conditional.append(sent)

    barrier = pltpu.get_barrier_semaphore()

    def greet(target):
        pl.semaphore_signal(barrier, inc=1, device_id=target, device_id_type=MESH)

    far = dev((z + 3 + 2 * low) % 4, x, y, 1 - low, low)
    for dz in (2, 1, 3):
        greet(dev((z + dz) % 4, x, y, core, core))
    greet(ring_dev(z, 4))

    @pl.when(same)
    def _():
        for dx, flip in ((2, 1), (2, 0), (1, 1), (3, 1), (1, 0), (3, 0), (0, 1)):
            greet(dev(z, (x + dx) % 4, y, core, (low + flip) % 2))

    @pl.when(jnp.logical_not(same))
    def _():
        greet(far)
        greet(dev(z, x, y, core, core))

    greet(ring_dev(z, 7 - 6 * core))
    greet(ring_dev(z, 1 + 6 * core))

    for number in range(3, 7):
        loads[number].start()

    for number in range(3):
        loads[number].wait()
    v_own[...] = jnp.zeros((8, ATOMS), F32)
    for c in range(3):
        v_own[c : c + 1, :] = pos[c]
        v_own[4 + c : 5 + c, :] = mom[c] + (0.5 * DT) * force[c]
    pl.semaphore_wait(barrier, jnp.where(same, 13, 8))

    slot = x * 2 + core
    for dx in (2, 1, 3):
        send_to(v_own, v_all.at[slot], S1 + dx, S1 + slot, dev(z, (x + dx) % 4, y, low, low))
    send_or_keep(v_own, v_all.at[slot], S1, S1 + slot, dev(z, x, y, low, low))
    for number in range(7, 14):
        loads[number].start()
    for number in range(3, 7):
        loads[number].wait()
    lane = lanes_of((1, 2 * SIDE))
    rows384 = jnp.concatenate(
        [send[0:1, :], send[1:2, :], send[2:3, :], jnp.zeros((1, 128), jnp.int32)], 1
    )
    shifted = pltpu.roll(rows384, 64, 1)
    spread = jnp.where(
        lane < GHOST,
        rows384,
        jnp.where(jnp.logical_and(lane >= SIDE, lane < SIDE + GHOST), shifted, -1),
    ).astype(F32)
    table = neigh[...]
    pack_own[0:8, :] = jnp.where(table >= ATOMS + GHOST, table + (SIDE - GHOST), table).astype(F32)
    pack_own[8:9, :] = mass[...]
    pack_own[9:10, :] = charge[...]
    pack_own[10:11, :] = spread
    pack_own[11:16, :] = jnp.zeros((5, ATOMS), F32)
    swap = dev(z, x, y, core, low)
    send_or_keep(pack_own, pack_buf, PACK, PACK, far)
    send_or_keep(emb, emb_buf, EMB, EMB, far)

    for number in range(7, 14):
        loads[number].wait()

    eye = (rows_of((FEAT, FEAT)) == lanes_of((FEAT, FEAT))).astype(F32)
    eye_b = eye.astype(BF16)
    for layer in range(2):
        mix_t[layer] = dot_t(eye_b, mix[layer]).astype(BF16)
        update_t[layer] = dot_t(eye_b, update[layer]).astype(BF16)
        radial_t[layer] = dot_t(eye_b, radial[layer]).astype(BF16)
    readout_t[...] = dot_t(eye_b, readout[...]).astype(BF16)
    ew_col = jnp.sum(eye * ew[...], axis=1, keepdims=True)
    own_spread = jnp.broadcast_to(spread, (ATOMS, 2 * SIDE))
    atom_rows = rows_of((ATOMS, 2 * SIDE)).astype(F32)
    sel_own[...] = jnp.where(own_spread == atom_rows, 1.0, 0.0).astype(BF16)
    triple = wave[...].astype(F32)
    wave_buf[...] = jnp.zeros((16, KPART), F32)
    for part in range(3):
        wave_buf[4 * part : 4 * part + 3, :] = triple
    wave_t[...] = jnp.transpose(wave_buf[...]).astype(BF16)

    arrive(pack_buf, PACK)
    charges = pack_buf[9:10, :]
    send_row = pack_buf[10:11, :]
    sel[...] = jnp.where(jnp.broadcast_to(send_row, (ATOMS, 2 * SIDE)) == atom_rows, 1.0, 0.0).astype(BF16)
    send_index = jnp.broadcast_to(send_row, (8, 2 * SIDE)).astype(jnp.int32)

    row8 = rows_of((8, ATOMS))
    targets = [(2, 0), (2, 1), (1, 0), (3, 0), (1, 1), (3, 1), (0, 1), (0, 0)]

    def sums_copy(number, src, dst, first_sem):
        target = dev((z + number // 2) % 4, x, y, (low + number % 2) % 2, core)
        return copy(src.at[number], dst.at[z], first_sem + number, first_sem + z, target)

    @pl.when(same)
    def _():
        for k in range(8):
            arrive(v_all.at[k], S1 + k)
        upper = row8 < 4
        inv_mass = 1.0 / mass[...]
        scale = jnp.where(upper, inv_mass, -mass[...])
        beads_in = [v_all[k] for k in range(8)]
        total = beads_in[0]
        for k in range(1, 8):
            total = total + beads_in[k]
        centre_part = (total + DT * inv_mass * pltpu.roll(total, 4, 0)) * (1.0 / BEADS)
        centre_low = pltpu.roll(centre_part, 4, 0)
        first_row = rows_of((8, 1)) < 4
        for dz, flip in targets:
            z_to, low_to, number = (z + dz) % 4, (low + flip) % 2, 2 * dz + flip
            straight = None
            for k in range(8):
                shift = (8 * (z_to - z) + 2 * x + low_to - k + 64) % BEADS
                same_kind = coef[shift] * beads_in[k]
                other = jnp.where(first_row, coef[2 * BEADS + shift], coef[BEADS + shift]) * beads_in[k]
                straight = same_kind if k == 0 else straight + same_kind
                crossed = other if k == 0 else crossed + other
            moved = straight + scale * pltpu.roll(crossed, 4, 0)
            ma = jnp.where(upper, moved, centre_low)
            if number:
                ma_send[number] = ma
                mb_send[number] = moved[4:8]
                sums_copy(number, ma_send, ma_buf, MA).start()
            else:
                ma_buf[z] = ma
                mb_buf[z] = moved[4:8]

    def arrive_sums(buf, first_sem):
        @pl.when(jnp.logical_not(same))
        def _():
            arrive(buf.at[z], first_sem + z)

        for dz in (1, 3, 2):
            arrive(buf.at[(z + dz) % 4], first_sem + (z + dz) % 4)

    def pack_side(ref, value):
        ref[0:FEAT, :] = value[:, 0:128].astype(BF16)
        rest = jnp.concatenate([value[128:FEAT, 128:SIDE], jnp.zeros((256 - FEAT, 128), F32)], 0)
        ref[FEAT:PACKED, :] = (value[0:128, 128:SIDE] + pltpu.roll(rest, 64, 1)).astype(BF16)

    def unpack_side(ref, packed, first):
        ref[:, first : first + 128] = packed[0:FEAT, :]
        rest = packed[FEAT:PACKED, :].astype(F32)
        ref[0:128, first + 128 : first + SIDE] = rest.astype(BF16)
        ref[128:FEAT, first + 128 : first + SIDE] = pltpu.roll(rest, 64, 1)[0 : FEAT - 128].astype(BF16)

    def send_sides(src, dst, first_sem):
        for near in range(2):
            side = core if near == 0 else 1 - core
            send_to(
                src.at[side], dst.at[1 - side], first_sem + side, first_sem + 1 - side, ring_dev(z, 7 - 6 * side)
            )

    def send_features(layer, rounded):
        ghosts = dot(rounded, sel[...])
        for side in range(2):
            pack_side(fg_send.at[layer, side], ghosts[:, SIDE * side : SIDE * (side + 1)])
        send_sides(fg_send.at[layer], fg_buf.at[layer], FG + 2 * layer)

    def receive_features(layer):
        for side in range(2):
            arrive(fg_buf.at[layer, side], FG + 2 * layer + side)
            unpack_side(ext_rows, fg_buf.at[layer, side], ATOMS + SIDE * side)

    arrive(emb_buf, EMB)
    rounded = emb_buf[...]
    hidden[...] = rounded.astype(F32)
    ext_rows[:, :ATOMS] = rounded
    send_features(0, rounded)

    @pl.when(same)
    def _():
        for dz, flip in targets[:7]:
            sums_copy(2 * dz + flip, mb_send, mb_buf, MB).start()

    group_rows = [(rows_of((16, ATOMS)) + 16 * g).astype(F32) for g in range(8)]

    def build(j, carry):
        index = pack_buf[pl.ds(j, 1), :]
        at = pl.multiple_of(j * ATOMS, ATOMS)
        for block in range(EXT // 128):
            local = jnp.broadcast_to(index - 128.0 * block, (16, ATOMS))
            for g in range(8):
                first = 128 * block + 16 * g
                onehot[first : first + 16, pl.ds(at, ATOMS)] = jnp.where(
                    local == group_rows[g], 1.0, 0.0
                ).astype(BF16)
        return carry

    lax.fori_loop(0, NEIGH, build, 0)

    def gather_part(layer, first, last, fresh):
        def body(j, carry):
            at = pl.multiple_of(j * ATOMS, ATOMS)
            part = dot(ext_rows[:, first:last], onehot[first:last, pl.ds(at, ATOMS)])
            if not fresh:
                part = part + picked[layer, j].astype(F32)
            picked[layer, j] = part.astype(BF16)
            return carry

        lax.fori_loop(0, NEIGH, body, 0, unroll=True)

    gather_part(0, 0, ATOMS, True)

    arrive_sums(ma_buf, MA)
    moved = (ma_buf[0] + ma_buf[1]) + (ma_buf[2] + ma_buf[3])
    centre = moved[4:7]
    xp_send[...] = moved
    for c in range(3):
        blocks = [
            jnp.broadcast_to(moved[c : c + 1, 128 * n : 128 * n + 128], (8, 128)) for n in range(4)
        ]
        for n in range(4):
            got = lane_pick(blocks, send_index[:, 128 * n : 128 * n + 128])
            gh_send[n // 2, c : c + 1, 128 * (n % 2) : 128 * (n % 2) + 128] = got[0:1]
    gh_send[:, 3:4, :] = jnp.zeros((2, 1, SIDE), F32)
    send_sides(gh_send, gh_buf, GH)
    receive_features(0)
    gather_part(0, ATOMS, EXT, False)
    turns = centre * 0.25
    high = turns.astype(BF16).astype(F32)
    rest = turns - high
    middle = rest.astype(BF16).astype(F32)
    r_buf[...] = jnp.zeros((16, ATOMS), F32)
    for number, value in enumerate((high, middle, rest - middle)):
        r_buf[4 * number : 4 * number + 3, :] = value

    def ewald_sums():
        phase = r_buf[...].astype(BF16)

        def body(i, carry):
            at = pl.multiple_of(i * 128, 128)
            turn = dot(wave_t[pl.ds(at, 128), :], phase)
            half = (turn - jnp.round(turn)) * math.pi
            q = half * half
            s = half * (
                1.0
                + q
                * (
                    -1.6666666641e-1
                    + q * (8.3333293858e-3 + q * (-1.9840083133e-4 + q * (2.7523971075e-6 - 2.3868346521e-8 * q)))
                )
            )
            c = 1.0 + q * (
                -0.5
                + q
                * (
                    4.1666666658e-2
                    + q
                    * (
                        -1.3888888388e-3
                        + q * (2.4801544910e-5 + q * (-2.7556993055e-7 + 2.0737354e-9 * q))
                    )
                )
            )
            sin_buf[pl.ds(at, 128), :] = (2.0 * s * c).astype(BF16)
            cos_buf[pl.ds(at, 128), :] = (1.0 - 2.0 * s * s).astype(BF16)
            return carry

        lax.fori_loop(0, KPART // 128, body, 0, unroll=True)
        weights = stacked_parts(jnp.broadcast_to(charges, (8, ATOMS)))
        for number, ref in enumerate((cos_buf, sin_buf)):
            sums = dot_t(weights, ref[...])
            sa_buf[core, number : number + 1, :] = sums[0:1] + sums[8:9]
        send_to(sa_buf.at[core], sa_buf.at[core], SA, SA, dev(z, x, y, low, 1 - core))

    def ewald_ring():
        arrive(sa_buf.at[1 - core], SA)
        sb_buf[y] = sa_buf[0] + sa_buf[1]
        for dy in range(1, 4):
            send_to(sb_buf.at[y], sb_buf.at[y], SB + dy, SB + y, dev(z, x, (y + dy) % 4, low, core))

    ghosts_at = []
    for side in range(2):
        arrive(gh_buf.at[side], GH + side)
        ghosts_at.append(gh_buf[side])
    index8 = pack_buf[0:8, :].astype(jnp.int32)
    distance = None
    for c in range(3):
        blocks = [moved[c : c + 1, 128 * n : 128 * n + 128] for n in range(4)]
        for side in range(2):
            blocks += [ghosts_at[side][c : c + 1, 128 * n : 128 * n + 128] for n in range(2)]
        blocks = [jnp.broadcast_to(block, (8, 128)) for block in blocks]
        others = jnp.concatenate(
            [lane_pick(blocks, index8[:, 128 * n : 128 * n + 128]) for n in range(4)], 1
        )
        offset = others - moved[c : c + 1, :]
        offset_buf[c] = offset
        distance = offset * offset if c == 0 else distance + offset * offset
    dist_buf[...] = distance
    m_row = rows_of((BASIS, ATOMS))
    rates = jnp.where(m_row % 2 == 1, 0.125 * math.sqrt(2.0), 0.125) * jnp.left_shift(1, m_row // 2).astype(F32)
    for j in range(NEIGH):
        exact = 1.0 / (1.0 + rates * dist_buf[j : j + 1, :])
        basis_buf[j] = exact.astype(BF16)
        slope_buf[j] = -rates * exact * exact

    def ewald_forces():
        for dy in range(1, 4):
            arrive(sb_buf.at[(y + dy) % 4], SB + (y + dy) % 4)
        sums = (sb_buf[0] + sb_buf[1]) + (sb_buf[2] + sb_buf[3])
        recip = wave_buf[0:8, :] * (TWO_PI / 4.0)
        recip = jnp.where(row8 < 3, recip, 0.0)
        square = jnp.sum(recip * recip, axis=0, keepdims=True)
        damping = 48.0 / math.sqrt(KVEC * TOTAL_ATOMS) * jnp.exp(-0.002 * square) / square
        from_sin = stacked_parts(recip * (damping * sums[0:1]))
        from_cos = stacked_parts(recip * (damping * sums[1:2]))
        part = dot(from_sin, sin_buf[...]) - dot(from_cos, cos_buf[...])
        part = 2.0 * charges * (part[0:8] + part[8:16])
        e1_buf[x] = part[0:4]
        for dx in (2, 1, 3):
            send_to(e1_buf.at[x], e1_buf.at[x], E1 + dx, E1 + x, dev(z, (x + dx) % 4, y, low, core))

    def ewald_group_sum():
        for dx in (1, 3, 2):
            arrive(e1_buf.at[(x + dx) % 4], E1 + (x + dx) % 4)
        e2_send[...] = (e1_buf[0] + e1_buf[1]) + (e1_buf[2] + e1_buf[3])
        place = 2 * z + low
        for dz in (2, 1, 3, 0):
            for flip in (1, 0):
                if dz or flip:
                    send_to(
                        e2_send,
                        e2_buf.at[place],
                        E2 + 2 * dz + flip,
                        E2 + place,
                        dev((z + dz) % 4, x, y, core, (low + flip) % 2),
                    )
        send_or_keep(e2_send, e2_buf.at[place], E2, E2 + place, swap)

    def finish_layer(layer):
        msg[...] = jnp.zeros((FEAT, ATOMS), F32)

        def body(j, carry):
            edge = dot(radial_t[layer], basis_buf[j])
            msg[...] += edge * picked[layer, j].astype(F32)
            return carry

        lax.fori_loop(0, NEIGH, body, 0, unroll=True)
        message = msg[...]
        inverse = lax.rsqrt(jnp.sum(message * message, axis=0, keepdims=True) * (1.0 / FEAT) + 1e-6)
        normed = message * inverse
        normed_buf[layer] = normed
        inv_buf[layer] = jnp.broadcast_to(inverse, (8, ATOMS))
        pre = dot(mix_t[layer], normed.astype(BF16))
        pre_buf[layer] = pre
        gated = (pre * lax.logistic(pre)).astype(BF16)
        hidden[...] += dot(update_t[layer], gated)

    finish_layer(0)
    rounded = hidden[...].astype(BF16)
    ext_rows[:, :ATOMS] = rounded
    send_features(1, rounded)
    ewald_sums()
    gather_part(1, 0, ATOMS, True)
    ewald_ring()
    arrive_sums(mb_buf, MB)
    xp_send[4:8, :] = (mb_buf[0] + mb_buf[1]) + (mb_buf[2] + mb_buf[3])
    send_or_keep(xp_send, xp_buf, XP, XP, swap)
    receive_features(1)
    gather_part(1, ATOMS, EXT, False)
    finish_layer(1)

    def silu_slope(pre):
        sig = lax.logistic(pre)
        return sig * (1.0 + pre * (1.0 - sig))

    final = dot(readout_t[...], hidden[...].astype(BF16))
    dfinal = ew_col * silu_slope(final)
    cotan = dot(readout[...], dfinal.astype(BF16)).astype(BF16)

    def message_cotan(layer, cotan_b):
        dgated = dot(update[layer], cotan_b).astype(BF16).astype(F32)
        dpre = dgated * silu_slope(pre_buf[layer])
        dnormed = dot(mix[layer], dpre.astype(BF16)).astype(BF16).astype(F32)
        normed = normed_buf[layer]
        mean = jnp.sum(dnormed * normed, axis=0, keepdims=True) * (1.0 / FEAT)
        dmsg[...] = inv_buf[layer, 0:1, :] * (dnormed - normed * mean)

    def distance_cotan(layer):
        def body(j, carry):
            dedge = (picked[layer, j].astype(F32) * dmsg[...]).astype(BF16)
            dbasis = dot(radial[layer], dedge).astype(BF16).astype(F32)
            part = jnp.sum(dbasis * slope_buf[j], axis=0, keepdims=True)
            if layer == 1:
                ddist_buf[pl.ds(j, 1), :] = part
            else:
                ddist_buf[pl.ds(j, 1), :] += part
            return carry

        lax.fori_loop(0, NEIGH, body, 0, unroll=True)

    message_cotan(1, cotan)

    def row_cotan(j, carry):
        at = pl.multiple_of(j * ATOMS, ATOMS)
        edge = dot(radial_t[1], basis_buf[j])
        d_picked[:, pl.ds(at, ATOMS)] = (edge * dmsg[...]).astype(BF16)
        return carry

    lax.fori_loop(0, NEIGH, row_cotan, 0, unroll=True)
    for near in range(2):
        side = core if near == 0 else 1 - core
        first = pl.multiple_of(ATOMS + SIDE * side, SIDE)
        pack_side(dg_send.at[side], dot_t(d_picked[...], onehot[pl.ds(first, SIDE), :]))
        send_to(dg_send.at[side], dg_buf.at[1 - side], DG + side, DG + 1 - side, ring_dev(z, 7 - 6 * side))
    ewald_forces()
    for half in range(2):
        drows[:, SIDE * half : SIDE * half + SIDE] = dot_t(
            d_picked[...], onehot[SIDE * half : SIDE * half + SIDE, :]
        )
    distance_cotan(1)
    for near in (1, 0):
        side = core if near == 0 else 1 - core
        arrive(dg_buf.at[side], DG + side)
    for side in range(2):
        unpack_side(dg_rows, dg_buf.at[side], SIDE * side)
    returned = dot_t(dg_rows[...], sel[...])
    owned = (drows[...] + returned).astype(BF16).astype(F32)
    message_cotan(0, (cotan.astype(F32) + owned).astype(BF16))
    distance_cotan(0)
    ewald_group_sum()

    ddist = 2.0 * ddist_buf[...]
    edge_force = [offset_buf[c] * ddist for c in range(3)]
    for c in range(3):
        own = jnp.sum(edge_force[c], axis=0, keepdims=True)
        fo_send[c : c + 1, :] = own
    fo_send[3:4, :] = jnp.zeros((1, ATOMS), F32)

    parts = []
    zero_row = jnp.zeros((1, ATOMS), F32)
    for j in range(NEIGH):
        rows = [edge_force[c][j : j + 1, :] for c in range(3)] + [zero_row] * 5
        parts.append(stacked_parts(jnp.concatenate(rows, 0)))
    force_rows = jnp.concatenate(parts, 1)
    for near in range(2):
        side = core if near == 0 else 1 - core
        first = pl.multiple_of(ATOMS + SIDE * side, SIDE)
        both = dot_t(force_rows, onehot[pl.ds(first, SIDE), :])
        gg_send[side] = both[0:4] + both[8:12]
        send_to(
            gg_send.at[side], gg_buf.at[1 - side], GG + side, GG + 1 - side, swapped_ring_dev(7 - 6 * side)
        )
    both = dot_t(force_rows, onehot[:ATOMS, :])
    fo_send[...] = fo_send[...] - (both[0:4] + both[8:12])
    send_or_keep(fo_send, fo_buf, FO, FO, swap)

    arrive(xp_buf, XP)
    for side in range(2):
        arrive(gg_buf.at[side], GG + side)
    zero4 = jnp.zeros((4, SIDE), F32)
    returned = None
    for side in range(2):
        rows = stacked_parts(jnp.concatenate([gg_buf[side], zero4], 0))
        both = dot_t(rows, sel_own[:, SIDE * side : SIDE * side + SIDE])
        both = both[0:4] + both[8:12]
        returned = both if side == 0 else returned + both
    arrive(fo_buf, FO)
    for place in range(8):
        arrive(e2_buf.at[place], E2 + place)
    long_range = e2_buf[0]
    for place in range(1, 8):
        long_range = long_range + e2_buf[place]
    result = (fo_buf[...] - returned) + long_range
    for c in range(3):
        out[c] = xp_buf[c : c + 1, :]
        out[3 + c] = xp_buf[4 + c : 5 + c, :] + (0.5 * DT) * result[c : c + 1, :]
        out[6 + c] = result[c : c + 1, :]

    for sent in started:
        sent.wait_send()

    @pl.when(jnp.logical_not(same))
    def _():
        for sent in conditional:
            sent.wait_send()

    @pl.when(same)
    def _():
        for dz, flip in targets[:7]:
            sums_copy(2 * dz + flip, ma_send, ma_buf, MA).wait_send()
            sums_copy(2 * dz + flip, mb_send, mb_buf, MB).wait_send()


def local(
    positions,
    momenta,
    forces,
    masses,
    charges,
    embedding,
    neighbours,
    send_rows,
    wavevectors,
    radial_weight,
    mix_weight,
    update_weight,
    readout_weight,
    energy_weight,
):
    piece = (3, 1, ATOMS)
    scratch = [
        (piece, F32),
        (piece, F32),
        (piece, F32),
        ((1, ATOMS), F32),
        ((1, ATOMS), F32),
        ((NEIGH, ATOMS), jnp.int32),
        ((3, 128), jnp.int32),
        ((3, KPART), jnp.int32),
        ((2, BASIS, FEAT), BF16),
        ((2, FEAT, FEAT), BF16),
        ((2, FEAT, FEAT), BF16),
        ((FEAT, FEAT), BF16),
        ((1, FEAT), F32),
        ((8, ATOMS), F32),
        ((8, 8, ATOMS), F32),
        ((FEAT, ATOMS), BF16),
        ((16, ATOMS), F32),
        ((16, ATOMS), F32),
        ((8, 8, ATOMS), F32),
        ((4, 8, ATOMS), F32),
        ((8, 4, ATOMS), F32),
        ((4, 4, ATOMS), F32),
        ((2, 4, SIDE), F32),
        ((2, 4, SIDE), F32),
        ((2, 2, PACKED, 128), BF16),
        ((2, 2, PACKED, 128), BF16),
        ((2, PACKED, 128), BF16),
        ((2, PACKED, 128), BF16),
        ((FEAT, 2 * SIDE), BF16),
        ((2, 2, KPART), F32),
        ((4, 2, KPART), F32),
        ((4, 4, ATOMS), F32),
        ((4, ATOMS), F32),
        ((8, 4, ATOMS), F32),
        ((8, ATOMS), F32),
        ((8, ATOMS), F32),
        ((4, ATOMS), F32),
        ((4, ATOMS), F32),
        ((2, 4, SIDE), F32),
        ((2, 4, SIDE), F32),
        ((ATOMS, 2 * SIDE), BF16),
        ((ATOMS, 2 * SIDE), BF16),
        ((EXT, NEIGH * ATOMS), BF16),
        ((FEAT, EXT), BF16),
        ((2, NEIGH, FEAT, ATOMS), BF16),
        ((FEAT, NEIGH * ATOMS), BF16),
        ((NEIGH, BASIS, ATOMS), BF16),
        ((NEIGH, BASIS, ATOMS), F32),
        ((NEIGH, ATOMS), F32),
        ((NEIGH, ATOMS), F32),
        ((3, NEIGH, ATOMS), F32),
        ((FEAT, ATOMS), F32),
        ((FEAT, ATOMS), F32),
        ((FEAT, ATOMS), F32),
        ((FEAT, ATOMS), F32),
        ((2, FEAT, ATOMS), F32),
        ((2, FEAT, ATOMS), F32),
        ((2, 8, ATOMS), F32),
        ((2, FEAT, FEAT), BF16),
        ((2, FEAT, FEAT), BF16),
        ((FEAT, FEAT), BF16),
        ((2, FEAT, BASIS), BF16),
        ((16, KPART), F32),
        ((KPART, 16), BF16),
        ((16, ATOMS), F32),
        ((KPART, ATOMS), BF16),
        ((KPART, ATOMS), BF16),
    ]
    out = pl.pallas_call(
        step_kernel,
        out_shape=jax.ShapeDtypeStruct((9, 1, ATOMS), F32),
        in_specs=[pl.BlockSpec(memory_space=pltpu.HBM)] * 15,
        out_specs=pl.BlockSpec(memory_space=pltpu.VMEM),
        scratch_shapes=[pltpu.SMEM((3 * BEADS,), F32)]
        + [pltpu.VMEM(shape, kind) for shape, kind in scratch]
        + [
            pltpu.SemaphoreType.DMA((N_SEMS,)),
            pltpu.SemaphoreType.DMA((N_SEMS,)),
            pltpu.SemaphoreType.DMA((14,)),
        ],
        compiler_params=pltpu.CompilerParams(
            collective_id=0, has_side_effects=True, vmem_limit_bytes=60 * 1024 * 1024
        ),
        cost_estimate=pl.CostEstimate(flops=16_000_000_000, bytes_accessed=2_000_000, transcendentals=1_000_000),
    )(
        jnp.asarray(ring_tables()),
        positions,
        momenta,
        forces,
        masses.reshape(1, ATOMS),
        charges.reshape(1, ATOMS),
        embedding.T,
        neighbours,
        send_rows.reshape(3, 128),
        wavevectors,
        radial_weight,
        mix_weight,
        update_weight,
        readout_weight,
        energy_weight.reshape(1, FEAT),
    )
    return out[0:3], out[3:6], out[6:9]


def solution(mesh):
    own = P(None, "bead", "dom")
    placed = (
        own,
        own,
        own,
        P("dom"),
        P("dom"),
        P("dom", None),
        P(None, "dom"),
        P("dom"),
        P(),
        P(),
        P(),
        P(),
        P(),
        P(),
    )
    return jax.shard_map(local, mesh=mesh, in_specs=placed, out_specs=(own, own, own), check_vma=False)
```

```python
import math

import jax
import jax.numpy as jnp
import numpy as np
from jax import lax
from jax.experimental import pallas as pl
from jax.experimental.pallas import tpu as pltpu
from jax.sharding import PartitionSpec as P

MESH = pl.DeviceIdType.MESH
F32 = jnp.float32
BF16 = jnp.bfloat16

BEADS = 32
ATOMS = 512
TOTAL_ATOMS = 4096
GHOST = 192
SIDE = 256
EXT = ATOMS + 2 * SIDE
NEIGH = 8
FEAT = 240
BASIS = 16
KVEC = 16384
KPART = KVEC // BEADS
DT = 0.25
TWO_PI = 2.0 * math.pi
PACKED = FEAT + 128

S1, EMB, PACK, MA, MB, GH, FG, DG, SA, SB, E1, E2, XP, FO, GG, N_SEMS = np.cumsum(
    [0, 8, 1, 1, 8, 8, 2, 4, 2, 1, 4, 4, 8, 1, 1, 2]
).tolist()


def ring_tables():
    k = np.arange(BEADS)
    b = np.arange(BEADS)[:, None]
    angle = 2.0 * np.pi / BEADS * (b * k % BEADS)
    half = BEADS // 2
    basis = np.where(k < half, np.cos(angle), np.sin(angle)) * math.sqrt(2.0 / BEADS)
    basis = np.where(k == 0, math.sqrt(1.0 / BEADS), basis)
    basis = np.where(k == half, math.sqrt(1.0 / BEADS) * (1 - 2 * (b % 2)), basis)
    omega = 3.2 * np.sin(np.pi * k / BEADS)
    cosine, sine = np.cos(omega * DT), np.sin(omega * DT)
    drift = np.where(k == 0, DT, sine / np.where(k == 0, 1.0, omega))
    rows = [(basis * value) @ basis.T for value in (cosine, drift, omega * sine)]
    return np.concatenate([row[0] for row in rows]).astype(np.float32)


def dot(a, b):
    return lax.dot_general(a, b, (((1,), (0,)), ((), ())), preferred_element_type=F32)


def dot_t(a, b):
    return lax.dot_general(a, b, (((1,), (1,)), ((), ())), preferred_element_type=F32)


def rows_of(shape):
    return lax.broadcasted_iota(jnp.int32, shape, 0)


def lanes_of(shape):
    return lax.broadcasted_iota(jnp.int32, shape, 1)


def two_parts(value):
    high = value.astype(BF16)
    return high, (value - high.astype(F32)).astype(BF16)


def stacked_parts(value):
    high = value.astype(BF16).astype(F32)
    return jnp.concatenate([high, value - high], 0).astype(BF16)


def lane_pick(tables, index):
    result = None
    for number, block in enumerate(tables):
        local = index - 128 * number
        inside = jnp.logical_and(local >= 0, local < 128)
        got = jnp.take_along_axis(block, jnp.where(inside, local, 0), axis=1, mode="promise_in_bounds")
        result = jnp.where(inside, got, 0.0 if result is None else result)
    return result


def step_kernel(
    coef_in,
    pos_in,
    mom_in,
    force_in,
    mass_in,
    charge_in,
    emb,
    neigh_in,
    send_in,
    wave_in,
    radial_in,
    mix_in,
    update_in,
    readout_in,
    ew_in,
    out,
    coef,
    pos,
    mom,
    force,
    mass,
    charge,
    neigh,
    send,
    wave,
    radial,
    mix,
    update,
    readout,
    ew,
    v_own,
    v_all,
    emb_buf,
    pack_own,
    pack_buf,
    ma_send,
    ma_buf,
    mb_send,
    mb_buf,
    gh_send,
    gh_buf,
    fg_send,
    fg_buf,
    dg_send,
    dg_buf,
    dg_rows,
    sa_buf,
    sb_buf,
    e1_buf,
    e2_send,
    e2_buf,
    xp_send,
    xp_buf,
    fo_send,
    fo_buf,
    gg_send,
    gg_buf,
    sel,
    sel_own,
    onehot,
    ext_rows,
    picked,
    d_picked,
    basis_buf,
    slope_buf,
    dist_buf,
    ddist_buf,
    offset_buf,
    msg,
    dmsg,
    drows,
    hidden,
    pre_buf,
    normed_buf,
    inv_buf,
    mix_t,
    update_t,
    readout_t,
    radial_t,
    wave_buf,
    wave_t,
    r_buf,
    cos_buf,
    sin_buf,
    send_sem,
    recv_sem,
    load_sem,
):
    bead = lax.axis_index("bead")
    dom = lax.axis_index("dom")
    z, x, core = bead // 8, (bead // 2) % 4, bead % 2
    y, low = dom // 2, dom % 2
    ring = 2 * y + core

    def dev(z_, x_, y_, low_, core_):
        return ((z_ * 4 + x_) * 2 + core_, y_ * 2 + low_)

    def ring_dev(z_, step):
        place = (ring + step) % 8
        return dev(z_, x, place // 2, low, place % 2)

    def swapped_ring_dev(step):
        place = (ring + step) % 8
        return dev(z, x, place // 2, place % 2, low)

    def copy(src, dst, send_at, recv_at, target):
        return pltpu.make_async_remote_copy(
            src_ref=src,
            dst_ref=dst,
            send_sem=send_sem.at[send_at],
            recv_sem=recv_sem.at[recv_at],
            device_id=target,
            device_id_type=MESH,
        )

    def arrive(dst, recv_at):
        copy(dst, dst, 0, recv_at, dev(z, x, y, low, 1 - core)).wait_recv()

    started = []

    def send_to(src, dst, send_at, recv_at, target):
        sent = copy(src, dst, send_at, recv_at, target)
        sent.start()
        started.append(sent)

    k_first = pl.multiple_of((bead - core + low) * KPART, KPART)
    loads = {}
    for number, (src, dst) in enumerate(
        (
            (pos_in, pos),
            (mom_in, mom),
            (force_in, force),
            (mass_in, mass),
            (charge_in, charge),
            (neigh_in, neigh),
            (send_in, send),
            (coef_in, coef),
            (radial_in, radial),
            (mix_in, mix),
            (update_in, update),
            (readout_in, readout),
            (ew_in, ew),
            (wave_in.at[:, pl.ds(k_first, KPART)], wave),
        )
    ):
        loads[number] = pltpu.make_async_copy(src, dst, load_sem.at[number])
        if number < 7:
            loads[number].start()

    same = low == core
    conditional = []

    def send_or_keep(src, dst, send_at, recv_at, target):
        sent = copy(src, dst, send_at, recv_at, target)

        @pl.when(same)
        def _():
            pltpu.make_async_copy(src, dst, recv_sem.at[recv_at]).start()

        @pl.when(jnp.logical_not(same))
        def _():
            sent.start()

        conditional.append(sent)

    barrier = pltpu.get_barrier_semaphore()

    def greet(target):
        pl.semaphore_signal(barrier, inc=1, device_id=target, device_id_type=MESH)

    far = dev((z + 3 + 2 * low) % 4, x, y, 1 - low, low)
    for dz in (2, 1, 3):
        greet(dev((z + dz) % 4, x, y, core, core))
    greet(ring_dev(z, 4))

    @pl.when(same)
    def _():
        for dx, flip in ((2, 1), (2, 0), (1, 1), (3, 1), (1, 0), (3, 0), (0, 1)):
            greet(dev(z, (x + dx) % 4, y, core, (low + flip) % 2))

    @pl.when(jnp.logical_not(same))
    def _():
        greet(far)
        greet(dev(z, x, y, core, core))

    greet(ring_dev(z, 7 - 6 * core))
    greet(ring_dev(z, 1 + 6 * core))

    for number in range(7, 14):
        loads[number].start()

    for number in range(7):
        loads[number].wait()
    v_own[...] = jnp.zeros((8, ATOMS), F32)
    for c in range(3):
        v_own[c : c + 1, :] = pos[c]
        v_own[4 + c : 5 + c, :] = mom[c] + (0.5 * DT) * force[c]
    lane = lanes_of((1, 2 * SIDE))
    rows384 = jnp.concatenate(
        [send[0:1, :], send[1:2, :], send[2:3, :], jnp.zeros((1, 128), jnp.int32)], 1
    )
    shifted = pltpu.roll(rows384, 64, 1)
    spread = jnp.where(
        lane < GHOST,
        rows384,
        jnp.where(jnp.logical_and(lane >= SIDE, lane < SIDE + GHOST), shifted, -1),
    ).astype(F32)
    table = neigh[...]
    pack_own[0:8, :] = jnp.where(table >= ATOMS + GHOST, table + (SIDE - GHOST), table).astype(F32)
    pack_own[8:9, :] = mass[...]
    pack_own[9:10, :] = charge[...]
    pack_own[10:11, :] = spread
    pack_own[11:16, :] = jnp.zeros((5, ATOMS), F32)
    pl.semaphore_wait(barrier, jnp.where(same, 13, 8))

    slot = x * 2 + core
    for dx in (2, 1, 3):
        send_to(v_own, v_all.at[slot], S1 + dx, S1 + slot, dev(z, (x + dx) % 4, y, low, low))
    send_or_keep(v_own, v_all.at[slot], S1, S1 + slot, dev(z, x, y, low, low))
    swap = dev(z, x, y, core, low)
    send_or_keep(pack_own, pack_buf, PACK, PACK, far)
    send_or_keep(emb, emb_buf, EMB, EMB, far)

    for number in range(7, 14):
        loads[number].wait()

    eye = (rows_of((FEAT, FEAT)) == lanes_of((FEAT, FEAT))).astype(F32)
    eye_b = eye.astype(BF16)
    for layer in range(2):
        mix_t[layer] = dot_t(eye_b, mix[layer]).astype(BF16)
        update_t[layer] = dot_t(eye_b, update[layer]).astype(BF16)
        radial_t[layer] = dot_t(eye_b, radial[layer]).astype(BF16)
    readout_t[...] = dot_t(eye_b, readout[...]).astype(BF16)
    ew_col = jnp.sum(eye * ew[...], axis=1, keepdims=True)
    own_spread = jnp.broadcast_to(spread, (ATOMS, 2 * SIDE))
    atom_rows = rows_of((ATOMS, 2 * SIDE)).astype(F32)
    sel_own[...] = jnp.where(own_spread == atom_rows, 1.0, 0.0).astype(BF16)
    triple = wave[...].astype(F32)
    wave_buf[...] = jnp.zeros((16, KPART), F32)
    for part in range(3):
        wave_buf[4 * part : 4 * part + 3, :] = triple
    wave_t[...] = jnp.transpose(wave_buf[...]).astype(BF16)

    arrive(pack_buf, PACK)
    charges = pack_buf[9:10, :]
    send_row = pack_buf[10:11, :]
    sel[...] = jnp.where(jnp.broadcast_to(send_row, (ATOMS, 2 * SIDE)) == atom_rows, 1.0, 0.0).astype(BF16)
    send_index = jnp.broadcast_to(send_row, (8, 2 * SIDE)).astype(jnp.int32)

    def finish_sends(always, if_apart):
        for sent in always:
            sent.wait_send()
        always.clear()

        @pl.when(jnp.logical_not(same))
        def _():
            for sent in if_apart:
                sent.wait_send()

        if_apart.clear()

    row8 = rows_of((8, ATOMS))
    targets = [(2, 0), (2, 1), (1, 0), (3, 0), (1, 1), (3, 1), (0, 1), (0, 0)]

    def sums_copy(number, src, dst, first_sem):
        target = dev((z + number // 2) % 4, x, y, (low + number % 2) % 2, core)
        return copy(src.at[number], dst.at[z], first_sem + number, first_sem + z, target)

    @pl.when(same)
    def _():
        for k in range(8):
            arrive(v_all.at[k], S1 + k)
        upper = row8 < 4
        inv_mass = 1.0 / mass[...]
        scale = jnp.where(upper, inv_mass, -mass[...])
        beads_in = [v_all[k] for k in range(8)]
        total = beads_in[0]
        for k in range(1, 8):
            total = total + beads_in[k]
        centre_part = (total + DT * inv_mass * pltpu.roll(total, 4, 0)) * (1.0 / BEADS)
        centre_low = pltpu.roll(centre_part, 4, 0)
        first_row = rows_of((8, 1)) < 4
        for dz, flip in targets:
            z_to, low_to, number = (z + dz) % 4, (low + flip) % 2, 2 * dz + flip
            straight = None
            for k in range(8):
                shift = (8 * (z_to - z) + 2 * x + low_to - k + 64) % BEADS
                same_kind = coef[shift] * beads_in[k]
                other = jnp.where(first_row, coef[2 * BEADS + shift], coef[BEADS + shift]) * beads_in[k]
                straight = same_kind if k == 0 else straight + same_kind
                crossed = other if k == 0 else crossed + other
            moved = straight + scale * pltpu.roll(crossed, 4, 0)
            ma = jnp.where(upper, moved, centre_low)
            if number:
                ma_send[number] = ma
                mb_send[number] = moved[4:8]
                sums_copy(number, ma_send, ma_buf, MA).start()
            else:
                ma_buf[z] = ma
                mb_buf[z] = moved[4:8]

    def arrive_sums(buf, first_sem):
        @pl.when(jnp.logical_not(same))
        def _():
            arrive(buf.at[z], first_sem + z)

        for dz in (1, 3, 2):
            arrive(buf.at[(z + dz) % 4], first_sem + (z + dz) % 4)

    def pack_side(ref, value):
        ref[0:FEAT, :] = value[:, 0:128].astype(BF16)
        rest = jnp.concatenate([value[128:FEAT, 128:SIDE], jnp.zeros((256 - FEAT, 128), F32)], 0)
        ref[FEAT:PACKED, :] = (value[0:128, 128:SIDE] + pltpu.roll(rest, 64, 1)).astype(BF16)

    def unpack_side(ref, packed, first):
        ref[:, first : first + 128] = packed[0:FEAT, :]
        rest = packed[FEAT:PACKED, :].astype(F32)
        ref[0:128, first + 128 : first + SIDE] = rest.astype(BF16)
        ref[128:FEAT, first + 128 : first + SIDE] = pltpu.roll(rest, 64, 1)[0 : FEAT - 128].astype(BF16)

    def send_sides(src, dst, first_sem):
        for near in range(2):
            side = core if near == 0 else 1 - core
            send_to(
                src.at[side], dst.at[1 - side], first_sem + side, first_sem + 1 - side, ring_dev(z, 7 - 6 * side)
            )

    def send_features(layer, rounded):
        ghosts = dot(rounded, sel[...])
        for side in range(2):
            pack_side(fg_send.at[layer, side], ghosts[:, SIDE * side : SIDE * (side + 1)])
        send_sides(fg_send.at[layer], fg_buf.at[layer], FG + 2 * layer)

    def receive_features(layer):
        for side in range(2):
            arrive(fg_buf.at[layer, side], FG + 2 * layer + side)
            unpack_side(ext_rows, fg_buf.at[layer, side], ATOMS + SIDE * side)

    arrive(emb_buf, EMB)
    rounded = emb_buf[...]
    hidden[...] = rounded.astype(F32)
    ext_rows[:, :ATOMS] = rounded
    send_features(0, rounded)

    @pl.when(same)
    def _():
        for dz, flip in targets[:7]:
            sums_copy(2 * dz + flip, mb_send, mb_buf, MB).start()

    group_rows = [(rows_of((16, ATOMS)) + 16 * g).astype(F32) for g in range(8)]

    def build(j, carry):
        index = pack_buf[pl.ds(j, 1), :]
        at = pl.multiple_of(j * ATOMS, ATOMS)
        for block in range(EXT // 128):
            local = jnp.broadcast_to(index - 128.0 * block, (16, ATOMS))
            for g in range(8):
                first = 128 * block + 16 * g
                onehot[first : first + 16, pl.ds(at, ATOMS)] = jnp.where(
                    local == group_rows[g], 1.0, 0.0
                ).astype(BF16)
        return carry

    lax.fori_loop(0, NEIGH, build, 0)

    def gather_part(layer, first, last, fresh):
        def body(j, carry):
            at = pl.multiple_of(j * ATOMS, ATOMS)
            part = dot(ext_rows[:, first:last], onehot[first:last, pl.ds(at, ATOMS)])
            if not fresh:
                part = part + picked[layer, j].astype(F32)
            picked[layer, j] = part.astype(BF16)
            return carry

        lax.fori_loop(0, NEIGH, body, 0, unroll=True)

    gather_part(0, 0, ATOMS, True)

    arrive_sums(ma_buf, MA)
    moved = (ma_buf[0] + ma_buf[1]) + (ma_buf[2] + ma_buf[3])
    centre = moved[4:7]
    xp_send[...] = moved
    for c in range(3):
        blocks = [
            jnp.broadcast_to(moved[c : c + 1, 128 * n : 128 * n + 128], (8, 128)) for n in range(4)
        ]
        for n in range(4):
            got = lane_pick(blocks, send_index[:, 128 * n : 128 * n + 128])
            gh_send[n // 2, c : c + 1, 128 * (n % 2) : 128 * (n % 2) + 128] = got[0:1]
    gh_send[:, 3:4, :] = jnp.zeros((2, 1, SIDE), F32)
    send_sides(gh_send, gh_buf, GH)
    receive_features(0)
    gather_part(0, ATOMS, EXT, False)
    turns = centre * 0.25
    high = turns.astype(BF16).astype(F32)
    rest = turns - high
    middle = rest.astype(BF16).astype(F32)
    r_buf[...] = jnp.zeros((16, ATOMS), F32)
    for number, value in enumerate((high, middle, rest - middle)):
        r_buf[4 * number : 4 * number + 3, :] = value

    def ewald_sums():
        phase = r_buf[...].astype(BF16)

        def body(i, carry):
            at = pl.multiple_of(i * 128, 128)
            turn = dot(wave_t[pl.ds(at, 128), :], phase)
            half = (turn - jnp.round(turn)) * math.pi
            q = half * half
            s = half * (
                1.0
                + q
                * (
                    -1.6666666641e-1
                    + q * (8.3333293858e-3 + q * (-1.9840083133e-4 + q * (2.7523971075e-6 - 2.3868346521e-8 * q)))
                )
            )
            c = 1.0 + q * (
                -0.5
                + q
                * (
                    4.1666666658e-2
                    + q
                    * (
                        -1.3888888388e-3
                        + q * (2.4801544910e-5 + q * (-2.7556993055e-7 + 2.0737354e-9 * q))
                    )
                )
            )
            sin_buf[pl.ds(at, 128), :] = (2.0 * s * c).astype(BF16)
            cos_buf[pl.ds(at, 128), :] = (1.0 - 2.0 * s * s).astype(BF16)
            return carry

        lax.fori_loop(0, KPART // 128, body, 0, unroll=True)
        weights = stacked_parts(jnp.broadcast_to(charges, (8, ATOMS)))
        for number, ref in enumerate((cos_buf, sin_buf)):
            sums = dot_t(weights, ref[...])
            sa_buf[core, number : number + 1, :] = sums[0:1] + sums[8:9]
        send_to(sa_buf.at[core], sa_buf.at[core], SA, SA, dev(z, x, y, low, 1 - core))

    def ewald_ring():
        arrive(sa_buf.at[1 - core], SA)
        sb_buf[y] = sa_buf[0] + sa_buf[1]
        for dy in range(1, 4):
            send_to(sb_buf.at[y], sb_buf.at[y], SB + dy, SB + y, dev(z, x, (y + dy) % 4, low, core))

    ghosts_at = []
    for side in range(2):
        arrive(gh_buf.at[side], GH + side)
        ghosts_at.append(gh_buf[side])
    index8 = pack_buf[0:8, :].astype(jnp.int32)
    distance = None
    for c in range(3):
        blocks = [moved[c : c + 1, 128 * n : 128 * n + 128] for n in range(4)]
        for side in range(2):
            blocks += [ghosts_at[side][c : c + 1, 128 * n : 128 * n + 128] for n in range(2)]
        blocks = [jnp.broadcast_to(block, (8, 128)) for block in blocks]
        others = jnp.concatenate(
            [lane_pick(blocks, index8[:, 128 * n : 128 * n + 128]) for n in range(4)], 1
        )
        offset = others - moved[c : c + 1, :]
        offset_buf[c] = offset
        distance = offset * offset if c == 0 else distance + offset * offset
    dist_buf[...] = distance
    m_row = rows_of((BASIS, ATOMS))
    rates = jnp.where(m_row % 2 == 1, 0.125 * math.sqrt(2.0), 0.125) * jnp.left_shift(1, m_row // 2).astype(F32)
    for j in range(NEIGH):
        exact = 1.0 / (1.0 + rates * dist_buf[j : j + 1, :])
        basis_buf[j] = exact.astype(BF16)
        slope_buf[j] = -rates * exact * exact

    def ewald_forces():
        for dy in range(1, 4):
            arrive(sb_buf.at[(y + dy) % 4], SB + (y + dy) % 4)
        sums = (sb_buf[0] + sb_buf[1]) + (sb_buf[2] + sb_buf[3])
        recip = wave_buf[0:8, :] * (TWO_PI / 4.0)
        recip = jnp.where(row8 < 3, recip, 0.0)
        square = jnp.sum(recip * recip, axis=0, keepdims=True)
        damping = 48.0 / math.sqrt(KVEC * TOTAL_ATOMS) * jnp.exp(-0.002 * square) / square
        from_sin = stacked_parts(recip * (damping * sums[0:1]))
        from_cos = stacked_parts(recip * (damping * sums[1:2]))
        part = dot(from_sin, sin_buf[...]) - dot(from_cos, cos_buf[...])
        part = 2.0 * charges * (part[0:8] + part[8:16])
        e1_buf[x] = part[0:4]
        for dx in (2, 1, 3):
            send_to(e1_buf.at[x], e1_buf.at[x], E1 + dx, E1 + x, dev(z, (x + dx) % 4, y, low, core))

    def ewald_group_sum():
        for dx in (1, 3, 2):
            arrive(e1_buf.at[(x + dx) % 4], E1 + (x + dx) % 4)
        e2_send[...] = (e1_buf[0] + e1_buf[1]) + (e1_buf[2] + e1_buf[3])
        place = 2 * z + low
        for dz in (2, 1, 3, 0):
            for flip in (1, 0):
                if dz or flip:
                    send_to(
                        e2_send,
                        e2_buf.at[place],
                        E2 + 2 * dz + flip,
                        E2 + place,
                        dev((z + dz) % 4, x, y, core, (low + flip) % 2),
                    )
        send_or_keep(e2_send, e2_buf.at[place], E2, E2 + place, swap)

    def finish_layer(layer):
        msg[...] = jnp.zeros((FEAT, ATOMS), F32)

        def body(j, carry):
            edge = dot(radial_t[layer], basis_buf[j])
            msg[...] += edge * picked[layer, j].astype(F32)
            return carry

        lax.fori_loop(0, NEIGH, body, 0, unroll=True)
        message = msg[...]
        inverse = lax.rsqrt(jnp.sum(message * message, axis=0, keepdims=True) * (1.0 / FEAT) + 1e-6)
        normed = message * inverse
        normed_buf[layer] = normed
        inv_buf[layer] = jnp.broadcast_to(inverse, (8, ATOMS))
        pre = dot(mix_t[layer], normed.astype(BF16))
        pre_buf[layer] = pre
        gated = (pre * lax.logistic(pre)).astype(BF16)
        hidden[...] += dot(update_t[layer], gated)

    finish_layer(0)
    rounded = hidden[...].astype(BF16)
    ext_rows[:, :ATOMS] = rounded
    send_features(1, rounded)
    ewald_sums()
    gather_part(1, 0, ATOMS, True)
    ewald_ring()
    arrive_sums(mb_buf, MB)
    xp_send[4:8, :] = (mb_buf[0] + mb_buf[1]) + (mb_buf[2] + mb_buf[3])
    send_or_keep(xp_send, xp_buf, XP, XP, swap)
    receive_features(1)
    gather_part(1, ATOMS, EXT, False)
    finish_layer(1)

    def silu_slope(pre):
        sig = lax.logistic(pre)
        return sig * (1.0 + pre * (1.0 - sig))

    final = dot(readout_t[...], hidden[...].astype(BF16))
    dfinal = ew_col * silu_slope(final)
    cotan = dot(readout[...], dfinal.astype(BF16)).astype(BF16)

    def message_cotan(layer, cotan_b):
        dgated = dot(update[layer], cotan_b).astype(BF16).astype(F32)
        dpre = dgated * silu_slope(pre_buf[layer])
        dnormed = dot(mix[layer], dpre.astype(BF16)).astype(BF16).astype(F32)
        normed = normed_buf[layer]
        mean = jnp.sum(dnormed * normed, axis=0, keepdims=True) * (1.0 / FEAT)
        dmsg[...] = inv_buf[layer, 0:1, :] * (dnormed - normed * mean)

    def distance_cotan(layer):
        def body(j, carry):
            dedge = (picked[layer, j].astype(F32) * dmsg[...]).astype(BF16)
            dbasis = dot(radial[layer], dedge).astype(BF16).astype(F32)
            part = jnp.sum(dbasis * slope_buf[j], axis=0, keepdims=True)
            if layer == 1:
                ddist_buf[pl.ds(j, 1), :] = part
            else:
                ddist_buf[pl.ds(j, 1), :] += part
            return carry

        lax.fori_loop(0, NEIGH, body, 0, unroll=True)

    message_cotan(1, cotan)

    def row_cotan(j, carry):
        at = pl.multiple_of(j * ATOMS, ATOMS)
        edge = dot(radial_t[1], basis_buf[j])
        d_picked[:, pl.ds(at, ATOMS)] = (edge * dmsg[...]).astype(BF16)
        return carry

    lax.fori_loop(0, NEIGH, row_cotan, 0, unroll=True)
    for near in range(2):
        side = core if near == 0 else 1 - core
        first = pl.multiple_of(ATOMS + SIDE * side, SIDE)
        pack_side(dg_send.at[side], dot_t(d_picked[...], onehot[pl.ds(first, SIDE), :]))
        send_to(dg_send.at[side], dg_buf.at[1 - side], DG + side, DG + 1 - side, ring_dev(z, 7 - 6 * side))
    ewald_forces()
    for half in range(2):
        drows[:, SIDE * half : SIDE * half + SIDE] = dot_t(
            d_picked[...], onehot[SIDE * half : SIDE * half + SIDE, :]
        )
    distance_cotan(1)
    for near in (1, 0):
        side = core if near == 0 else 1 - core
        arrive(dg_buf.at[side], DG + side)
    for side in range(2):
        unpack_side(dg_rows, dg_buf.at[side], SIDE * side)
    returned = dot_t(dg_rows[...], sel[...])
    owned = (drows[...] + returned).astype(BF16).astype(F32)
    message_cotan(0, (cotan.astype(F32) + owned).astype(BF16))
    distance_cotan(0)
    early, early_apart = list(started), list(conditional)
    started.clear()
    conditional.clear()
    ewald_group_sum()

    ddist = 2.0 * ddist_buf[...]
    edge_force = [offset_buf[c] * ddist for c in range(3)]
    for c in range(3):
        own = jnp.sum(edge_force[c], axis=0, keepdims=True)
        fo_send[c : c + 1, :] = own
    fo_send[3:4, :] = jnp.zeros((1, ATOMS), F32)

    parts = []
    zero_row = jnp.zeros((1, ATOMS), F32)
    for j in range(NEIGH):
        rows = [edge_force[c][j : j + 1, :] for c in range(3)] + [zero_row] * 5
        parts.append(stacked_parts(jnp.concatenate(rows, 0)))
    force_rows = jnp.concatenate(parts, 1)
    for near in range(2):
        side = core if near == 0 else 1 - core
        first = pl.multiple_of(ATOMS + SIDE * side, SIDE)
        both = dot_t(force_rows, onehot[pl.ds(first, SIDE), :])
        gg_send[side] = both[0:4] + both[8:12]
        send_to(
            gg_send.at[side], gg_buf.at[1 - side], GG + side, GG + 1 - side, swapped_ring_dev(7 - 6 * side)
        )
    both = dot_t(force_rows, onehot[:ATOMS, :])
    fo_send[...] = fo_send[...] - (both[0:4] + both[8:12])
    send_or_keep(fo_send, fo_buf, FO, FO, swap)

    finish_sends(early, early_apart)

    @pl.when(same)
    def _():
        for dz, flip in targets[:7]:
            sums_copy(2 * dz + flip, ma_send, ma_buf, MA).wait_send()
            sums_copy(2 * dz + flip, mb_send, mb_buf, MB).wait_send()

    arrive(xp_buf, XP)
    for side in range(2):
        arrive(gg_buf.at[side], GG + side)
    zero4 = jnp.zeros((4, SIDE), F32)
    returned = None
    for side in range(2):
        rows = stacked_parts(jnp.concatenate([gg_buf[side], zero4], 0))
        both = dot_t(rows, sel_own[:, SIDE * side : SIDE * side + SIDE])
        both = both[0:4] + both[8:12]
        returned = both if side == 0 else returned + both
    arrive(fo_buf, FO)
    for place in range(8):
        arrive(e2_buf.at[place], E2 + place)
    long_range = e2_buf[0]
    for place in range(1, 8):
        long_range = long_range + e2_buf[place]
    result = (fo_buf[...] - returned) + long_range
    for c in range(3):
        out[c] = xp_buf[c : c + 1, :]
        out[3 + c] = xp_buf[4 + c : 5 + c, :] + (0.5 * DT) * result[c : c + 1, :]
        out[6 + c] = result[c : c + 1, :]

    finish_sends(started, conditional)


def local(
    positions,
    momenta,
    forces,
    masses,
    charges,
    embedding,
    neighbours,
    send_rows,
    wavevectors,
    radial_weight,
    mix_weight,
    update_weight,
    readout_weight,
    energy_weight,
):
    piece = (3, 1, ATOMS)
    scratch = [
        (piece, F32),
        (piece, F32),
        (piece, F32),
        ((1, ATOMS), F32),
        ((1, ATOMS), F32),
        ((NEIGH, ATOMS), jnp.int32),
        ((3, 128), jnp.int32),
        ((3, KPART), jnp.int32),
        ((2, BASIS, FEAT), BF16),
        ((2, FEAT, FEAT), BF16),
        ((2, FEAT, FEAT), BF16),
        ((FEAT, FEAT), BF16),
        ((1, FEAT), F32),
        ((8, ATOMS), F32),
        ((8, 8, ATOMS), F32),
        ((FEAT, ATOMS), BF16),
        ((16, ATOMS), F32),
        ((16, ATOMS), F32),
        ((8, 8, ATOMS), F32),
        ((4, 8, ATOMS), F32),
        ((8, 4, ATOMS), F32),
        ((4, 4, ATOMS), F32),
        ((2, 4, SIDE), F32),
        ((2, 4, SIDE), F32),
        ((2, 2, PACKED, 128), BF16),
        ((2, 2, PACKED, 128), BF16),
        ((2, PACKED, 128), BF16),
        ((2, PACKED, 128), BF16),
        ((FEAT, 2 * SIDE), BF16),
        ((2, 2, KPART), F32),
        ((4, 2, KPART), F32),
        ((4, 4, ATOMS), F32),
        ((4, ATOMS), F32),
        ((8, 4, ATOMS), F32),
        ((8, ATOMS), F32),
        ((8, ATOMS), F32),
        ((4, ATOMS), F32),
        ((4, ATOMS), F32),
        ((2, 4, SIDE), F32),
        ((2, 4, SIDE), F32),
        ((ATOMS, 2 * SIDE), BF16),
        ((ATOMS, 2 * SIDE), BF16),
        ((EXT, NEIGH * ATOMS), BF16),
        ((FEAT, EXT), BF16),
        ((2, NEIGH, FEAT, ATOMS), BF16),
        ((FEAT, NEIGH * ATOMS), BF16),
        ((NEIGH, BASIS, ATOMS), BF16),
        ((NEIGH, BASIS, ATOMS), F32),
        ((NEIGH, ATOMS), F32),
        ((NEIGH, ATOMS), F32),
        ((3, NEIGH, ATOMS), F32),
        ((FEAT, ATOMS), F32),
        ((FEAT, ATOMS), F32),
        ((FEAT, ATOMS), F32),
        ((FEAT, ATOMS), F32),
        ((2, FEAT, ATOMS), F32),
        ((2, FEAT, ATOMS), F32),
        ((2, 8, ATOMS), F32),
        ((2, FEAT, FEAT), BF16),
        ((2, FEAT, FEAT), BF16),
        ((FEAT, FEAT), BF16),
        ((2, FEAT, BASIS), BF16),
        ((16, KPART), F32),
        ((KPART, 16), BF16),
        ((16, ATOMS), F32),
        ((KPART, ATOMS), BF16),
        ((KPART, ATOMS), BF16),
    ]
    out = pl.pallas_call(
        step_kernel,
        out_shape=jax.ShapeDtypeStruct((9, 1, ATOMS), F32),
        in_specs=[pl.BlockSpec(memory_space=pltpu.HBM)] * 15,
        out_specs=pl.BlockSpec(memory_space=pltpu.VMEM),
        scratch_shapes=[pltpu.SMEM((3 * BEADS,), F32)]
        + [pltpu.VMEM(shape, kind) for shape, kind in scratch]
        + [
            pltpu.SemaphoreType.DMA((N_SEMS,)),
            pltpu.SemaphoreType.DMA((N_SEMS,)),
            pltpu.SemaphoreType.DMA((14,)),
        ],
        compiler_params=pltpu.CompilerParams(
            collective_id=0, has_side_effects=True, vmem_limit_bytes=60 * 1024 * 1024
        ),
        cost_estimate=pl.CostEstimate(flops=16_000_000_000, bytes_accessed=2_000_000, transcendentals=1_000_000),
    )(
        jnp.asarray(ring_tables()),
        positions,
        momenta,
        forces,
        masses.reshape(1, ATOMS),
        charges.reshape(1, ATOMS),
        embedding.T,
        neighbours,
        send_rows.reshape(3, 128),
        wavevectors,
        radial_weight,
        mix_weight,
        update_weight,
        readout_weight,
        energy_weight.reshape(1, FEAT),
    )
    return out[0:3], out[3:6], out[6:9]


def solution(mesh):
    own = P(None, "bead", "dom")
    placed = (
        own,
        own,
        own,
        P("dom"),
        P("dom"),
        P("dom", None),
        P(None, "dom"),
        P("dom"),
        P(),
        P(),
        P(),
        P(),
        P(),
        P(),
    )
    return jax.shard_map(local, mesh=mesh, in_specs=placed, out_specs=(own, own, own), check_vma=False)
```

```python
import math

import jax
import jax.numpy as jnp
import numpy as np
from jax import lax
from jax.experimental import pallas as pl
from jax.experimental.pallas import tpu as pltpu
from jax.sharding import PartitionSpec as P

MESH = pl.DeviceIdType.MESH
F32 = jnp.float32
BF16 = jnp.bfloat16

BEADS = 32
ATOMS = 512
TOTAL_ATOMS = 4096
GHOST = 192
SIDE = 256
EXT = ATOMS + 2 * SIDE
NEIGH = 8
FEAT = 240
BASIS = 16
KVEC = 16384
KPART = KVEC // BEADS
DT = 0.25
TWO_PI = 2.0 * math.pi
PACKED = FEAT + 128

S1, EMB, PACK, MA, MB, GH, FG, DG, SA, SB, E1, E2, XP, FO, GG, N_SEMS = np.cumsum(
    [0, 8, 1, 1, 8, 8, 2, 4, 2, 1, 4, 4, 8, 1, 1, 2]
).tolist()


def ring_tables():
    k = np.arange(BEADS)
    b = np.arange(BEADS)[:, None]
    angle = 2.0 * np.pi / BEADS * (b * k % BEADS)
    half = BEADS // 2
    basis = np.where(k < half, np.cos(angle), np.sin(angle)) * math.sqrt(2.0 / BEADS)
    basis = np.where(k == 0, math.sqrt(1.0 / BEADS), basis)
    basis = np.where(k == half, math.sqrt(1.0 / BEADS) * (1 - 2 * (b % 2)), basis)
    omega = 3.2 * np.sin(np.pi * k / BEADS)
    cosine, sine = np.cos(omega * DT), np.sin(omega * DT)
    drift = np.where(k == 0, DT, sine / np.where(k == 0, 1.0, omega))
    rows = [(basis * value) @ basis.T for value in (cosine, drift, omega * sine)]
    return np.concatenate([row[0] for row in rows]).astype(np.float32)


def dot(a, b):
    return lax.dot_general(a, b, (((1,), (0,)), ((), ())), preferred_element_type=F32)


def dot_t(a, b):
    return lax.dot_general(a, b, (((1,), (1,)), ((), ())), preferred_element_type=F32)


def rows_of(shape):
    return lax.broadcasted_iota(jnp.int32, shape, 0)


def lanes_of(shape):
    return lax.broadcasted_iota(jnp.int32, shape, 1)


def two_parts(value):
    high = value.astype(BF16)
    return high, (value - high.astype(F32)).astype(BF16)


def stacked_parts(value):
    high = value.astype(BF16).astype(F32)
    return jnp.concatenate([high, value - high], 0).astype(BF16)


def lane_pick(tables, index):
    result = None
    for number, block in enumerate(tables):
        local = index - 128 * number
        inside = jnp.logical_and(local >= 0, local < 128)
        got = jnp.take_along_axis(block, jnp.where(inside, local, 0), axis=1, mode="promise_in_bounds")
        result = jnp.where(inside, got, 0.0 if result is None else result)
    return result


def step_kernel(
    coef_in,
    pos_in,
    mom_in,
    force_in,
    mass_in,
    charge_in,
    emb,
    neigh_in,
    send_in,
    wave_in,
    radial_in,
    mix_in,
    update_in,
    readout_in,
    ew_in,
    out,
    coef,
    pos,
    mom,
    force,
    mass,
    charge,
    neigh,
    send,
    wave,
    radial,
    mix,
    update,
    readout,
    ew,
    v_own,
    v_all,
    emb_buf,
    pack_own,
    pack_buf,
    ma_send,
    ma_buf,
    mb_send,
    mb_buf,
    gh_send,
    gh_buf,
    fg_send,
    fg_buf,
    dg_send,
    dg_buf,
    dg_rows,
    sa_buf,
    sb_buf,
    e1_buf,
    e2_send,
    e2_buf,
    xp_send,
    xp_buf,
    fo_send,
    fo_buf,
    gg_send,
    gg_buf,
    sel,
    sel_own,
    onehot,
    ext_rows,
    picked,
    d_picked,
    basis_buf,
    slope_buf,
    dist_buf,
    ddist_buf,
    offset_buf,
    msg,
    dmsg,
    drows,
    hidden,
    pre_buf,
    normed_buf,
    inv_buf,
    mix_t,
    update_t,
    readout_t,
    radial_t,
    wave_buf,
    wave_t,
    r_buf,
    cos_buf,
    sin_buf,
    send_sem,
    recv_sem,
    load_sem,
):
    bead = lax.axis_index("bead")
    dom = lax.axis_index("dom")
    z, x, core = bead // 8, (bead // 2) % 4, bead % 2
    y, low = dom // 2, dom % 2
    ring = 2 * y + core

    def dev(z_, x_, y_, low_, core_):
        return ((z_ * 4 + x_) * 2 + core_, y_ * 2 + low_)

    def ring_dev(z_, step):
        place = (ring + step) % 8
        return dev(z_, x, place // 2, low, place % 2)

    def swapped_ring_dev(step):
        place = (ring + step) % 8
        return dev(z, x, place // 2, place % 2, low)

    def copy(src, dst, send_at, recv_at, target):
        return pltpu.make_async_remote_copy(
            src_ref=src,
            dst_ref=dst,
            send_sem=send_sem.at[send_at],
            recv_sem=recv_sem.at[recv_at],
            device_id=target,
            device_id_type=MESH,
        )

    def arrive(dst, recv_at):
        copy(dst, dst, 0, recv_at, dev(z, x, y, low, 1 - core)).wait_recv()

    started = []

    def send_to(src, dst, send_at, recv_at, target):
        sent = copy(src, dst, send_at, recv_at, target)
        sent.start()
        started.append(sent)

    k_first = pl.multiple_of((bead - core + low) * KPART, KPART)
    loads = {}
    for number, (src, dst) in enumerate(
        (
            (pos_in, pos),
            (mom_in, mom),
            (force_in, force),
            (mass_in, mass),
            (charge_in, charge),
            (neigh_in, neigh),
            (send_in, send),
            (coef_in, coef),
            (radial_in, radial),
            (mix_in, mix),
            (update_in, update),
            (readout_in, readout),
            (ew_in, ew),
            (wave_in.at[:, pl.ds(k_first, KPART)], wave),
        )
    ):
        loads[number] = pltpu.make_async_copy(src, dst, load_sem.at[number])
        if number < 7:
            loads[number].start()

    same = low == core
    conditional = []

    def send_or_keep(src, dst, send_at, recv_at, target):
        sent = copy(src, dst, send_at, recv_at, target)

        @pl.when(same)
        def _():
            pltpu.make_async_copy(src, dst, recv_sem.at[recv_at]).start()

        @pl.when(jnp.logical_not(same))
        def _():
            sent.start()

        conditional.append(sent)

    barrier = pltpu.get_barrier_semaphore()

    def greet(target):
        pl.semaphore_signal(barrier, inc=1, device_id=target, device_id_type=MESH)

    far = dev((z + 3 + 2 * low) % 4, x, y, 1 - low, low)
    for dz in (2, 1, 3):
        greet(dev((z + dz) % 4, x, y, core, core))
    greet(ring_dev(z, 4))

    @pl.when(same)
    def _():
        for dx, flip in ((2, 1), (2, 0), (1, 1), (3, 1), (1, 0), (3, 0), (0, 1)):
            greet(dev(z, (x + dx) % 4, y, core, (low + flip) % 2))

    @pl.when(jnp.logical_not(same))
    def _():
        greet(far)
        greet(dev(z, x, y, core, core))

    greet(ring_dev(z, 7 - 6 * core))
    greet(ring_dev(z, 1 + 6 * core))

    for number in range(7, 14):
        loads[number].start()

    for number in range(7):
        loads[number].wait()
    v_own[...] = jnp.zeros((8, ATOMS), F32)
    for c in range(3):
        v_own[c : c + 1, :] = pos[c]
        v_own[4 + c : 5 + c, :] = mom[c] + (0.5 * DT) * force[c]
    lane = lanes_of((1, 2 * SIDE))
    rows384 = jnp.concatenate(
        [send[0:1, :], send[1:2, :], send[2:3, :], jnp.zeros((1, 128), jnp.int32)], 1
    )
    shifted = pltpu.roll(rows384, 64, 1)
    spread = jnp.where(
        lane < GHOST,
        rows384,
        jnp.where(jnp.logical_and(lane >= SIDE, lane < SIDE + GHOST), shifted, -1),
    ).astype(F32)
    table = neigh[...]
    pack_own[0:8, :] = jnp.where(table >= ATOMS + GHOST, table + (SIDE - GHOST), table).astype(F32)
    pack_own[8:9, :] = mass[...]
    pack_own[9:10, :] = charge[...]
    pack_own[10:11, :] = spread
    pack_own[11:16, :] = jnp.zeros((5, ATOMS), F32)
    pl.semaphore_wait(barrier, jnp.where(same, 13, 8))

    slot = x * 2 + core
    for dx in (2, 1, 3):
        send_to(v_own, v_all.at[slot], S1 + dx, S1 + slot, dev(z, (x + dx) % 4, y, low, low))
    send_or_keep(v_own, v_all.at[slot], S1, S1 + slot, dev(z, x, y, low, low))
    swap = dev(z, x, y, core, low)
    send_or_keep(pack_own, pack_buf, PACK, PACK, far)
    send_or_keep(emb, emb_buf, EMB, EMB, far)

    for number in range(7, 14):
        loads[number].wait()

    eye = (rows_of((FEAT, FEAT)) == lanes_of((FEAT, FEAT))).astype(F32)
    eye_b = eye.astype(BF16)
    for layer in range(2):
        mix_t[layer] = dot_t(eye_b, mix[layer]).astype(BF16)
        update_t[layer] = dot_t(eye_b, update[layer]).astype(BF16)
        radial_t[layer] = dot_t(eye_b, radial[layer]).astype(BF16)
    readout_t[...] = dot_t(eye_b, readout[...]).astype(BF16)
    ew_col = jnp.sum(eye * ew[...], axis=1, keepdims=True)
    own_spread = jnp.broadcast_to(spread, (ATOMS, 2 * SIDE))
    atom_rows = rows_of((ATOMS, 2 * SIDE)).astype(F32)
    sel_own[...] = jnp.where(own_spread == atom_rows, 1.0, 0.0).astype(BF16)
    triple = wave[...].astype(F32)
    wave_buf[...] = jnp.zeros((16, KPART), F32)
    for part in range(3):
        wave_buf[4 * part : 4 * part + 3, :] = triple
    wave_t[...] = jnp.transpose(wave_buf[...]).astype(BF16)

    arrive(pack_buf, PACK)
    charges = pack_buf[9:10, :]
    send_row = pack_buf[10:11, :]
    sel[...] = jnp.where(jnp.broadcast_to(send_row, (ATOMS, 2 * SIDE)) == atom_rows, 1.0, 0.0).astype(BF16)
    send_index = jnp.broadcast_to(send_row, (8, 2 * SIDE)).astype(jnp.int32)

    row8 = rows_of((8, ATOMS))
    targets = [(2, 0), (2, 1), (1, 0), (3, 0), (1, 1), (3, 1), (0, 1), (0, 0)]

    def sums_copy(number, src, dst, first_sem):
        target = dev((z + number // 2) % 4, x, y, (low + number % 2) % 2, core)
        return copy(src.at[number], dst.at[z], first_sem + number, first_sem + z, target)

    @pl.when(same)
    def _():
        for k in range(8):
            arrive(v_all.at[k], S1 + k)
        upper = row8 < 4
        inv_mass = 1.0 / mass[...]
        scale = jnp.where(upper, inv_mass, -mass[...])
        beads_in = [v_all[k] for k in range(8)]
        total = beads_in[0]
        for k in range(1, 8):
            total = total + beads_in[k]
        centre_part = (total + DT * inv_mass * pltpu.roll(total, 4, 0)) * (1.0 / BEADS)
        centre_low = pltpu.roll(centre_part, 4, 0)
        first_row = rows_of((8, 1)) < 4
        for dz, flip in targets:
            z_to, low_to, number = (z + dz) % 4, (low + flip) % 2, 2 * dz + flip
            straight = None
            for k in range(8):
                shift = (8 * (z_to - z) + 2 * x + low_to - k + 64) % BEADS
                same_kind = coef[shift] * beads_in[k]
                other = jnp.where(first_row, coef[2 * BEADS + shift], coef[BEADS + shift]) * beads_in[k]
                straight = same_kind if k == 0 else straight + same_kind
                crossed = other if k == 0 else crossed + other
            moved = straight + scale * pltpu.roll(crossed, 4, 0)
            ma = jnp.where(upper, moved, centre_low)
            if number:
                ma_send[number] = ma
                mb_send[number] = moved[4:8]
                sums_copy(number, ma_send, ma_buf, MA).start()
            else:
                ma_buf[z] = ma
                mb_buf[z] = moved[4:8]

    def arrive_sums(buf, first_sem):
        @pl.when(jnp.logical_not(same))
        def _():
            arrive(buf.at[z], first_sem + z)

        for dz in (1, 3, 2):
            arrive(buf.at[(z + dz) % 4], first_sem + (z + dz) % 4)

    def pack_side(ref, value):
        ref[0:FEAT, :] = value[:, 0:128].astype(BF16)
        rest = jnp.concatenate([value[128:FEAT, 128:SIDE], jnp.zeros((256 - FEAT, 128), F32)], 0)
        ref[FEAT:PACKED, :] = (value[0:128, 128:SIDE] + pltpu.roll(rest, 64, 1)).astype(BF16)

    def unpack_side(ref, packed, first):
        ref[:, first : first + 128] = packed[0:FEAT, :]
        rest = packed[FEAT:PACKED, :].astype(F32)
        ref[0:128, first + 128 : first + SIDE] = rest.astype(BF16)
        ref[128:FEAT, first + 128 : first + SIDE] = pltpu.roll(rest, 64, 1)[0 : FEAT - 128].astype(BF16)

    def send_sides(src, dst, first_sem):
        for near in range(2):
            side = core if near == 0 else 1 - core
            send_to(
                src.at[side], dst.at[1 - side], first_sem + side, first_sem + 1 - side, ring_dev(z, 7 - 6 * side)
            )

    def send_features(layer, rounded):
        ghosts = dot(rounded, sel[...])
        for side in range(2):
            pack_side(fg_send.at[layer, side], ghosts[:, SIDE * side : SIDE * (side + 1)])
        send_sides(fg_send.at[layer], fg_buf.at[layer], FG + 2 * layer)

    def receive_features(layer):
        for side in range(2):
            arrive(fg_buf.at[layer, side], FG + 2 * layer + side)
            unpack_side(ext_rows, fg_buf.at[layer, side], ATOMS + SIDE * side)

    arrive(emb_buf, EMB)
    rounded = emb_buf[...]
    hidden[...] = rounded.astype(F32)
    ext_rows[:, :ATOMS] = rounded
    send_features(0, rounded)

    @pl.when(same)
    def _():
        for dz, flip in targets[:7]:
            sums_copy(2 * dz + flip, mb_send, mb_buf, MB).start()

    group_rows = [(rows_of((16, ATOMS)) + 16 * g).astype(F32) for g in range(8)]

    def build(j, carry):
        index = pack_buf[pl.ds(j, 1), :]
        at = pl.multiple_of(j * ATOMS, ATOMS)
        for block in range(EXT // 128):
            local = jnp.broadcast_to(index - 128.0 * block, (16, ATOMS))
            for g in range(8):
                first = 128 * block + 16 * g
                onehot[first : first + 16, pl.ds(at, ATOMS)] = jnp.where(
                    local == group_rows[g], 1.0, 0.0
                ).astype(BF16)
        return carry

    lax.fori_loop(0, NEIGH, build, 0)

    def gather_part(layer, first, last, fresh):
        def body(j, carry):
            at = pl.multiple_of(j * ATOMS, ATOMS)
            part = dot(ext_rows[:, first:last], onehot[first:last, pl.ds(at, ATOMS)])
            if not fresh:
                part = part + picked[layer, j].astype(F32)
            picked[layer, j] = part.astype(BF16)
            return carry

        lax.fori_loop(0, NEIGH, body, 0, unroll=True)

    gather_part(0, 0, ATOMS, True)

    arrive_sums(ma_buf, MA)
    moved = (ma_buf[0] + ma_buf[1]) + (ma_buf[2] + ma_buf[3])
    centre = moved[4:7]
    xp_send[...] = moved
    for c in range(3):
        blocks = [
            jnp.broadcast_to(moved[c : c + 1, 128 * n : 128 * n + 128], (8, 128)) for n in range(4)
        ]
        for n in range(4):
            got = lane_pick(blocks, send_index[:, 128 * n : 128 * n + 128])
            gh_send[n // 2, c : c + 1, 128 * (n % 2) : 128 * (n % 2) + 128] = got[0:1]
    gh_send[:, 3:4, :] = jnp.zeros((2, 1, SIDE), F32)
    send_sides(gh_send, gh_buf, GH)
    receive_features(0)
    gather_part(0, ATOMS, EXT, False)
    turns = centre * 0.25
    high = turns.astype(BF16).astype(F32)
    rest = turns - high
    middle = rest.astype(BF16).astype(F32)
    r_buf[...] = jnp.zeros((16, ATOMS), F32)
    for number, value in enumerate((high, middle, rest - middle)):
        r_buf[4 * number : 4 * number + 3, :] = value

    def ewald_sums():
        phase = r_buf[...].astype(BF16)

        def body(i, carry):
            at = pl.multiple_of(i * 128, 128)
            turn = dot(wave_t[pl.ds(at, 128), :], phase)
            half = (turn - jnp.round(turn)) * math.pi
            q = half * half
            s = half * (
                1.0
                + q
                * (
                    -1.6666666641e-1
                    + q * (8.3333293858e-3 + q * (-1.9840083133e-4 + q * (2.7523971075e-6 - 2.3868346521e-8 * q)))
                )
            )
            c = 1.0 + q * (
                -0.5
                + q
                * (
                    4.1666666658e-2
                    + q
                    * (
                        -1.3888888388e-3
                        + q * (2.4801544910e-5 + q * (-2.7556993055e-7 + 2.0737354e-9 * q))
                    )
                )
            )
            sin_buf[pl.ds(at, 128), :] = (2.0 * s * c).astype(BF16)
            cos_buf[pl.ds(at, 128), :] = (1.0 - 2.0 * s * s).astype(BF16)
            return carry

        lax.fori_loop(0, KPART // 128, body, 0, unroll=True)
        weights = stacked_parts(jnp.broadcast_to(charges, (8, ATOMS)))
        for number, ref in enumerate((cos_buf, sin_buf)):
            sums = dot_t(weights, ref[...])
            sa_buf[core, number : number + 1, :] = sums[0:1] + sums[8:9]
        send_to(sa_buf.at[core], sa_buf.at[core], SA, SA, dev(z, x, y, low, 1 - core))

    def ewald_ring():
        arrive(sa_buf.at[1 - core], SA)
        sb_buf[y] = sa_buf[0] + sa_buf[1]
        for dy in range(1, 4):
            send_to(sb_buf.at[y], sb_buf.at[y], SB + dy, SB + y, dev(z, x, (y + dy) % 4, low, core))

    ghosts_at = []
    for side in range(2):
        arrive(gh_buf.at[side], GH + side)
        ghosts_at.append(gh_buf[side])
    index8 = pack_buf[0:8, :].astype(jnp.int32)
    distance = None
    for c in range(3):
        blocks = [moved[c : c + 1, 128 * n : 128 * n + 128] for n in range(4)]
        for side in range(2):
            blocks += [ghosts_at[side][c : c + 1, 128 * n : 128 * n + 128] for n in range(2)]
        blocks = [jnp.broadcast_to(block, (8, 128)) for block in blocks]
        others = jnp.concatenate(
            [lane_pick(blocks, index8[:, 128 * n : 128 * n + 128]) for n in range(4)], 1
        )
        offset = others - moved[c : c + 1, :]
        offset_buf[c] = offset
        distance = offset * offset if c == 0 else distance + offset * offset
    dist_buf[...] = distance
    m_row = rows_of((BASIS, ATOMS))
    rates = jnp.where(m_row % 2 == 1, 0.125 * math.sqrt(2.0), 0.125) * jnp.left_shift(1, m_row // 2).astype(F32)
    for j in range(NEIGH):
        exact = 1.0 / (1.0 + rates * dist_buf[j : j + 1, :])
        basis_buf[j] = exact.astype(BF16)
        slope_buf[j] = -rates * exact * exact

    def ewald_forces():
        for dy in range(1, 4):
            arrive(sb_buf.at[(y + dy) % 4], SB + (y + dy) % 4)
        sums = (sb_buf[0] + sb_buf[1]) + (sb_buf[2] + sb_buf[3])
        recip = wave_buf[0:8, :] * (TWO_PI / 4.0)
        recip = jnp.where(row8 < 3, recip, 0.0)
        square = jnp.sum(recip * recip, axis=0, keepdims=True)
        damping = 48.0 / math.sqrt(KVEC * TOTAL_ATOMS) * jnp.exp(-0.002 * square) / square
        from_sin = stacked_parts(recip * (damping * sums[0:1]))
        from_cos = stacked_parts(recip * (damping * sums[1:2]))
        part = dot(from_sin, sin_buf[...]) - dot(from_cos, cos_buf[...])
        part = 2.0 * charges * (part[0:8] + part[8:16])
        e1_buf[x] = part[0:4]
        for dx in (2, 1, 3):
            send_to(e1_buf.at[x], e1_buf.at[x], E1 + dx, E1 + x, dev(z, (x + dx) % 4, y, low, core))

    def ewald_group_sum():
        for dx in (1, 3, 2):
            arrive(e1_buf.at[(x + dx) % 4], E1 + (x + dx) % 4)
        e2_send[...] = (e1_buf[0] + e1_buf[1]) + (e1_buf[2] + e1_buf[3])
        place = 2 * z + low
        for dz in (2, 1, 3, 0):
            for flip in (1, 0):
                if dz or flip:
                    send_to(
                        e2_send,
                        e2_buf.at[place],
                        E2 + 2 * dz + flip,
                        E2 + place,
                        dev((z + dz) % 4, x, y, core, (low + flip) % 2),
                    )
        send_or_keep(e2_send, e2_buf.at[place], E2, E2 + place, swap)

    def finish_layer(layer):
        msg[...] = jnp.zeros((FEAT, ATOMS), F32)

        def body(j, carry):
            edge = dot(radial_t[layer], basis_buf[j])
            msg[...] += edge * picked[layer, j].astype(F32)
            return carry

        lax.fori_loop(0, NEIGH, body, 0, unroll=True)
        message = msg[...]
        inverse = lax.rsqrt(jnp.sum(message * message, axis=0, keepdims=True) * (1.0 / FEAT) + 1e-6)
        normed = message * inverse
        normed_buf[layer] = normed
        inv_buf[layer] = jnp.broadcast_to(inverse, (8, ATOMS))
        pre = dot(mix_t[layer], normed.astype(BF16))
        pre_buf[layer] = pre
        gated = (pre * lax.logistic(pre)).astype(BF16)
        hidden[...] += dot(update_t[layer], gated)

    finish_layer(0)
    rounded = hidden[...].astype(BF16)
    ext_rows[:, :ATOMS] = rounded
    send_features(1, rounded)
    ewald_sums()

    def receive_side(side):
        arrive(fg_buf.at[1, side], FG + 2 + side)
        packed = fg_buf.at[1, side]
        first = pl.multiple_of(ATOMS + SIDE * side, SIDE)
        later = pl.multiple_of(first + 128, 128)
        ext_rows[:, pl.ds(first, 128)] = packed[0:FEAT, :]
        rest = packed[FEAT:PACKED, :].astype(F32)
        ext_rows[0:128, pl.ds(later, 128)] = rest.astype(BF16)
        ext_rows[128:FEAT, pl.ds(later, 128)] = pltpu.roll(rest, 64, 1)[0 : FEAT - 128].astype(BF16)
        return pl.ds(first, SIDE)

    def gather_side(rows, with_own):
        def body(j, carry):
            columns = pl.ds(pl.multiple_of(j * ATOMS, ATOMS), ATOMS)
            part = dot(ext_rows[:, rows], onehot[rows, columns])
            if with_own:
                part = part + dot(ext_rows[:, :ATOMS], onehot[:ATOMS, columns])
            else:
                part = part + picked[1, j].astype(F32)
            picked[1, j] = part.astype(BF16)
            return carry

        lax.fori_loop(0, NEIGH, body, 0, unroll=True)

    gather_side(receive_side(1 - core), True)
    ewald_ring()
    arrive_sums(mb_buf, MB)
    xp_send[4:8, :] = (mb_buf[0] + mb_buf[1]) + (mb_buf[2] + mb_buf[3])
    send_or_keep(xp_send, xp_buf, XP, XP, swap)
    gather_side(receive_side(core), False)
    finish_layer(1)

    def silu_slope(pre):
        sig = lax.logistic(pre)
        return sig * (1.0 + pre * (1.0 - sig))

    final = dot(readout_t[...], hidden[...].astype(BF16))
    dfinal = ew_col * silu_slope(final)
    cotan = dot(readout[...], dfinal.astype(BF16)).astype(BF16)

    def message_cotan(layer, cotan_b):
        dgated = dot(update[layer], cotan_b).astype(BF16).astype(F32)
        dpre = dgated * silu_slope(pre_buf[layer])
        dnormed = dot(mix[layer], dpre.astype(BF16)).astype(BF16).astype(F32)
        normed = normed_buf[layer]
        mean = jnp.sum(dnormed * normed, axis=0, keepdims=True) * (1.0 / FEAT)
        dmsg[...] = inv_buf[layer, 0:1, :] * (dnormed - normed * mean)

    def distance_cotan(layer):
        def body(j, carry):
            dedge = (picked[layer, j].astype(F32) * dmsg[...]).astype(BF16)
            dbasis = dot(radial[layer], dedge).astype(BF16).astype(F32)
            part = jnp.sum(dbasis * slope_buf[j], axis=0, keepdims=True)
            if layer == 1:
                ddist_buf[pl.ds(j, 1), :] = part
            else:
                ddist_buf[pl.ds(j, 1), :] += part
            return carry

        lax.fori_loop(0, NEIGH, body, 0, unroll=True)

    message_cotan(1, cotan)

    def row_cotan(j, carry):
        at = pl.multiple_of(j * ATOMS, ATOMS)
        edge = dot(radial_t[1], basis_buf[j])
        d_picked[:, pl.ds(at, ATOMS)] = (edge * dmsg[...]).astype(BF16)
        return carry

    lax.fori_loop(0, NEIGH, row_cotan, 0, unroll=True)
    for near in range(2):
        side = core if near == 0 else 1 - core
        first = pl.multiple_of(ATOMS + SIDE * side, SIDE)
        pack_side(dg_send.at[side], dot_t(d_picked[...], onehot[pl.ds(first, SIDE), :]))
        send_to(dg_send.at[side], dg_buf.at[1 - side], DG + side, DG + 1 - side, ring_dev(z, 7 - 6 * side))
    ewald_forces()
    for half in range(2):
        drows[:, SIDE * half : SIDE * half + SIDE] = dot_t(
            d_picked[...], onehot[SIDE * half : SIDE * half + SIDE, :]
        )
    distance_cotan(1)
    for near in (1, 0):
        side = core if near == 0 else 1 - core
        arrive(dg_buf.at[side], DG + side)
    for side in range(2):
        unpack_side(dg_rows, dg_buf.at[side], SIDE * side)
    returned = dot_t(dg_rows[...], sel[...])
    owned = (drows[...] + returned).astype(BF16).astype(F32)
    message_cotan(0, (cotan.astype(F32) + owned).astype(BF16))
    distance_cotan(0)
    ewald_group_sum()

    ddist = 2.0 * ddist_buf[...]
    edge_force = [offset_buf[c] * ddist for c in range(3)]
    for c in range(3):
        own = jnp.sum(edge_force[c], axis=0, keepdims=True)
        fo_send[c : c + 1, :] = own
    fo_send[3:4, :] = jnp.zeros((1, ATOMS), F32)

    parts = []
    zero_row = jnp.zeros((1, ATOMS), F32)
    for j in range(NEIGH):
        rows = [edge_force[c][j : j + 1, :] for c in range(3)] + [zero_row] * 5
        parts.append(stacked_parts(jnp.concatenate(rows, 0)))
    force_rows = jnp.concatenate(parts, 1)
    for near in range(2):
        side = core if near == 0 else 1 - core
        first = pl.multiple_of(ATOMS + SIDE * side, SIDE)
        both = dot_t(force_rows, onehot[pl.ds(first, SIDE), :])
        gg_send[side] = both[0:4] + both[8:12]
        send_to(
            gg_send.at[side], gg_buf.at[1 - side], GG + side, GG + 1 - side, swapped_ring_dev(7 - 6 * side)
        )
    both = dot_t(force_rows, onehot[:ATOMS, :])
    fo_send[...] = fo_send[...] - (both[0:4] + both[8:12])
    send_or_keep(fo_send, fo_buf, FO, FO, swap)

    arrive(xp_buf, XP)
    for side in range(2):
        arrive(gg_buf.at[side], GG + side)
    zero4 = jnp.zeros((4, SIDE), F32)
    returned = None
    for side in range(2):
        rows = stacked_parts(jnp.concatenate([gg_buf[side], zero4], 0))
        both = dot_t(rows, sel_own[:, SIDE * side : SIDE * side + SIDE])
        both = both[0:4] + both[8:12]
        returned = both if side == 0 else returned + both
    arrive(fo_buf, FO)
    for place in range(8):
        arrive(e2_buf.at[place], E2 + place)
    long_range = e2_buf[0]
    for place in range(1, 8):
        long_range = long_range + e2_buf[place]
    result = (fo_buf[...] - returned) + long_range
    for c in range(3):
        out[c] = xp_buf[c : c + 1, :]
        out[3 + c] = xp_buf[4 + c : 5 + c, :] + (0.5 * DT) * result[c : c + 1, :]
        out[6 + c] = result[c : c + 1, :]

    for sent in started:
        sent.wait_send()

    @pl.when(jnp.logical_not(same))
    def _():
        for sent in conditional:
            sent.wait_send()

    @pl.when(same)
    def _():
        for dz, flip in targets[:7]:
            sums_copy(2 * dz + flip, ma_send, ma_buf, MA).wait_send()
            sums_copy(2 * dz + flip, mb_send, mb_buf, MB).wait_send()


def local(
    positions,
    momenta,
    forces,
    masses,
    charges,
    embedding,
    neighbours,
    send_rows,
    wavevectors,
    radial_weight,
    mix_weight,
    update_weight,
    readout_weight,
    energy_weight,
):
    piece = (3, 1, ATOMS)
    scratch = [
        (piece, F32),
        (piece, F32),
        (piece, F32),
        ((1, ATOMS), F32),
        ((1, ATOMS), F32),
        ((NEIGH, ATOMS), jnp.int32),
        ((3, 128), jnp.int32),
        ((3, KPART), jnp.int32),
        ((2, BASIS, FEAT), BF16),
        ((2, FEAT, FEAT), BF16),
        ((2, FEAT, FEAT), BF16),
        ((FEAT, FEAT), BF16),
        ((1, FEAT), F32),
        ((8, ATOMS), F32),
        ((8, 8, ATOMS), F32),
        ((FEAT, ATOMS), BF16),
        ((16, ATOMS), F32),
        ((16, ATOMS), F32),
        ((8, 8, ATOMS), F32),
        ((4, 8, ATOMS), F32),
        ((8, 4, ATOMS), F32),
        ((4, 4, ATOMS), F32),
        ((2, 4, SIDE), F32),
        ((2, 4, SIDE), F32),
        ((2, 2, PACKED, 128), BF16),
        ((2, 2, PACKED, 128), BF16),
        ((2, PACKED, 128), BF16),
        ((2, PACKED, 128), BF16),
        ((FEAT, 2 * SIDE), BF16),
        ((2, 2, KPART), F32),
        ((4, 2, KPART), F32),
        ((4, 4, ATOMS), F32),
        ((4, ATOMS), F32),
        ((8, 4, ATOMS), F32),
        ((8, ATOMS), F32),
        ((8, ATOMS), F32),
        ((4, ATOMS), F32),
        ((4, ATOMS), F32),
        ((2, 4, SIDE), F32),
        ((2, 4, SIDE), F32),
        ((ATOMS, 2 * SIDE), BF16),
        ((ATOMS, 2 * SIDE), BF16),
        ((EXT, NEIGH * ATOMS), BF16),
        ((FEAT, EXT), BF16),
        ((2, NEIGH, FEAT, ATOMS), BF16),
        ((FEAT, NEIGH * ATOMS), BF16),
        ((NEIGH, BASIS, ATOMS), BF16),
        ((NEIGH, BASIS, ATOMS), F32),
        ((NEIGH, ATOMS), F32),
        ((NEIGH, ATOMS), F32),
        ((3, NEIGH, ATOMS), F32),
        ((FEAT, ATOMS), F32),
        ((FEAT, ATOMS), F32),
        ((FEAT, ATOMS), F32),
        ((FEAT, ATOMS), F32),
        ((2, FEAT, ATOMS), F32),
        ((2, FEAT, ATOMS), F32),
        ((2, 8, ATOMS), F32),
        ((2, FEAT, FEAT), BF16),
        ((2, FEAT, FEAT), BF16),
        ((FEAT, FEAT), BF16),
        ((2, FEAT, BASIS), BF16),
        ((16, KPART), F32),
        ((KPART, 16), BF16),
        ((16, ATOMS), F32),
        ((KPART, ATOMS), BF16),
        ((KPART, ATOMS), BF16),
    ]
    out = pl.pallas_call(
        step_kernel,
        out_shape=jax.ShapeDtypeStruct((9, 1, ATOMS), F32),
        in_specs=[pl.BlockSpec(memory_space=pltpu.HBM)] * 15,
        out_specs=pl.BlockSpec(memory_space=pltpu.VMEM),
        scratch_shapes=[pltpu.SMEM((3 * BEADS,), F32)]
        + [pltpu.VMEM(shape, kind) for shape, kind in scratch]
        + [
            pltpu.SemaphoreType.DMA((N_SEMS,)),
            pltpu.SemaphoreType.DMA((N_SEMS,)),
            pltpu.SemaphoreType.DMA((14,)),
        ],
        compiler_params=pltpu.CompilerParams(
            collective_id=0, has_side_effects=True, vmem_limit_bytes=60 * 1024 * 1024
        ),
        cost_estimate=pl.CostEstimate(flops=16_000_000_000, bytes_accessed=2_000_000, transcendentals=1_000_000),
    )(
        jnp.asarray(ring_tables()),
        positions,
        momenta,
        forces,
        masses.reshape(1, ATOMS),
        charges.reshape(1, ATOMS),
        embedding.T,
        neighbours,
        send_rows.reshape(3, 128),
        wavevectors,
        radial_weight,
        mix_weight,
        update_weight,
        readout_weight,
        energy_weight.reshape(1, FEAT),
    )
    return out[0:3], out[3:6], out[6:9]


def solution(mesh):
    own = P(None, "bead", "dom")
    placed = (
        own,
        own,
        own,
        P("dom"),
        P("dom"),
        P("dom", None),
        P(None, "dom"),
        P("dom"),
        P(),
        P(),
        P(),
        P(),
        P(),
        P(),
    )
    return jax.shard_map(local, mesh=mesh, in_specs=placed, out_specs=(own, own, own), check_vma=False)
```
